32 devices in a mesh: dp: 16 (over z, x, core), seq: 2 (over y).
Axes of the slice: x: 2, y: 2, z: 4, core: 2. Of those that a mesh axis runs over, the one named last changes fastest.
Arguments:
- tokens: bfloat16 [16, 1024, 768], P('dp', 'seq'), may hold values from -6 to 6
- split_points: int32 [16], P('dp'), may hold values from 128 to 896, as said below
- cotangent: bfloat16 [16, 1024, 768], P('dp', 'seq'), may hold values from -6 to 6
- norm_gain: bfloat16 [2, 768], P(None, ('dp', 'seq')), may hold values from 0.5 to 1.5
- in_weight: bfloat16 [2, 768, 2304], P(None, ('dp', 'seq')), may hold values from -0.21875 to 0.21875
- short_taps: bfloat16 [2, 5, 2304], P(None, None, ('dp', 'seq')), may hold values from -2.5 to 2.5
- cond_taps: bfloat16 [2, 5, 768], P(None, None, ('dp', 'seq')), may hold values from -2.5 to 2.5
- out_weight: bfloat16 [2, 768, 768], P(None, ('dp', 'seq')), may hold values from -0.21875 to 0.21875
- mlp_gain: bfloat16 [2, 768], P(None, ('dp', 'seq')), may hold values from 0.5 to 1.5
- gate_up: bfloat16 [2, 768, 6144], P(None, ('dp', 'seq')), may hold values from -0.21875 to 0.21875
- down_weight: bfloat16 [2, 3072, 768], P(None, ('dp', 'seq')), may hold values from -0.21875 to 0.21875
Outputs:
- activations: bfloat16 [16, 1024, 768], P('dp', 'seq')
- token_grad: float32 [16, 1024, 768], P('dp', 'seq')
- norm_gain_grad: float32 [2, 768], P(None, ('dp', 'seq'))
- in_weight_grad: float32 [2, 768, 2304], P(None, ('dp', 'seq'))
- short_taps_grad: float32 [2, 5, 2304], P(None, None, ('dp', 'seq'))
- cond_taps_grad: float32 [2, 5, 768], P(None, None, ('dp', 'seq'))
- out_weight_grad: float32 [2, 768, 768], P(None, ('dp', 'seq'))
- mlp_gain_grad: float32 [2, 768], P(None, ('dp', 'seq'))
- gate_up_grad: float32 [2, 768, 6144], P(None, ('dp', 'seq'))
- down_weight_grad: float32 [2, 3072, 768], P(None, ('dp', 'seq'))
The draws below stay inside these ranges and needn't reach their ends.
Inputs may be any that keep to these rules, and one draw needn't show every extreme that they name: `split_points`: each split point lies at least 128 rows from both ends of its pair and from row 512.
All inputs are finite; a program needn't handle non-finite values.
Results may differ from the reference program's by a relative error of at most 0.025.
Values may be sent and summed in bfloat16 or wider, within the bound.
A program may use at most 448 MiB of HBM per device.

```python
import functools
import math
import jax
import jax.numpy as jnp
from jax import lax

D = 768
FF = 3072
LAYERS = 2
LENGTH = 1024
SEQS = 16


def draw_split_points(key, part):
    key = jax.random.fold_in(key, 7)
    first_key, second_key = jax.random.split(key)
    quarter = LENGTH // 8
    offset = jax.random.randint(first_key, (SEQS,), quarter, LENGTH // 2 - quarter + 1)
    halves = jax.random.randint(second_key, (SEQS,), 0, 2)
    return (offset + halves * (LENGTH // 2)).astype(jnp.int32)


def levels(own_key, extent, shards, least, top_value):
    def one(position, shards_of):
        steps = jax.random.uniform(jax.random.fold_in(jax.random.fold_in(own_key, 6), position), (shards_of,), jnp.float32, least / len(shards), top_value / len(shards))
        return jnp.repeat(jnp.exp(steps), extent[position] // shards_of).reshape((-1,) + (1,) * (len(extent) - position - 1))

    level = one(*shards[0])
    for cut in shards[1:]:
        level = level * one(*cut)
    return level


def bell_draw(own_key, extent, width, reach, shards=(), dtype=jnp.bfloat16):
    level = levels(own_key, extent, shards, -0.22, 0.18) if shards else 1.0
    entries = jax.random.normal(own_key, extent, jnp.float32) * width * level
    return jnp.minimum(jnp.maximum(entries, -reach), reach).astype(dtype)


def setup_inputs(seed: int = 0) -> dict:
    seeds = jax.random.split(jax.random.key(seed), 12)
    return {
        "tokens": bell_draw(seeds[0], (SEQS, LENGTH, D), 1.0, 6.0, ((0, 16), (1, 2))),
        "split_points": draw_split_points(jax.random.fold_in(seeds[11], 71), 0),
        "cotangent": bell_draw(seeds[2], (SEQS, LENGTH, D), 1.0, 6.0, ((0, 16), (1, 2))),
        "norm_gain": jnp.clip(1.0 + 0.1 * jax.random.normal(seeds[3], (LAYERS, D), jnp.float32), 0.5, 1.5).astype(jnp.bfloat16),
        "in_weight": bell_draw(seeds[4], (LAYERS, D, 3 * D), D ** -0.5, 0.21875, ((1, 32),)),
        "short_taps": bell_draw(seeds[5], (LAYERS, 5, 3 * D), 5 ** -0.5, 2.5, ((2, 32),)),
        "cond_taps": bell_draw(seeds[6], (LAYERS, 5, D), 5 ** -0.5, 2.5, ((2, 32),)),
        "out_weight": bell_draw(seeds[7], (LAYERS, D, D), D ** -0.5, 0.21875, ((1, 32),)),
        "mlp_gain": jnp.clip(1.0 + 0.1 * jax.random.normal(seeds[8], (LAYERS, D), jnp.float32), 0.5, 1.5).astype(jnp.bfloat16),
        "gate_up": bell_draw(seeds[9], (LAYERS, D, 2 * FF), D ** -0.5, 0.21875, ((1, 32),)),
        "down_weight": bell_draw(seeds[10], (LAYERS, FF, D), (FF // 4) ** -0.5, 0.21875, ((1, 32),)),
    }


highest = lax.Precision.HIGHEST
epsilon = 1e-05

@jax.custom_vjp
def low(v):
    return lax.optimization_barrier(v.astype(jnp.bfloat16)).astype(jnp.float32)

@jax.custom_vjp
def low_back(v):
    return v

def low_keep(v):
    return (low(v), None)

def low_pass(kept, grad):
    return (grad,)

def back_keep(v):
    return (v, None)

def back_low(kept, grad):
    return (low(grad),)
low.defvjp(low_keep, low_pass)
low_back.defvjp(back_keep, back_low)

def normalize(inputs, gain):
    center = inputs - lax.optimization_barrier(jnp.mean(inputs, axis=-1, keepdims=True))
    spread = lax.optimization_barrier(jnp.mean(center * center, axis=-1, keepdims=True))
    return center * lax.rsqrt(spread + epsilon) * gain

def decay_table(positions, channels, length, features):
    rates = jnp.exp(math.log(1.0 / length) + channels / (features - 1) * math.log(4.0))
    every = jnp.arange(length).astype(jnp.float32)
    scales = lax.rsqrt(lax.optimization_barrier(jnp.sum(jnp.exp(-2.0 * every[:, None] * rates[None, :]), axis=0)))
    return jnp.exp(-positions[:, None] * rates[None, :]) * scales[None, :]

def tap_masks(split_at, row_start, row_count, length):
    places = row_start - 2 + jnp.arange(row_count + 4)
    inside = (places >= 0) & (places < length)
    segment = jnp.where(inside[None, :], (places[None, :] >= split_at[:, None]).astype(jnp.int32), -1)
    center = segment[:, 2:2 + row_count]
    return jnp.stack([(segment[:, offset:offset + row_count] == center).astype(jnp.float32) for offset in range(5)])

def taps_apply(padded, tap_weights, tap_mask):
    row_count = tap_mask.shape[2]
    summed = jnp.zeros(padded.shape[:1] + (row_count,) + padded.shape[2:], jnp.float32)
    for offset in range(5):
        summed = summed + tap_weights[offset] * padded[:, offset:offset + row_count] * tap_mask[offset][:, :, None]
    return summed

def spectral_ref(filters, signal, split_at):
    period = 2 * LENGTH
    first = (jnp.arange(LENGTH)[None, :] < split_at[:, None]).astype(jnp.float32)[:, :, None]
    filt_hat = jnp.fft.rfft(filters, n=period, axis=1)
    summed = jnp.zeros_like(signal)
    for inside in (first, 1.0 - first):
        part_hat = jnp.fft.rfft(signal * inside, n=period, axis=1)
        summed = summed + inside * jnp.fft.irfft(filt_hat * part_hat, n=period, axis=1)[:, :LENGTH]
    return summed

def project(left, right):
    return jnp.einsum('gtd,de->gte', left, right, precision=highest)

def run_group(inputs, weights, split_at):
    tap_mask = tap_masks(split_at, 0, LENGTH, LENGTH)
    decay = decay_table(jnp.arange(LENGTH).astype(jnp.float32), jnp.arange(D).astype(jnp.float32), LENGTH, D)
    stream = inputs
    for layer_index in range(LAYERS):
        norm_g, in_w, short_w, cond_w, out_w, mlp_g, gate_w, down_w = [member[layer_index] for member in weights]
        normed = low(normalize(stream, norm_g))
        branches = low(low_back(project(normed, in_w)))
        padded = jnp.pad(branches, ((0, 0), (2, 2), (0, 0)))
        mixed = taps_apply(padded, short_w, tap_mask)
        query = mixed[..., :D]
        key_part = low(mixed[..., D:2 * D])
        value_part = low(mixed[..., 2 * D:])
        cond = taps_apply(jnp.pad(key_part, ((0, 0), (2, 2), (0, 0))), cond_w, tap_mask)
        filters = low(cond * decay)
        convolved = spectral_ref(filters, value_part, split_at)
        gated = low(query * convolved)
        middle = stream + low_back(project(gated, out_w))
        normed_mlp = low(normalize(middle, mlp_g))
        pre = low_back(project(normed_mlp, gate_w))
        hidden = low(jax.nn.gelu(pre[..., :FF], approximate=True) * pre[..., FF:])
        stream = middle + low_back(project(hidden, down_w))
    return stream

def reference(tokens, split_points, cotangent, norm_gain, in_weight, short_taps, cond_taps, out_weight, mlp_gain, gate_up, down_weight):
    weights = tuple((member.astype(jnp.float32) for member in (norm_gain, in_weight, short_taps, cond_taps, out_weight, mlp_gain, gate_up, down_weight)))
    group = math.gcd(SEQS, 8)
    blocks = SEQS // group
    inputs = tokens.astype(jnp.float32).reshape(blocks, group, LENGTH, D)
    splits = split_points.reshape(blocks, group)
    cots = cotangent.astype(jnp.float32).reshape(blocks, group, LENGTH, D)

    def visit(carry, item):
        block_in, block_split, block_cot = item
        outputs, back = jax.vjp(functools.partial(run_group, split_at=block_split), block_in, weights)
        grad_in, grad_w = back(block_cot)
        carry = jax.tree.map(jnp.add, carry, grad_w)
        return (carry, (outputs, grad_in))
    zeros = jax.tree.map(jnp.zeros_like, weights)
    totals, (outputs, grads_in) = lax.scan(visit, zeros, (inputs, splits, cots))
    return (outputs.reshape(SEQS, LENGTH, D).astype(jnp.bfloat16), grads_in.reshape(SEQS, LENGTH, D), totals[0], totals[1], totals[2], totals[3], totals[4], totals[5], totals[6], totals[7])
```

```python
import functools
import math

import numpy as np
import jax
import jax.numpy as jnp
from jax import lax
from jax.experimental import pallas as pl
from jax.experimental.pallas import tpu as pltpu
from jax.sharding import PartitionSpec as P

BF = jnp.bfloat16
F32 = jnp.float32
EPS = 1e-05
AXES = ("dp", "seq")
GAP = 128
VMEM_LIMIT = 60 * 2**20
STRIP = 128
CHUNK = 64


def transform_matrix(length):
    half = length - GAP
    freq = np.arange(half)[:, None]
    place = np.arange(length)[None, :]
    angle = ((2 * freq + 1) * place % (4 * half)).astype(np.float64) * (math.pi / (2 * half))
    both = np.stack([np.cos(angle), -np.sin(angle)])
    both = both.reshape(2, half // 128, 128, length).transpose(1, 0, 2, 3)
    return both.reshape(2 * half, length).astype(np.float32)


def decay_table(length, features):
    channels = jnp.arange(features).astype(F32)
    positions = jnp.arange(length).astype(F32)
    rates = jnp.exp(math.log(1.0 / length) + channels / (features - 1) * math.log(4.0))
    scales = lax.rsqrt(jnp.sum(jnp.exp(-2.0 * positions[:, None] * rates[None, :]), axis=0))
    return jnp.exp(-positions[:, None] * rates[None, :]) * scales[None, :]


def dot(a, b, dims=((1,), (0,))):
    return lax.dot_general(a, b, (dims, ((), ())), preferred_element_type=F32)


def tap_same(row0, split):
    t = row0 + lax.broadcasted_iota(jnp.int32, (CHUNK, STRIP), 0)
    here = t >= split
    return [
        None if off == 2 else jnp.where(((t + (off - 2)) >= split) == here, 1.0, 0.0)
        for off in range(5)
    ]


def shifted(ref, row0, cols, same):
    block = ref[pl.ds(row0, CHUNK + 16), cols]
    out = []
    for off in range(5):
        turned = pltpu.roll(block, (2 - off) % (CHUNK + 16), 0) if off != 2 else block
        rows = turned[8 : 8 + CHUNK]
        out.append(rows if same[off] is None else rows * same[off])
    return out


def clear_ends(ref, length):
    ref[0:8, :] = jnp.zeros((8, ref.shape[1]), F32)
    ref[8 + length : 16 + length, :] = jnp.zeros((8, ref.shape[1]), F32)


def mixer_forward_kernel(
    split_ref, br_ref, sw_ref, cw_ref, decay_ref, fwd_ref, inv_ref,
    gated_ref, q_ref, key_ref, conv_ref, fh_ref, uh_ref,
    pad, kpad, filt, u, prod,
):
    length, width = q_ref.shape
    half = length - GAP
    split = split_ref[0]
    strips = width // STRIP
    clear_ends(pad, length)
    clear_ends(kpad, length)
    pad[pl.ds(8, length), :] = br_ref[...].astype(F32)

    @pl.loop(0, length // CHUNK)
    def _(i):
        row0 = pl.multiple_of(i * CHUNK, CHUNK)
        rows = pl.ds(row0, CHUNK)
        same = tap_same(row0, split)
        first = row0 + lax.broadcasted_iota(jnp.int32, (CHUNK, STRIP), 0) < split
        for part in range(3):
            for strip in range(strips):
                cols = pl.ds(part * width + strip * STRIP, STRIP)
                own = pl.ds(strip * STRIP, STRIP)
                total = None
                for off, x in enumerate(shifted(pad, row0, cols, same)):
                    term = x * sw_ref[off : off + 1, cols]
                    total = term if total is None else total + term
                low = total.astype(BF)
                if part == 0:
                    q_ref[rows, own] = low
                elif part == 1:
                    key_ref[rows, own] = low
                    kpad[pl.ds(row0 + 8, CHUNK), own] = low.astype(F32)
                else:
                    low = low.astype(F32)
                    u[0, rows, own] = jnp.where(first, low, 0.0).astype(BF)
                    u[1, rows, own] = jnp.where(first, 0.0, low).astype(BF)

    @pl.loop(0, length // CHUNK)
    def _(i):
        row0 = pl.multiple_of(i * CHUNK, CHUNK)
        rows = pl.ds(row0, CHUNK)
        same = tap_same(row0, split)
        for strip in range(strips):
            cols = pl.ds(strip * STRIP, STRIP)
            total = None
            for off, x in enumerate(shifted(kpad, row0, cols, same)):
                term = x * cw_ref[off : off + 1, cols]
                total = term if total is None else total + term
            filt[rows, cols] = (total * decay_ref[rows, cols]).astype(BF)

    scale = 1.0 / half

    @pl.loop(0, half // 128)
    def _(i):
        rows = pl.ds(pl.multiple_of(i * 256, 256), 256)
        f = dot(fwd_ref[rows, pl.ds(0, half)], filt[pl.ds(0, half), :])
        fr, fi = f[:128], f[128:]
        fh_ref[rows, :] = f.astype(BF)
        for m in range(2):
            s = dot(fwd_ref[rows, :], u[m])
            uh_ref[m, rows, :] = s.astype(BF)
            sr, si = s[:128], s[128:]
            prod[m, rows, :] = jnp.concatenate(
                [(fr * sr - fi * si) * scale, (fr * si + fi * sr) * scale], axis=0
            ).astype(BF)

    corner = split // 256

    @pl.loop(0, length // 256)
    def _(i):
        rows = pl.ds(pl.multiple_of(i * 256, 256), 256)
        pick = (i > corner).astype(jnp.int32)
        conv_ref[rows, :] = dot(inv_ref[rows, :], prod[pick]).astype(BF)

        @pl.when(i == corner)
        def _():
            later = i * 256 + lax.broadcasted_iota(jnp.int32, (256, width), 0) >= split
            other = dot(inv_ref[rows, :], prod[1])
            conv_ref[rows, :] = jnp.where(later, other, conv_ref[rows, :].astype(F32)).astype(BF)

        gated_ref[rows, :] = (q_ref[rows, :].astype(F32) * conv_ref[rows, :].astype(F32)).astype(BF)


def mixer_backward_kernel(
    split_ref, mid_ref, ow_ref, br_ref, sw_ref, cw_ref, decay_ref, fwd_ref, inv_ref,
    q_ref, key_ref, conv_ref, fh_ref, uh_ref,
    dbr_ref, dsw_ref, dcw_ref,
    pad, epad, kpad, g, prod,
):
    length, width = q_ref.shape
    half = length - GAP
    split = split_ref[0]
    strips = width // STRIP
    clear_ends(pad, length)
    clear_ends(epad, length)
    clear_ends(kpad, length)
    kpad[pl.ds(8, length), :] = key_ref[...].astype(F32)

    @pl.loop(0, length // 256)
    def _(i):
        row0 = pl.multiple_of(i * 256, 256)
        rows = pl.ds(row0, 256)
        dg = dot(mid_ref[rows, :], ow_ref[...], ((1,), (1,)))
        first = row0 + lax.broadcasted_iota(jnp.int32, (256, width), 0) < split
        pad[pl.ds(row0 + 8, 256), pl.ds(0, width)] = dg * conv_ref[rows, :].astype(F32)
        dc = dg * q_ref[rows, :].astype(F32)
        g[0, rows, :] = jnp.where(first, dc, 0.0).astype(BF)
        g[1, rows, :] = jnp.where(first, 0.0, dc).astype(BF)

    scale = 1.0 / half

    @pl.loop(0, half // 128)
    def _(i):
        rows = pl.ds(pl.multiple_of(i * 256, 256), 256)
        f = fh_ref[rows, :].astype(F32)
        fr, fi = f[:128], f[128:]
        er = None
        for m in range(2):
            s = dot(fwd_ref[rows, :], g[m])
            sr, si = s[:128], s[128:]
            prod[m, rows, :] = jnp.concatenate(
                [(fr * sr + fi * si) * scale, (fr * si - fi * sr) * scale], axis=0
            ).astype(BF)
            w = uh_ref[m, rows, :].astype(F32)
            wr, wi = w[:128], w[128:]
            tr = wr * sr + wi * si
            ti = wr * si - wi * sr
            er, ei = (tr, ti) if er is None else (er + tr, ei + ti)
        prod[2, rows, :] = jnp.concatenate([er * scale, ei * scale], axis=0).astype(BF)

    corner = split // 256
    value_cols = pl.ds(2 * width, width)

    @pl.loop(0, length // 256)
    def _(i):
        row0 = pl.multiple_of(i * 256, 256)
        rows = pl.ds(row0, 256)
        spot = pl.ds(row0 + 8, 256)
        pick = (i > corner).astype(jnp.int32)
        pad[spot, value_cols] = dot(inv_ref[rows, :], prod[pick])

        @pl.when(i == corner)
        def _():
            later = i * 256 + lax.broadcasted_iota(jnp.int32, (256, width), 0) >= split
            other = dot(inv_ref[rows, :], prod[1])
            pad[spot, value_cols] = jnp.where(later, other, pad[spot, value_cols])

        inside = row0 + lax.broadcasted_iota(jnp.int32, (256, width), 0) < half
        d_filt = dot(inv_ref[rows, :], prod[2])
        epad[spot, :] = jnp.where(inside, d_filt, 0.0) * decay_ref[rows, :]

    dsw_ref[...] = jnp.zeros(dsw_ref.shape, F32)
    dcw_ref[...] = jnp.zeros(dcw_ref.shape, F32)

    @pl.loop(0, length // CHUNK)
    def _(i):
        row0 = pl.multiple_of(i * CHUNK, CHUNK)
        spot = pl.ds(row0 + 8, CHUNK)
        same = tap_same(row0, split)
        for strip in range(strips):
            cols = pl.ds(strip * STRIP, STRIP)
            e = epad[spot, cols]
            total = None
            for off, x in enumerate(shifted(epad, row0, cols, same)):
                term = x * cw_ref[4 - off : 5 - off, cols]
                total = term if total is None else total + term
            pad[spot, pl.ds(width + strip * STRIP, STRIP)] = total
            for off, x in enumerate(shifted(kpad, row0, cols, same)):
                dcw_ref[pl.ds(off * 8, 8), cols] += (x * e).reshape(CHUNK // 8, 8, STRIP).sum(0)

    @pl.loop(0, 3 * strips)
    def _(strip):
        cols = pl.ds(pl.multiple_of(strip * STRIP, STRIP), STRIP)
        kpad[pl.ds(8, length), pl.ds(0, STRIP)] = br_ref[:, cols].astype(F32)

        @pl.loop(0, length // CHUNK)
        def _(i):
            row0 = pl.multiple_of(i * CHUNK, CHUNK)
            same = tap_same(row0, split)
            e = pad[pl.ds(row0 + 8, CHUNK), cols]
            total = None
            for off, x in enumerate(shifted(pad, row0, cols, same)):
                term = x * sw_ref[4 - off : 5 - off, cols]
                total = term if total is None else total + term
            dbr_ref[pl.ds(row0, CHUNK), cols] = total.astype(BF)
            for off, x in enumerate(shifted(kpad, row0, pl.ds(0, STRIP), same)):
                dsw_ref[pl.ds(off * 8, 8), cols] += (x * e).reshape(CHUNK // 8, 8, STRIP).sum(0)


def local_call(kernel, outs, scratch, n_in):
    vmem = pl.BlockSpec(memory_space=pltpu.VMEM)
    return pl.pallas_call(
        kernel,
        out_shape=[jax.ShapeDtypeStruct(shape, dtype) for shape, dtype in outs],
        in_specs=[pl.BlockSpec(memory_space=pltpu.SMEM)] + [vmem] * (n_in - 1),
        out_specs=[vmem] * len(outs),
        scratch_shapes=[pltpu.VMEM(shape, dtype) for shape, dtype in scratch],
        compiler_params=pltpu.CompilerParams(vmem_limit_bytes=VMEM_LIMIT),
    )


def mixer_forward(split, branches, sw, cw, decay, fwd, inv):
    length, width = decay.shape
    bins = fwd.shape[0]
    tall = (length, width)
    return local_call(
        mixer_forward_kernel,
        [(tall, BF)] * 4 + [((bins, width), BF), ((2, bins, width), BF)],
        [
            ((length + 16, 3 * width), F32),
            ((length + 16, width), F32),
            (tall, BF),
            ((2,) + tall, BF),
            ((2, bins, width), BF),
        ],
        7,
    )(split, branches, sw, cw, decay, fwd, inv)


def mixer_backward(split, mid, ow, branches, sw, cw, decay, fwd, inv, q, key, conv, fh, uh):
    length, width = decay.shape
    bins = fwd.shape[0]
    dbr, dsw, dcw = local_call(
        mixer_backward_kernel,
        [((length, 3 * width), BF), ((40, 3 * width), F32), ((40, width), F32)],
        [
            ((length + 16, 3 * width), F32),
            ((length + 16, width), F32),
            ((length + 16, width), F32),
            ((2, length, width), BF),
            ((3, bins, width), BF),
        ],
        14,
    )(split, mid, ow, branches, sw, cw, decay, fwd, inv, q, key, conv, fh, uh)
    return dbr, dsw.reshape(5, 8, -1).sum(1), dcw.reshape(5, 8, -1).sum(1)


def cube(dp_count):
    bits = (dp_count // 2).bit_length() - 1
    core, seq = bits, bits + 1
    last, rest = [bits - 1], list(range(bits - 1))
    return bits, core, seq, (rest + [seq] + last, rest + last + [seq], last + [seq] + rest)


def place(bits):
    dp, seq = lax.axis_index("dp"), lax.axis_index("seq")
    coords = [(dp // (2 << (bits - 1 - d))) % 2 for d in range(bits)] + [dp % 2, seq]

    def neighbour(d):
        if d == bits + 1:
            return dp, 1 - seq
        step = 1 if d == bits else 2 << (bits - 1 - d)
        return dp + step * (1 - 2 * coords[d]), seq

    return coords, neighbour


def region(fixed, dims):
    return tuple(fixed[d] if d in fixed else slice(None) for d in range(dims))


def greet(neighbours):
    barrier = pltpu.get_barrier_semaphore()
    for device in neighbours:
        pl.semaphore_signal(barrier, inc=1, device_id=device, device_id_type=pl.DeviceIdType.MESH)
    pl.semaphore_wait(barrier, len(neighbours))


def remote(src, dst, send, recv, device):
    copy = pltpu.make_async_remote_copy(
        src_ref=src, dst_ref=dst, send_sem=send, recv_sem=recv,
        device_id=device, device_id_type=pl.DeviceIdType.MESH,
    )
    copy.start()
    return copy


UNITS = ((0, 0), (0, 1), (1, 0), (2, 0))
ORDERS = (0, 1, 2, 0)


def piece_of(shape, unit):
    array, piece = UNITS[unit]
    cols = shape[-1] // 2 if array == 0 else shape[-1]
    return tuple(slice(None) for _ in shape[:-1]) + (pl.ds(piece * cols, cols),), cols


def gather_kernel(dp_count, own, full, sems):
    bits, core_dim, seq_dim, orders = cube(dp_count)
    dims = bits + 2
    coords, neighbour = place(bits)
    core = coords[core_dim]
    sibling = neighbour(core_dim)
    greet([neighbour(d) for d in range(dims)])
    ici_send, ici_recv, core_send, core_recv, local = sems
    mine = region({d: coords[d] for d in range(dims)}, dims)
    everything = slice(None)
    waits = []
    ready = []
    for u, (array, _) in enumerate(UNITS):
        tail, _ = piece_of(own[array].shape[1:], u)
        here = full[array].at[(everything,) + mine + tail]
        start = pltpu.make_async_copy(own[array].at[(everything,) + tail], here, local.at[u])
        start.start()
        first = remote(own[array].at[(everything,) + tail], here, core_send.at[u, 0], core_recv.at[u, 0], sibling)
        ready.append((start, first))
        waits.append(first)
    stages = dims - 1
    last = [None] * len(UNITS)
    for t in range(stages + 1):
        for u, (array, _) in enumerate(UNITS):
            tail, _ = piece_of(own[array].shape[1:], u)
            order = orders[ORDERS[u]]
            if t == 0:
                ready[u][0].wait()
                ready[u][1].wait_recv()
            else:
                last[u].wait_recv()
                d = order[t - 1]
                fixed = {e: coords[e] for e in order[t:]}
                fixed[d] = 1 - coords[d]
                got = full[array].at[(core,) + region(fixed, dims) + tail]
                waits.append(remote(got, got, core_send.at[u, t], core_recv.at[u, t], sibling))
            if t < stages:
                fixed = {e: coords[e] for e in order[t:]}
                held = full[array].at[(core,) + region(fixed, dims) + tail]
                last[u] = remote(held, held, ici_send.at[u, t], ici_recv.at[u, t], neighbour(order[t]))
                ready.append(last[u])
    for copy in waits[: len(UNITS)]:
        copy.wait_send()
    for copy in waits[len(UNITS) :]:
        copy.wait()
    for copy in ready[len(UNITS) :]:
        copy.wait_send()


def gather_weights(own, dp_count, number):
    bits, _, _, _ = cube(dp_count)
    stages = bits + 1
    units = len(UNITS)

    def body(*refs):
        gather_kernel(dp_count, refs[:3], refs[3:6], refs[6:])

    grid = (2,) * (bits + 2)
    anywhere = pl.BlockSpec(memory_space=pl.ANY)
    return pl.pallas_call(
        body,
        out_shape=[jax.ShapeDtypeStruct(x.shape[:1] + grid + x.shape[1:], x.dtype) for x in own],
        in_specs=[anywhere] * 3,
        out_specs=[anywhere] * 3,
        scratch_shapes=[pltpu.SemaphoreType.DMA((units, stages))] * 2
        + [pltpu.SemaphoreType.DMA((units, stages + 1))] * 2
        + [pltpu.SemaphoreType.DMA((units,))],
        compiler_params=pltpu.CompilerParams(collective_id=number, has_side_effects=True),
    )(*own)


def scatter_kernel(dp_count, grads, outs, held, first, arrived, final, sems):
    bits, core_dim, seq_dim, orders = cube(dp_count)
    dims = bits + 2
    stages = dims - 1
    coords, neighbour = place(bits)
    core = coords[core_dim]
    sibling = neighbour(core_dim)
    greet([neighbour(d) for d in range(dims)])
    ici_send, ici_recv, core_send, core_recv, local = sems
    everything = region({}, dims)

    def add(u, fixed, extra, free):
        count = 2 ** len(free)

        @pl.loop(0, count)
        def _(i):
            at = {d: (i // 2 ** (len(free) - 1 - j)) % 2 for j, d in enumerate(free)}
            index = tuple(at[d] if d in at else fixed[d] for d in range(dims))
            held[u][index] += extra[tuple(at[d] for d in free)]

    starts = []
    for u, (array, _) in enumerate(UNITS):
        tail, _ = piece_of(grads[array].shape[1 + dims :], u)
        load = pltpu.make_async_copy(grads[array].at[(core,) + everything + tail], held[u], local.at[u, 0])
        load.start()
        starts.append((
            load,
            remote(grads[array].at[(1 - core,) + everything + tail], first[u], core_send.at[u, 0], core_recv.at[u, 0], sibling),
        ))
    copies = []
    last = [None] * len(UNITS)
    for t in range(stages + 1):
        for u, (array, _) in enumerate(UNITS):
            order = orders[ORDERS[u]][::-1]
            if t == 0:
                starts[u][0].wait()
                starts[u][1].wait_recv()
                add(u, {}, first[u], list(range(dims)))
            else:
                last[u].wait_recv()
                fixed = {d: coords[d] for d in order[:t]}
                add(u, fixed, arrived[u][t - 1], [d for d in range(dims) if d not in fixed])
            fixed = {d: coords[d] for d in order[:t]}
            if t < stages:
                fixed[order[t]] = 1 - coords[order[t]]
                last[u] = remote(
                    held[u].at[region(fixed, dims)], arrived[u][t], ici_send.at[u, t], ici_recv.at[u, t], neighbour(order[t])
                )
                copies.append(last[u])
            else:
                fixed[core_dim] = 1 - core
                last[u] = remote(held[u].at[region(fixed, dims)], final[u], core_send.at[u, 1], core_recv.at[u, 1], sibling)
    ends = []
    for u, (array, _) in enumerate(UNITS):
        tail, _ = piece_of(grads[array].shape[1 + dims :], u)
        mine = region({d: coords[d] for d in range(dims)}, dims)
        own = pltpu.make_async_copy(held[u].at[mine], outs[array].at[(core,) + tail], local.at[u, 1])
        own.start()
        last[u].wait_recv()
        other = pltpu.make_async_copy(final[u], outs[array].at[(1 - core,) + tail], local.at[u, 2])
        other.start()
        ends += [own, other]
    for copy in ends:
        copy.wait()
    for copy in copies + last + [s[1] for s in starts]:
        copy.wait_send()


def scatter_grads(grads, dp_count, number):
    bits, _, _, orders = cube(dp_count)
    dims = bits + 2
    stages = dims - 1
    units = len(UNITS)
    grid = (2,) * dims
    slabs = []
    for u, (array, _) in enumerate(UNITS):
        shape = grads[array].shape[1 + dims :]
        _, cols = piece_of(shape, u)
        slabs.append(shape[:-1] + (cols,))

    def body(*refs):
        grads_in, outs, refs = refs[:3], refs[3:6], refs[6:]
        held, first, final, refs = refs[:units], refs[units : 2 * units], refs[2 * units : 3 * units], refs[3 * units :]
        arrived = [refs[u * stages : (u + 1) * stages] for u in range(units)]
        scatter_kernel(dp_count, grads_in, outs, held, first, arrived, final, refs[units * stages :])

    anywhere = pl.BlockSpec(memory_space=pl.ANY)
    return pl.pallas_call(
        body,
        out_shape=[jax.ShapeDtypeStruct(x.shape[:1] + x.shape[1 + dims :], x.dtype) for x in grads],
        in_specs=[anywhere] * 3,
        out_specs=[anywhere] * 3,
        scratch_shapes=[pltpu.VMEM(grid + slab, BF) for slab in slabs] * 2
        + [pltpu.VMEM(slab, BF) for slab in slabs]
        + [pltpu.VMEM((2,) * (dims - 1 - t) + slab, BF) for slab in slabs for t in range(stages)]
        + [pltpu.SemaphoreType.DMA((units, stages))] * 2
        + [pltpu.SemaphoreType.DMA((units, 2))] * 2
        + [pltpu.SemaphoreType.DMA((units, 3))],
        compiler_params=pltpu.CompilerParams(
            collective_id=number, has_side_effects=True, vmem_limit_bytes=VMEM_LIMIT
        ),
    )(*grads)


def norm_parts(x):
    center = x - jnp.mean(x, axis=-1, keepdims=True)
    r = lax.rsqrt(jnp.mean(center * center, axis=-1, keepdims=True) + EPS)
    return center * r, r


def norm_back(x, gain, d):
    xhat, r = norm_parts(x)
    h = d * gain
    dx = r * (h - jnp.mean(h, axis=-1, keepdims=True) - xhat * jnp.mean(h * xhat, axis=-1, keepdims=True))
    return dx, jnp.sum(d * xhat, axis=0)


def gate_value(pre):
    return jax.nn.gelu(pre[0], approximate=True) * pre[1]


def shards(
    tokens, split_points, cotangent, norm_gain, in_weight, short_taps, cond_taps,
    out_weight, mlp_gain, gate_up, down_weight,
):
    rows, features = tokens.shape[1:]
    dp_count, seq_count = lax.axis_size("dp"), lax.axis_size("seq")
    devices = dp_count * seq_count
    length = rows * seq_count
    width = features // 2
    layers = in_weight.shape[0]
    share = norm_gain.shape[1]
    hidden = down_weight.shape[1] * devices
    core = lax.axis_index("dp") % 2
    seq = lax.axis_index("seq")

    swap = [(4 * k + a, 4 * k + 3 - a) for k in range(devices // 4) for a in (1, 2)]
    flip = [(i, i ^ 1) for i in range(dp_count)]

    def swap_rows(x):
        return jnp.where(core == seq, x, lax.ppermute(x, AXES, swap))

    def sibling(x):
        return lax.ppermute(x, "dp", flip)

    def beside(own, other, axis):
        return jnp.where(
            core == 0,
            jnp.concatenate([own, other], axis=axis),
            jnp.concatenate([other, own], axis=axis),
        )

    def half_of(x, which, axis):
        size = x.shape[axis] // 2
        return lax.dynamic_slice_in_dim(x, which * size, size, axis)

    def own_channels(x):
        parts = x.shape[-1] // features
        x = x.reshape(x.shape[:-1] + (parts, 2, width))
        x = lax.dynamic_index_in_dim(x, core, x.ndim - 2, keepdims=False)
        return x.reshape(x.shape[:-2] + (parts * width,))

    split = swap_rows(split_points)
    stream = swap_rows(tokens).reshape(rows, features).astype(F32)
    grad = swap_rows(cotangent).reshape(rows, features).astype(F32)
    table = transform_matrix(length)
    fwd = jnp.asarray(table, BF)
    inv = jnp.asarray(np.ascontiguousarray(table.T), BF)
    decay = own_channels(decay_table(length, features))

    def halves(x):
        parts = x.shape[-1] // features
        x = x.reshape(x.shape[:-1] + (parts, 2, width))
        x = jnp.moveaxis(x, -2, 0)
        return x.reshape(x.shape[:-2] + (parts * width,))

    lane = 128
    bits = cube(dp_count)[0]
    grid = (2,) * (bits + 2)
    small_sizes = [share, 15 * share, 5 * share, share]
    small_ends = np.cumsum([0] + small_sizes)
    small_rows = share * lane

    weights = []
    gains = []
    for layer in range(layers):
        small = jnp.concatenate(
            [x[layer].reshape(-1) for x in (norm_gain, short_taps, cond_taps, mlp_gain)]
        )
        small = jnp.pad(small, (0, 2 * small_rows - small.shape[0])).reshape(2, share, lane)
        own = [
            gate_up[layer].reshape(share, 2, hidden).transpose(1, 0, 2),
            halves(down_weight[layer]).reshape(2, hidden // features, share, width),
            jnp.concatenate([halves(in_weight[layer]), halves(out_weight[layer]), small], axis=2),
        ]
        gu_w, down_w, rest = gather_weights(own, dp_count, layer)
        gu_w = gu_w.reshape(2, features, hidden)
        down_w = down_w.reshape(2, hidden, width)
        rest = rest.reshape(2, features, 4 * width + lane)
        in_w = lax.dynamic_index_in_dim(rest, core, 0, keepdims=False)[:, : 3 * width]
        out_w = jnp.concatenate([rest[0, :, 3 * width : 4 * width], rest[1, :, 3 * width : 4 * width]], axis=1)
        weights.append((in_w, out_w, gu_w, down_w))
        small = rest[:, :, 4 * width :].reshape(2, devices, small_rows).transpose(1, 0, 2)
        small = small.reshape(devices, 2 * small_rows).astype(F32)
        ng, st, ct, mg = [small[:, small_ends[i] : small_ends[i + 1]] for i in range(4)]
        st = st.reshape(devices, 5, 3 * share).transpose(1, 0, 2).reshape(5, 3 * features)
        ct = ct.reshape(devices, 5, share).transpose(1, 0, 2).reshape(5, features)
        gains.append(
            (
                ng.reshape(features),
                jnp.pad(own_channels(st), ((0, 3), (0, 0))),
                jnp.pad(own_channels(ct), ((0, 3), (0, 0))),
                mg.reshape(features),
            )
        )

    kept = []
    for layer in range(layers):
        in_w, out_w, gu_w, down_w = weights[layer]
        ng, st, ct, mg = gains[layer]
        normed = (norm_parts(stream)[0] * ng).astype(BF)
        normed_all = beside(normed, sibling(normed), 0)
        branches = dot(normed_all, in_w).astype(BF)
        gated, q, key, conv, fh, uh = mixer_forward(
            split, branches, st, ct, decay, fwd, inv
        )
        mine = half_of(gated, core, 0)
        gated_rows = beside(mine, sibling(half_of(gated, 1 - core, 0)), 1)
        middle = stream + dot(gated_rows, out_w)
        normed_mlp = (norm_parts(middle)[0] * mg).astype(BF)
        pre = jnp.stack([dot(normed_mlp, gu_w[h]).astype(BF) for h in range(2)])
        hid = gate_value(pre.astype(F32)).astype(BF)
        kept.append((stream, normed_all, branches, gated, q, key, conv, fh, uh, middle, normed_mlp, pre, hid))
        stream = middle + jnp.concatenate([dot(hid, down_w[h]) for h in range(2)], axis=1)
    activations = swap_rows(stream.astype(BF)[None])

    scattered = []
    for layer in reversed(range(layers)):
        in_w, out_w, gu_w, down_w = weights[layer]
        ng, st, ct, mg = gains[layer]
        x, normed_all, branches, gated, q, key, conv, fh, uh, middle, normed_mlp, pre, hid = kept[layer]
        g_low = grad.astype(BF)
        g_half = [g_low[:, :width], g_low[:, width:]]
        d_down = jnp.stack([dot(hid, x, ((0,), (0,))).astype(BF) for x in g_half])
        d_hidden = sum(dot(x, w, ((1,), (1,))) for x, w in zip(g_half, down_w))
        (d_pre,) = jax.vjp(gate_value, pre.astype(F32))[1](d_hidden)
        d_pre = d_pre.astype(BF)
        d_gu = jnp.stack([dot(normed_mlp, d_pre[h], ((0,), (0,))).astype(BF) for h in range(2)])
        d_normed_mlp = sum(dot(d_pre[h], gu_w[h], ((1,), (1,))) for h in range(2))
        d_part, d_mg = norm_back(middle, mg, d_normed_mlp)
        d_middle = grad + d_part
        m_low = d_middle.astype(BF)
        m_all = beside(m_low, sibling(m_low), 0)
        d_branches, d_st, d_ct = mixer_backward(
            split, m_all, half_of(out_w, core, 0), branches, st, ct, decay, fwd, inv,
            q, key, conv, fh, uh,
        )
        d_out = dot(gated, m_all, ((0,), (0,)))
        d_in = dot(normed_all, d_branches, ((0,), (0,)))
        d_normed_all = dot(d_branches, in_w, ((1,), (1,)))
        d_normed = half_of(d_normed_all, core, 0) + sibling(half_of(d_normed_all, 1 - core, 0))
        d_part, d_ng = norm_back(x, ng, d_normed)
        grad = d_middle + d_part

        def spread(x, axis):
            return beside(x, jnp.zeros_like(x), axis)

        d_st = spread(d_st.reshape(5, 3, width), 2).reshape(5, 3 * features)
        d_ct = spread(d_ct, 1)
        d_st = d_st.reshape(5, devices, 3 * share).transpose(1, 0, 2).reshape(devices, -1)
        d_ct = d_ct.reshape(5, devices, share).transpose(1, 0, 2).reshape(devices, -1)
        small = jnp.concatenate([d_ng.reshape(devices, share), d_st, d_ct, d_mg.reshape(devices, share)], axis=1)
        small = jnp.pad(small, ((0, 0), (0, 2 * small_rows - small.shape[1]))).astype(BF)
        small = small.reshape(devices, 2, share, lane).transpose(1, 0, 2, 3).reshape(2, features, lane)
        d_in = spread(d_in.astype(BF)[None], 0)
        d_out = spread(halves(d_out.astype(BF)), 1)
        rest = jnp.concatenate([d_in, d_out, small], axis=2)
        pieces = [
            d_gu.reshape((2,) + grid + (share, hidden)),
            d_down.reshape((2,) + grid + (hidden // features, share, width)),
            rest.reshape((2,) + grid + (share, 4 * width + lane)),
        ]
        scattered.append(scatter_grads(pieces, dp_count, layers + layer))
    token_grad = swap_rows(grad[None])

    def joined(x):
        parts = x.shape[-1] // width
        x = jnp.moveaxis(x.reshape(x.shape[:-1] + (parts, width)), 0, -2)
        return x.reshape(x.shape[:-3] + (parts * features,))

    results = []
    for s_gu, s_down, s_rest in scattered[::-1]:
        small = s_rest[:, :, 4 * width :].reshape(-1)
        results.append(
            [small[small_ends[i] : small_ends[i + 1]] for i in range(4)]
            + [
                joined(s_rest[:, :, : 3 * width]),
                joined(s_rest[:, :, 3 * width : 4 * width]),
                s_gu.transpose(1, 0, 2).reshape(share, 2 * hidden),
                joined(s_down.reshape(2, -1, width)),
            ]
        )
    g_ng, g_st, g_ct, g_mg, g_in, g_out, g_gu, g_down = [jnp.stack(x).astype(F32) for x in zip(*results)]
    return (
        activations,
        token_grad,
        g_ng,
        g_in,
        g_st.reshape(layers, 5, 3 * share),
        g_ct.reshape(layers, 5, share),
        g_out,
        g_mg,
        g_gu,
        g_down,
    )


def solution(mesh):
    every = ("dp", "seq")
    rows, part = P("dp", "seq", None), P(None, every, None)
    vector, taps = P(None, every), P(None, None, every)
    return jax.shard_map(
        shards,
        mesh=mesh,
        in_specs=(rows, P("dp"), rows, vector, part, taps, taps, part, vector, part, part),
        out_specs=(rows, rows, vector, part, taps, taps, part, vector, part, part),
        check_vma=False,
    )
```

```python
import functools
import math

import numpy as np
import jax
import jax.numpy as jnp
from jax import lax
from jax.experimental import pallas as pl
from jax.experimental.pallas import tpu as pltpu
from jax.sharding import PartitionSpec as P

BF = jnp.bfloat16
F32 = jnp.float32
EPS = 1e-05
AXES = ("dp", "seq")
GAP = 128
VMEM_LIMIT = 60 * 2**20
STRIP = 128
LANES = 128
BINS = 448
ROWS = 256
CHUNK = 64


def transform_matrix(length):
    half = length - GAP
    freq = np.arange(half)[:, None]
    place = np.arange(length)[None, :]
    angle = ((2 * freq + 1) * place % (4 * half)).astype(np.float64) * (math.pi / (2 * half))
    both = np.stack([np.cos(angle), -np.sin(angle)])
    both = both.reshape(2, half // BINS, BINS, length).transpose(1, 0, 2, 3)
    return both.reshape(2 * half, length).astype(np.float32)


def decay_table(length, features):
    channels = jnp.arange(features).astype(F32)
    positions = jnp.arange(length).astype(F32)
    rates = jnp.exp(math.log(1.0 / length) + channels / (features - 1) * math.log(4.0))
    scales = lax.rsqrt(jnp.sum(jnp.exp(-2.0 * positions[:, None] * rates[None, :]), axis=0))
    return jnp.exp(-positions[:, None] * rates[None, :]) * scales[None, :]


def dot(a, b, dims=((1,), (0,))):
    return lax.dot_general(a, b, (dims, ((), ())), preferred_element_type=F32)


def tap_same(row0, split):
    t = row0 + lax.broadcasted_iota(jnp.int32, (CHUNK, STRIP), 0)
    here = t >= split
    return [
        None if off == 2 else jnp.where(((t + (off - 2)) >= split) == here, 1.0, 0.0)
        for off in range(5)
    ]


def shifted(ref, row0, cols, same):
    block = ref[pl.ds(row0, CHUNK + 16), cols]
    out = []
    for off in range(5):
        turned = pltpu.roll(block, (2 - off) % (CHUNK + 16), 0) if off != 2 else block
        rows = turned[8 : 8 + CHUNK]
        out.append(rows if same[off] is None else rows * same[off])
    return out


def over_chunks(length, split, body):
    @pl.loop(0, length // CHUNK)
    def _(i):
        row0 = pl.multiple_of(i * CHUNK, CHUNK)
        touched = (split > row0 - 2) & (split < row0 + CHUNK + 2)

        @pl.when(touched)
        def _():
            body(row0, tap_same(row0, split))

        @pl.when(jnp.logical_not(touched))
        def _():
            body(row0, [None] * 5)


def weigh(rows, w_ref, cols, flip):
    total = None
    for off, x in enumerate(rows):
        tap = 4 - off if flip else off
        term = x * w_ref[tap : tap + 1, cols]
        total = term if total is None else total + term
    return total


def clear_ends(ref, length):
    ref[0:8, :] = jnp.zeros((8, ref.shape[1]), F32)
    ref[8 + length : 16 + length, :] = jnp.zeros((8, ref.shape[1]), F32)


def fetch(pairs, sems):
    copies = [pltpu.make_async_copy(src, dst, sems.at[i]) for i, (src, dst) in enumerate(pairs)]
    for copy in copies:
        copy.start()
    return copies


def mixer_forward_kernel(
    scalar_ref, own_ref, other_ref, sw_ref, cw_ref, iw_hbm, decay_hbm, fwd_hbm, inv_hbm,
    gated_ref, mine_ref, send_ref, br_hbm, q_hbm, key_hbm, conv_hbm, fh_hbm, uh_hbm,
    iw_ref, decay_ref, fwd_ref, inv_ref, br_ref, q_ref, key_ref, conv_ref, fh_ref, uh_ref,
    pad, kpad, filt, u, prod, in_sems, out_sems,
):
    length, width = q_ref.shape
    rows_own = own_ref.shape[0]
    half = length - GAP
    split, core = scalar_ref[0], scalar_ref[1]
    strips = width // STRIP
    loads = fetch(
        [
            (iw_hbm.at[core, :, pl.ds(0, 3 * width)], iw_ref),
            (decay_hbm, decay_ref),
            (fwd_hbm, fwd_ref),
            (inv_hbm, inv_ref),
        ],
        in_sems,
    )
    outs = [(br_ref, br_hbm), (q_ref, q_hbm), (key_ref, key_hbm), (fh_ref, fh_hbm), (uh_ref, uh_hbm), (conv_ref, conv_hbm)]
    stores = [pltpu.make_async_copy(src, dst, out_sems.at[i]) for i, (src, dst) in enumerate(outs)]
    clear_ends(pad, length)
    clear_ends(kpad, length)
    loads[0].wait()
    for ref, side in ((own_ref, core), (other_ref, 1 - core)):

        @pl.loop(0, rows_own // ROWS)
        def _(i):
            row0 = pl.multiple_of(side * rows_own + i * ROWS, ROWS)
            low = dot(ref[pl.ds(pl.multiple_of(i * ROWS, ROWS), ROWS), :], iw_ref[...]).astype(BF)
            br_ref[pl.ds(row0, ROWS), :] = low
            pad[pl.ds(row0 + 8, ROWS), :] = low.astype(F32)

    stores[0].start()

    def mix(row0, same):
        rows = pl.ds(row0, CHUNK)
        first = row0 + lax.broadcasted_iota(jnp.int32, (CHUNK, STRIP), 0) < split
        for part in range(3):
            for strip in range(strips):
                cols = pl.ds(part * width + strip * STRIP, STRIP)
                own = pl.ds(strip * STRIP, STRIP)
                low = weigh(shifted(pad, row0, cols, same), sw_ref, cols, False).astype(BF)
                if part == 0:
                    q_ref[rows, own] = low
                elif part == 1:
                    key_ref[rows, own] = low
                    kpad[pl.ds(row0 + 8, CHUNK), own] = low.astype(F32)
                else:
                    low = low.astype(F32)
                    u[0, rows, own] = jnp.where(first, low, 0.0).astype(BF)
                    u[1, rows, own] = jnp.where(first, 0.0, low).astype(BF)

    over_chunks(length, split, mix)
    stores[1].start()
    stores[2].start()
    loads[1].wait()

    def make_filter(row0, same):
        rows = pl.ds(row0, CHUNK)
        for strip in range(strips):
            cols = pl.ds(strip * STRIP, STRIP)
            total = weigh(shifted(kpad, row0, cols, same), cw_ref, cols, False)
            filt[rows, cols] = (total * decay_ref[rows, cols]).astype(BF)

    over_chunks(length, split, make_filter)
    scale = 1.0 / half
    loads[2].wait()

    @pl.loop(0, half // BINS)
    def _(i):
        rows = pl.ds(pl.multiple_of(i * 2 * BINS, 2 * BINS), 2 * BINS)
        f = dot(fwd_ref[rows, pl.ds(0, half)], filt[pl.ds(0, half), :])
        fr, fi = f[:BINS], f[BINS:]
        fh_ref[rows, :] = f.astype(BF)
        for m in range(2):
            s = dot(fwd_ref[rows, :], u[m])
            uh_ref[m, rows, :] = s.astype(BF)
            sr, si = s[:BINS], s[BINS:]
            prod[m, rows, :] = jnp.concatenate(
                [(fr * sr - fi * si) * scale, (fr * si + fi * sr) * scale], axis=0
            ).astype(BF)

    stores[3].start()
    stores[4].start()
    corner = split // ROWS
    loads[3].wait()

    @pl.loop(0, length // ROWS)
    def _(i):
        rows = pl.ds(pl.multiple_of(i * ROWS, ROWS), ROWS)
        pick = (i > corner).astype(jnp.int32)
        conv_ref[rows, :] = dot(inv_ref[rows, :], prod[pick]).astype(BF)

        @pl.when(i == corner)
        def _():
            later = i * ROWS + lax.broadcasted_iota(jnp.int32, (ROWS, width), 0) >= split
            other = dot(inv_ref[rows, :], prod[1])
            conv_ref[rows, :] = jnp.where(later, other, conv_ref[rows, :].astype(F32)).astype(BF)

        gated_ref[rows, :] = (q_ref[rows, :].astype(F32) * conv_ref[rows, :].astype(F32)).astype(BF)

    stores[5].start()
    mine_ref[...] = gated_ref[pl.ds(pl.multiple_of(core * rows_own, ROWS), rows_own), :]
    send_ref[...] = gated_ref[pl.ds(pl.multiple_of((1 - core) * rows_own, ROWS), rows_own), :]
    for copy in stores:
        copy.wait()


def mixer_backward_kernel(
    scalar_ref, mid_own_ref, mid_other_ref, sw_ref, cw_ref,
    w_hbm, own_hbm, other_hbm, gated_hbm, br_hbm, decay_hbm, fwd_hbm, inv_hbm, q_hbm, key_hbm, conv_hbm, fh_hbm, uh_hbm,
    rest_ref, dn_ref, dn_send_ref, dsw_ref, dcw_ref,
    ow_ref, iw_ref, own_ref, other_ref, gated_ref, br_ref, decay_ref, fwd_ref, inv_ref, q_ref, key_ref, conv_ref, fh_ref,
    uh_ref, pad, epad, kpad, g, prod, mid_ref, dbr_ref, dsw_sum, dcw_sum, in_sems,
):
    length, width = q_ref.shape
    rows_own, features = own_ref.shape
    half = length - GAP
    split, core = scalar_ref[0], scalar_ref[1]
    strips = width // STRIP
    part = pl.ds(pl.multiple_of(core * width, STRIP), width)
    apart = pl.ds(pl.multiple_of((1 - core) * width, STRIP), width)
    near = pl.ds(pl.multiple_of(core * rows_own, ROWS), rows_own)
    far = pl.ds(pl.multiple_of((1 - core) * rows_own, ROWS), rows_own)
    out_cols = pl.ds(3 * width, width)
    loads = fetch(
        [
            (w_hbm.at[0, part, out_cols], ow_ref.at[0]),
            (w_hbm.at[1, part, out_cols], ow_ref.at[1]),
            (conv_hbm, conv_ref),
            (q_hbm, q_ref),
            (fwd_hbm, fwd_ref),
            (fh_hbm, fh_ref),
            (uh_hbm, uh_ref),
            (inv_hbm, inv_ref),
            (decay_hbm, decay_ref),
            (key_hbm, key_ref),
            (br_hbm, br_ref),
            (gated_hbm, gated_ref),
            (own_hbm, own_ref),
            (other_hbm, other_ref),
            (w_hbm.at[core, :, pl.ds(0, 3 * width)], iw_ref),
        ],
        in_sems,
    )
    mid_ref[near, :] = mid_own_ref[...]
    mid_ref[far, :] = mid_other_ref[...]
    clear_ends(pad, length)
    clear_ends(epad, length)
    clear_ends(kpad, length)
    dsw_sum[...] = jnp.zeros(dsw_sum.shape, F32)
    dcw_sum[...] = jnp.zeros(dcw_sum.shape, F32)
    rest_ref[1 - core, :, pl.ds(0, 3 * width)] = jnp.zeros((features, 3 * width), BF)
    for h in range(2):
        rest_ref[h, apart, out_cols] = jnp.zeros((width, width), BF)
    for copy in loads[:4]:
        copy.wait()
    out_w = jnp.concatenate([ow_ref[0], ow_ref[1]], axis=1)

    @pl.loop(0, length // ROWS)
    def _(i):
        row0 = pl.multiple_of(i * ROWS, ROWS)
        rows = pl.ds(row0, ROWS)
        dg = dot(mid_ref[rows, :], out_w, ((1,), (1,)))
        first = row0 + lax.broadcasted_iota(jnp.int32, (ROWS, width), 0) < split
        pad[pl.ds(row0 + 8, ROWS), pl.ds(0, width)] = dg * conv_ref[rows, :].astype(F32)
        dc = dg * q_ref[rows, :].astype(F32)
        g[0, rows, :] = jnp.where(first, dc, 0.0).astype(BF)
        g[1, rows, :] = jnp.where(first, 0.0, dc).astype(BF)

    scale = 1.0 / half
    for copy in loads[4:7]:
        copy.wait()

    @pl.loop(0, half // BINS)
    def _(i):
        rows = pl.ds(pl.multiple_of(i * 2 * BINS, 2 * BINS), 2 * BINS)
        f = fh_ref[rows, :].astype(F32)
        fr, fi = f[:BINS], f[BINS:]
        er = None
        for m in range(2):
            s = dot(fwd_ref[rows, :], g[m])
            sr, si = s[:BINS], s[BINS:]
            prod[m, rows, :] = jnp.concatenate(
                [(fr * sr + fi * si) * scale, (fr * si - fi * sr) * scale], axis=0
            ).astype(BF)
            w = uh_ref[m, rows, :].astype(F32)
            wr, wi = w[:BINS], w[BINS:]
            tr = wr * sr + wi * si
            ti = wr * si - wi * sr
            er, ei = (tr, ti) if er is None else (er + tr, ei + ti)
        prod[2, rows, :] = jnp.concatenate([er * scale, ei * scale], axis=0).astype(BF)

    corner = split // ROWS
    value_cols = pl.ds(2 * width, width)
    for copy in loads[7:10]:
        copy.wait()
    kpad[pl.ds(8, length), :] = key_ref[...].astype(F32)

    @pl.loop(0, length // ROWS)
    def _(i):
        row0 = pl.multiple_of(i * ROWS, ROWS)
        rows = pl.ds(row0, ROWS)
        spot = pl.ds(row0 + 8, ROWS)
        pick = (i > corner).astype(jnp.int32)
        pad[spot, value_cols] = dot(inv_ref[rows, :], prod[pick])

        @pl.when(i == corner)
        def _():
            later = i * ROWS + lax.broadcasted_iota(jnp.int32, (ROWS, width), 0) >= split
            other = dot(inv_ref[rows, :], prod[1])
            pad[spot, value_cols] = jnp.where(later, other, pad[spot, value_cols])

        inside = row0 + lax.broadcasted_iota(jnp.int32, (ROWS, width), 0) < half
        d_filt = dot(inv_ref[rows, :], prod[2])
        epad[spot, :] = jnp.where(inside, d_filt, 0.0) * decay_ref[rows, :]

    def key_taps(row0, same):
        spot = pl.ds(row0 + 8, CHUNK)
        for strip in range(strips):
            cols = pl.ds(strip * STRIP, STRIP)
            e = epad[spot, cols]
            pad[spot, pl.ds(width + strip * STRIP, STRIP)] = weigh(shifted(epad, row0, cols, same), cw_ref, cols, True)
            for off, x in enumerate(shifted(kpad, row0, cols, same)):
                dcw_sum[off, :, cols] += (x * e).reshape(CHUNK // 8, 8, STRIP).sum(0)

    over_chunks(length, split, key_taps)
    loads[10].wait()

    @pl.loop(0, 3 * strips)
    def _(strip):
        cols = pl.ds(pl.multiple_of(strip * STRIP, STRIP), STRIP)
        kpad[pl.ds(8, length), pl.ds(0, STRIP)] = br_ref[:, cols].astype(F32)

        def branch_taps(row0, same):
            e = pad[pl.ds(row0 + 8, CHUNK), cols]
            total = weigh(shifted(pad, row0, cols, same), sw_ref, cols, True)
            dbr_ref[pl.ds(row0, CHUNK), cols] = total.astype(BF)
            for off, x in enumerate(shifted(kpad, row0, pl.ds(0, STRIP), same)):
                dsw_sum[off, :, cols] += (x * e).reshape(CHUNK // 8, 8, STRIP).sum(0)

        over_chunks(length, split, branch_taps)

    dsw_ref[...] = jnp.sum(dsw_sum[...], axis=1)
    dcw_ref[...] = jnp.sum(dcw_sum[...], axis=1)
    for copy in loads[11:]:
        copy.wait()
    d_out = dot(gated_ref[...], mid_ref[...], ((0,), (0,))).astype(BF)
    for h in range(2):
        rest_ref[h, part, out_cols] = d_out[:, h * width : (h + 1) * width]
    for p in range(3):
        cols = pl.ds(p * width, width)
        d_in = dot(own_ref[...], dbr_ref[near, cols], ((0,), (0,)))
        d_in += dot(other_ref[...], dbr_ref[far, cols], ((0,), (0,)))
        rest_ref[core, :, cols] = d_in.astype(BF)
    dn_ref[...] = dot(dbr_ref[near, :], iw_ref[...], ((1,), (1,)))
    dn_send_ref[...] = dot(dbr_ref[far, :], iw_ref[...], ((1,), (1,))).astype(BF)


def local_call(kernel, args, direct, outs, direct_outs, scratch):
    vmem, anywhere = pl.BlockSpec(memory_space=pltpu.VMEM), pl.BlockSpec(memory_space=pl.ANY)
    return pl.pallas_call(
        kernel,
        out_shape=[jax.ShapeDtypeStruct(shape, dtype) for shape, dtype in outs],
        in_specs=[pl.BlockSpec(memory_space=pltpu.SMEM)]
        + [vmem] * (direct - 1)
        + [anywhere] * (len(args) - direct),
        out_specs=[vmem] * direct_outs + [anywhere] * (len(outs) - direct_outs),
        scratch_shapes=scratch,
        compiler_params=pltpu.CompilerParams(vmem_limit_bytes=VMEM_LIMIT),
    )(*args)


def mixer_forward(scalars, own, other, sw, cw, weight, decay, fwd, inv):
    length, width = decay.shape
    features = own.shape[1]
    bins = fwd.shape[0]
    tall, short, wide = (length, width), (own.shape[0], width), (length, 3 * width)
    kept = [(wide, BF), (tall, BF), (tall, BF), (tall, BF), ((bins, width), BF), ((2, bins, width), BF)]
    scratch = [((features, 3 * width), BF), (tall, F32), (fwd.shape, BF), (inv.shape, BF)] + kept
    scratch += [
        ((length + 16, 3 * width), F32),
        ((length + 16, width), F32),
        (tall, BF),
        ((2,) + tall, BF),
        ((2, bins, width), BF),
    ]
    return local_call(
        mixer_forward_kernel,
        (scalars, own, other, sw, cw, weight, decay, fwd, inv),
        5,
        [(tall, BF), (short, BF), (short, BF)] + kept,
        3,
        [pltpu.VMEM(*x) for x in scratch] + [pltpu.SemaphoreType.DMA((4,)), pltpu.SemaphoreType.DMA((6,))],
    )


def mixer_backward(scalars, mid_own, mid_other, sw, cw, weight, own, other, gated, br, decay, fwd, inv, q, key, conv, fh, uh):
    length, width = decay.shape
    bins = fwd.shape[0]
    rows, features = mid_own.shape
    held = (own, other, gated, br, decay, fwd, inv, q, key, conv, fh, uh)
    scratch = [((2, width, width), BF), ((features, 3 * width), BF)] + [(x.shape, x.dtype) for x in held]
    scratch += [
        ((length + 16, 3 * width), F32),
        ((length + 16, width), F32),
        ((length + 16, width), F32),
        ((2, length, width), BF),
        ((3, bins, width), BF),
        ((length, features), BF),
        ((length, 3 * width), BF),
        ((5, 8, 3 * width), F32),
        ((5, 8, width), F32),
    ]
    return local_call(
        mixer_backward_kernel,
        (scalars, mid_own, mid_other, sw, cw, weight) + held,
        5,
        [
            ((2, features, 4 * width), BF),
            ((rows, features), F32),
            ((rows, features), BF),
            ((5, 3 * width), F32),
            ((5, width), F32),
        ],
        5,
        [pltpu.VMEM(*x) for x in scratch] + [pltpu.SemaphoreType.DMA((15,))],
    )


def cube(dp_count):
    bits = (dp_count // 2).bit_length() - 1
    core, seq = bits, bits + 1
    low, rest = [bits - 1], list(range(bits - 1))
    orders = (
        rest + [seq] + low, rest + low + [seq], low + [seq] + rest,
        low + rest + [seq], [seq] + rest + low, [seq] + low + rest,
    )
    return bits, core, seq, orders


def place(bits):
    dp, seq = lax.axis_index("dp"), lax.axis_index("seq")
    coords = [(dp // (2 << (bits - 1 - d))) % 2 for d in range(bits)] + [dp % 2, seq]

    def neighbour(d):
        if d == bits + 1:
            return dp, 1 - seq
        step = 1 if d == bits else 2 << (bits - 1 - d)
        return dp + step * (1 - 2 * coords[d]), seq

    return coords, neighbour


def region(fixed, dims):
    return tuple(fixed[d] if d in fixed else slice(None) for d in range(dims))


def greet(neighbours):
    barrier = pltpu.get_barrier_semaphore()
    for device in neighbours:
        pl.semaphore_signal(barrier, inc=1, device_id=device, device_id_type=pl.DeviceIdType.MESH)
    pl.semaphore_wait(barrier, len(neighbours))


def remote(src, dst, send, recv, device):
    copy = pltpu.make_async_remote_copy(
        src_ref=src, dst_ref=dst, send_sem=send, recv_sem=recv,
        device_id=device, device_id_type=pl.DeviceIdType.MESH,
    )
    copy.start()
    return copy


GATHER_UNITS = (
    (3, 0, 640, 0, 0), (3, 640, 640, 1, 0), (3, 1280, 384, 2, 0),
    (0, 0, 768, 0, 1), (0, 768, 768, 1, 1), (2, 2, 2, 2, 1),
    (0, 1536, 768, 0, 2), (0, 2304, 768, 1, 2),
    (1, 0, 2, 0, 3), (1, 2, 2, 1, 3), (4, 1280, 384, 2, 3),
    (4, 0, 640, 0, 4), (4, 640, 640, 1, 4),
    (2, 0, 1, 0, 5), (2, 1, 1, 1, 5),
)
SCATTER_UNITS = (
    (0, 0, 768, 0, 0), (0, 768, 768, 1, 0), (2, 2, 2, 2, 0),
    (0, 1536, 768, 0, 1), (0, 2304, 768, 1, 1), (3, 1280, 256, 2, 1),
    (1, 0, 2, 0, 2), (1, 2, 2, 1, 2), (4, 1280, 256, 2, 2),
    (3, 0, 640, 0, 3), (3, 640, 640, 1, 3), (5, 0, 128, 2, 3),
    (4, 0, 640, 0, 4), (4, 640, 640, 1, 4),
    (2, 0, 1, 0, 5), (2, 1, 1, 1, 5),
)


def piece_of(unit, slabs):
    span = pl.ds(unit[1], unit[2])
    return (span, slice(None), slice(None)) if slabs else (slice(None), span)


def ticks(units, stages, shrinking):
    steps = [max(2**t, 2 ** (stages - 2)) for t in range(stages)]
    if shrinking:
        steps = steps[::-1]
    spacing = 2**stages // 4
    due = []
    for i, unit in enumerate(units):
        if shrinking:
            due.append((spacing * (unit[4] - 1) - 1, i, -1))
        due += [(spacing * unit[4] + sum(steps[:t]), i, t) for t in range(stages + 1)]
    return [(i, t) for _, i, t in sorted(due)]


def gather_kernel(dp_count, units, own, full, sems):
    bits, core_dim, _, orders = cube(dp_count)
    dims = bits + 2
    stages = dims - 1
    coords, neighbour = place(bits)
    core = coords[core_dim]
    sibling = neighbour(core_dim)
    greet([neighbour(d) for d in range(dims)])
    ici_send, ici_recv, core_send, core_recv, local = sems
    mine = region(dict(enumerate(coords)), dims)
    firsts, forwards, sends = [], [], []
    last = [None] * len(units)
    for u, unit in enumerate(units):
        array, tail = unit[0], piece_of(unit, len(own[unit[0]].shape) == 4)
        piece = own[array].at[(slice(None),) + tail]
        here = full[array].at[(slice(None),) + mine + tail]
        keep = pltpu.make_async_copy(piece, here, local.at[u])
        keep.start()
        firsts.append((keep, remote(piece, here, core_send.at[u, 0], core_recv.at[u, 0], sibling)))
    for u, t in ticks(units, stages, False):
        unit = units[u]
        array, tail, order = unit[0], piece_of(unit, len(own[unit[0]].shape) == 4), orders[unit[3]]
        fixed = {e: coords[e] for e in order[t:]}
        if t == 0:
            firsts[u][0].wait()
            firsts[u][1].wait_recv()
        else:
            last[u].wait_recv()
            got = full[array].at[(core,) + region(fixed | {order[t - 1]: 1 - coords[order[t - 1]]}, dims) + tail]
        if t < stages:
            held = full[array].at[(core,) + region(fixed, dims) + tail]
            last[u] = remote(held, held, ici_send.at[u, t], ici_recv.at[u, t], neighbour(order[t]))
            sends.append(last[u])
        if t > 0:
            forwards.append(remote(got, got, core_send.at[u, t], core_recv.at[u, t], sibling))
    for keep, copy in firsts:
        copy.wait_send()
    for copy in forwards:
        copy.wait()
    for copy in sends:
        copy.wait_send()


def gather_weights(own, dp_count, number):
    bits = cube(dp_count)[0]
    stages = bits + 1
    units = GATHER_UNITS
    arrays = len(own)
    count = len(units)

    def body(*refs):
        gather_kernel(dp_count, units, refs[:arrays], refs[arrays : 2 * arrays], refs[2 * arrays :])

    grid = (2,) * (bits + 2)
    anywhere = pl.BlockSpec(memory_space=pl.ANY)
    return pl.pallas_call(
        body,
        out_shape=[jax.ShapeDtypeStruct(x.shape[:1] + grid + x.shape[1:], x.dtype) for x in own],
        in_specs=[anywhere] * arrays,
        out_specs=[anywhere] * arrays,
        scratch_shapes=[pltpu.SemaphoreType.DMA((count, stages))] * 2
        + [pltpu.SemaphoreType.DMA((count, stages + 1))] * 2
        + [pltpu.SemaphoreType.DMA((count,))],
        compiler_params=pltpu.CompilerParams(collective_id=number, has_side_effects=True),
    )(*own)


def scatter_kernel(dp_count, units, grads, outs, held, first, arrived, final, sems):
    bits, core_dim, _, orders = cube(dp_count)
    dims = bits + 2
    stages = dims - 1
    coords, neighbour = place(bits)
    core = coords[core_dim]
    sibling = neighbour(core_dim)
    greet([neighbour(d) for d in range(dims)])
    ici_send, ici_recv, core_send, core_recv, local = sems
    everything = region({}, dims)

    def add(u, fixed, extra):
        free = [d for d in range(dims) if d not in fixed]

        @pl.loop(0, 2 ** len(free))
        def _(i):
            at = {d: (i // 2 ** (len(free) - 1 - j)) % 2 for j, d in enumerate(free)}
            index = tuple(at[d] if d in at else fixed[d] for d in range(dims))
            held[u][index] += extra[tuple(at[d] for d in free)]

    starts, sends = [None] * len(units), []
    last = [None] * len(units)
    for u, t in ticks(units, stages, True):
        if t < 0:
            array, tail = units[u][0], piece_of(units[u], len(outs[units[u][0]].shape) == 4)
            load = pltpu.make_async_copy(grads[array].at[(core,) + everything + tail], held[u], local.at[u, 0])
            load.start()
            other = grads[array].at[(1 - core,) + everything + tail]
            starts[u] = (load, remote(other, first[u], core_send.at[u, 0], core_recv.at[u, 0], sibling))
            continue
        order = orders[units[u][3]][::-1]
        fixed = {d: coords[d] for d in order[:t]}
        if t == 0:
            starts[u][0].wait()
            starts[u][1].wait_recv()
            add(u, fixed, first[u])
        else:
            last[u].wait_recv()
            add(u, fixed, arrived[u][t - 1])
        if t < stages:
            away = held[u].at[region(fixed | {order[t]: 1 - coords[order[t]]}, dims)]
            last[u] = remote(away, arrived[u][t], ici_send.at[u, t], ici_recv.at[u, t], neighbour(order[t]))
            sends.append(last[u])
        else:
            away = held[u].at[region(fixed | {core_dim: 1 - core}, dims)]
            last[u] = remote(away, final[u], core_send.at[u, 1], core_recv.at[u, 1], sibling)
    ends = []
    mine = region(dict(enumerate(coords)), dims)
    for u, unit in enumerate(units):
        array, tail = unit[0], piece_of(unit, len(outs[unit[0]].shape) == 4)
        own = pltpu.make_async_copy(held[u].at[mine], outs[array].at[(core,) + tail], local.at[u, 1])
        own.start()
        last[u].wait_recv()
        other = pltpu.make_async_copy(final[u], outs[array].at[(1 - core,) + tail], local.at[u, 2])
        other.start()
        ends += [own, other]
    for copy in ends:
        copy.wait()
    for copy in sends + last + [s[1] for s in starts]:
        copy.wait_send()


def scatter_grads(grads, dp_count, number):
    bits = cube(dp_count)[0]
    dims = bits + 2
    stages = dims - 1
    units = SCATTER_UNITS
    arrays = len(grads)
    count = len(units)
    grid = (2,) * dims
    slabs = []
    for array, _, size, _, _ in units:
        shape = grads[array].shape[1 + dims :]
        slabs.append((size,) + shape[1:] if len(shape) == 3 else shape[:-1] + (size,))

    def body(*refs):
        grads_in, outs, refs = refs[:arrays], refs[arrays : 2 * arrays], refs[2 * arrays :]
        held, first, final = refs[:count], refs[count : 2 * count], refs[2 * count : 3 * count]
        refs = refs[3 * count :]
        arrived = [refs[u * stages : (u + 1) * stages] for u in range(count)]
        scatter_kernel(dp_count, units, grads_in, outs, held, first, arrived, final, refs[count * stages :])

    anywhere = pl.BlockSpec(memory_space=pl.ANY)
    return pl.pallas_call(
        body,
        out_shape=[jax.ShapeDtypeStruct(x.shape[:1] + x.shape[1 + dims :], x.dtype) for x in grads],
        in_specs=[anywhere] * arrays,
        out_specs=[anywhere] * arrays,
        scratch_shapes=[pltpu.VMEM(grid + slab, BF) for slab in slabs] * 2
        + [pltpu.VMEM(slab, BF) for slab in slabs]
        + [pltpu.VMEM((2,) * (dims - 1 - t) + slab, BF) for slab in slabs for t in range(stages)]
        + [pltpu.SemaphoreType.DMA((count, stages))] * 2
        + [pltpu.SemaphoreType.DMA((count, 2))] * 2
        + [pltpu.SemaphoreType.DMA((count, 3))],
        compiler_params=pltpu.CompilerParams(
            collective_id=number, has_side_effects=True, vmem_limit_bytes=VMEM_LIMIT
        ),
    )(*grads)


def norm_parts(x):
    center = x - jnp.mean(x, axis=-1, keepdims=True)
    r = lax.rsqrt(jnp.mean(center * center, axis=-1, keepdims=True) + EPS)
    return center * r, r


def norm_back(x, gain, d):
    xhat, r = norm_parts(x)
    h = d * gain
    dx = r * (h - jnp.mean(h, axis=-1, keepdims=True) - xhat * jnp.mean(h * xhat, axis=-1, keepdims=True))
    return dx, jnp.sum(d * xhat, axis=0, keepdims=True)


SLOPE = math.sqrt(2.0 / math.pi)
CUBE = 0.044715


def gelu_parts(x):
    square = x * x
    t = jnp.tanh(SLOPE * (x + CUBE * square * x))
    flat = 0.5 + 0.5 * t
    return x * flat, flat + 0.5 * x * (1.0 - t * t) * (SLOPE + 3.0 * SLOPE * CUBE * square)


def mlp_forward_kernel(
    scalar_ref, x_ref, g0_ref, g1_ref, o0_ref, o1_ref, mg_ref, ng_ref, wg_ref, wu_ref, d0_ref, d1_ref,
    mid_ref, hm_ref, pre_ref, out_ref, next_ref,
):
    j = pl.program_id(0)

    @pl.when(j == 0)
    def _():
        width = g0_ref.shape[1]
        mid = x_ref[...]
        for ref, side in ((g0_ref, scalar_ref[1]), (g1_ref, 1 - scalar_ref[1])):
            rows = pl.ds(pl.multiple_of(side * width, STRIP), width)
            mid += dot(ref[...], jnp.concatenate([o0_ref[rows, :], o1_ref[rows, :]], axis=1))
        mid_ref[...] = mid
        out_ref[...] = mid
        hm_ref[...] = (norm_parts(mid)[0] * mg_ref[...]).astype(BF)

    gate = dot(hm_ref[...], wg_ref[...])
    up = dot(hm_ref[...], wu_ref[...])
    pre_ref[0] = gate.astype(BF)
    pre_ref[1] = up.astype(BF)
    hid = (gelu_parts(gate)[0] * up).astype(BF)
    down = jnp.concatenate([d0_ref[...], d1_ref[...]], axis=1)
    out_ref[...] += dot(hid, down)

    @pl.when(j == pl.num_programs(0) - 1)
    def _():
        next_ref[...] = (norm_parts(out_ref[...])[0] * ng_ref[...]).astype(BF)


def mlp_backward_kernel(
    g_ref, hm_ref, mid_ref, mg_ref, pre_ref, wg_ref, wu_ref, d0_ref, d1_ref,
    dgu_ref, ddn_ref, dmid_ref, mlow_ref, dmg_ref,
    glow, hm_t, acc,
):
    j = pl.program_id(0)
    width = d0_ref.shape[1]

    @pl.when(j == 0)
    def _():
        glow[...] = g_ref[...].astype(BF)
        hm_t[...] = hm_ref[...].T
        acc[...] = jnp.zeros(acc.shape, F32)

    down = jnp.concatenate([d0_ref[...], d1_ref[...]], axis=1)
    dh = dot(glow[...], down, ((1,), (1,)))
    value, slope = gelu_parts(pre_ref[0].astype(F32))
    up = pre_ref[1].astype(F32)
    hid = (value * up).astype(BF)
    d_gate = (dh * up * slope).astype(BF)
    d_up = (dh * value).astype(BF)
    d_down = dot(hid, glow[...], ((0,), (0,))).astype(BF)
    ddn_ref[0] = d_down[:, :width]
    ddn_ref[1] = d_down[:, width:]
    for h, d in enumerate((d_gate, d_up)):
        grad = dot(hm_t[...], d).astype(BF)
        if len(dgu_ref.shape) == 3:
            dgu_ref[h] = grad
        else:
            dgu_ref[:, h * TILE : (h + 1) * TILE] = grad
    acc[...] += dot(d_gate, wg_ref[...], ((1,), (1,))) + dot(d_up, wu_ref[...], ((1,), (1,)))

    @pl.when(j == pl.num_programs(0) - 1)
    def _():
        dx, dg = norm_back(mid_ref[...], mg_ref[...], acc[...])
        dmid = g_ref[...] + dx
        dmid_ref[...] = dmid
        mlow_ref[...] = dmid.astype(BF)
        dmg_ref[...] = dg


TILE = 512


def whole(shape):
    return pl.BlockSpec(shape, lambda j: (0,) * len(shape))


def weight_specs(layout, hidden, features):
    steps = hidden // TILE
    gate_up = pl.BlockSpec((features, TILE), lambda j: (0, j))
    up = pl.BlockSpec((features, TILE), lambda j: (1, j) if layout == "halves" else (0, steps + j))
    down = [
        pl.BlockSpec((TILE, features // 2), lambda j: (j, 0)),
        pl.BlockSpec((TILE, features // 2), lambda j: (steps + j, 0)),
    ]
    return [gate_up, up] + down


def mlp_forward(scalars, x, g0, g1, weight, mg, ng, weights):
    layout, gu, dn = weights
    rows, features = x.shape
    hidden = dn.shape[0] // 2
    square, vector = whole((rows, features)), whole((1, features))
    narrow = [whole(a.shape) for a in (g0, g1)]
    narrow += [pl.BlockSpec((features, features // 2), lambda j, h=h: (h, 3)) for h in range(2)]
    shapes = [((rows, features), F32), ((rows, features), BF), ((2, rows, hidden), BF), ((rows, features), F32), ((rows, features), BF)]
    return pl.pallas_call(
        mlp_forward_kernel,
        grid=(hidden // TILE,),
        out_shape=[jax.ShapeDtypeStruct(*s) for s in shapes],
        in_specs=[pl.BlockSpec(memory_space=pltpu.SMEM), square] + narrow + [vector] * 2 + weight_specs(layout, hidden, features),
        out_specs=[square, square, pl.BlockSpec((2, rows, TILE), lambda j: (0, 0, j)), square, square],
        compiler_params=pltpu.CompilerParams(vmem_limit_bytes=VMEM_LIMIT),
    )(scalars, x, g0, g1, weight, weight, mg, ng, gu, gu, dn, dn)


def mlp_backward(g, hm, mid, mg, pre, weights, side_by_side):
    layout, gu, dn = weights
    rows, features = g.shape
    hidden = pre.shape[2]
    width = features // 2
    square, vector = whole((rows, features)), whole((1, features))
    both = (features, 2 * hidden) if side_by_side else (2, features, hidden)
    shapes = [(both, BF), ((2, hidden, width), BF), ((rows, features), F32), ((rows, features), BF), ((1, features), F32)]
    return pl.pallas_call(
        mlp_backward_kernel,
        grid=(hidden // TILE,),
        out_shape=[jax.ShapeDtypeStruct(*s) for s in shapes],
        in_specs=[square] * 3
        + [vector, pl.BlockSpec((2, rows, TILE), lambda j: (0, 0, j))]
        + weight_specs(layout, hidden, features),
        out_specs=[
            pl.BlockSpec((features, 2 * TILE), lambda j: (0, j))
            if side_by_side
            else pl.BlockSpec((2, features, TILE), lambda j: (0, 0, j)),
            pl.BlockSpec((2, TILE, width), lambda j: (0, j, 0)),
            square, square, vector,
        ],
        scratch_shapes=[pltpu.VMEM((rows, features), BF), pltpu.VMEM((features, rows), BF), pltpu.VMEM((rows, features), F32)],
        compiler_params=pltpu.CompilerParams(vmem_limit_bytes=VMEM_LIMIT),
    )(g, hm, mid, mg, pre, gu, gu, dn, dn)


def shards(
    tokens, split_points, cotangent, norm_gain, in_weight, short_taps, cond_taps,
    out_weight, mlp_gain, gate_up, down_weight,
):
    rows, features = tokens.shape[1:]
    dp_count, seq_count = lax.axis_size("dp"), lax.axis_size("seq")
    devices = dp_count * seq_count
    length = rows * seq_count
    width = features // 2
    layers = in_weight.shape[0]
    share = norm_gain.shape[1]
    hidden = down_weight.shape[1] * devices
    core = lax.axis_index("dp") % 2
    seq = lax.axis_index("seq")

    swap = [(4 * k + a, 4 * k + 3 - a) for k in range(devices // 4) for a in (1, 2)]
    flip = [(i, i ^ 1) for i in range(dp_count)]

    def swap_rows(x):
        return jnp.where(core == seq, x, lax.ppermute(x, AXES, swap))

    def sibling(x):
        return lax.ppermute(x, "dp", flip)

    def beside(own, other, axis):
        return jnp.where(
            core == 0,
            jnp.concatenate([own, other], axis=axis),
            jnp.concatenate([other, own], axis=axis),
        )

    def half_of(x, which, axis):
        size = x.shape[axis] // 2
        return lax.dynamic_slice_in_dim(x, which * size, size, axis)

    def own_channels(x):
        parts = x.shape[-1] // features
        x = x.reshape(x.shape[:-1] + (parts, 2, width))
        x = lax.dynamic_index_in_dim(x, core, x.ndim - 2, keepdims=False)
        return x.reshape(x.shape[:-2] + (parts * width,))

    split = swap_rows(split_points)
    stream = swap_rows(tokens).reshape(rows, features).astype(F32)
    grad = swap_rows(cotangent).reshape(rows, features).astype(F32)
    table = transform_matrix(length)
    fwd = jnp.asarray(table, BF)
    inv = jnp.asarray(np.ascontiguousarray(table.T), BF)
    decay = own_channels(decay_table(length, features))

    def halves(x):
        parts = x.shape[-1] // features
        x = x.reshape(x.shape[:-1] + (parts, 2, width))
        x = jnp.moveaxis(x, -2, 0)
        return x.reshape(x.shape[:-2] + (parts * width,))

    grid = (2,) * (cube(dp_count)[0] + 2)

    small = jnp.concatenate(
        [
            norm_gain[:, :, None],
            mlp_gain[:, :, None],
            cond_taps.transpose(0, 2, 1),
            short_taps.reshape(layers, 5, share, 3).transpose(0, 2, 3, 1).reshape(layers, share, 15),
        ],
        axis=2,
    )
    small = jnp.pad(small, ((0, 0), (0, 0), (0, LANES - 22)))
    own = [gate_up[0].reshape(share, 2, hidden).transpose(1, 0, 2)]
    own += [halves(down_weight[layer]).reshape(2, hidden // features, share, width) for layer in range(layers)]
    for layer in range(layers):
        pair = jnp.stack([small[layer], jnp.zeros_like(small[layer])])
        own.append(jnp.concatenate([halves(in_weight[layer]), halves(out_weight[layer]), pair], axis=2))
    full = gather_weights(own, dp_count, 0)
    downs = [x.reshape(2 * hidden, width) for x in full[1 : 1 + layers]]
    mixer_w = [x.reshape(2, features, 4 * width + LANES) for x in full[1 + layers :]]
    late, _ = lax.optimization_barrier((gate_up[1:], full[0]))
    gate_ups = [("halves", full[0].reshape(2 * features, hidden))]
    gate_ups += [("plain", lax.all_gather(x, AXES, axis=0, tiled=True)) for x in late]
    ng, mg, ct, st = [], [], [], []
    for layer in range(layers):
        small = mixer_w[layer][0, :, 4 * width :].astype(F32).T
        ng.append(small[0:1])
        mg.append(small[1:2])
        ct.append(own_channels(small[2:7]))
        taps = small[7:22].reshape(3, 5, features).transpose(1, 2, 0).reshape(5, 3 * features)
        st.append(own_channels(taps))

    scalars = jnp.concatenate([split, core[None].astype(jnp.int32)])
    normed = (norm_parts(stream)[0] * ng[0]).astype(BF)
    kept = []
    for layer in range(layers):
        normed_far = sibling(normed)
        gated, mine, away, branches, q, key, conv, fh, uh = mixer_forward(
            scalars, normed, normed_far, st[layer], ct[layer], mixer_w[layer], decay, fwd, inv
        )
        middle, normed_mlp, pre, out, normed_next = mlp_forward(
            scalars, stream, mine, sibling(away), mixer_w[layer].reshape(2 * features, -1), mg[layer],
            ng[(layer + 1) % layers], gate_ups[layer] + (downs[layer],),
        )
        kept.append((stream, normed, normed_far, gated, branches, q, key, conv, fh, uh, middle, normed_mlp, pre))
        stream, normed = out, normed_next
    activations = swap_rows(stream.astype(BF)[None])

    summed = []
    early = [None] * layers
    for layer in reversed(range(layers)):
        x, normed, normed_far, gated, branches, q, key, conv, fh, uh, middle, normed_mlp, pre = kept[layer]
        d_gu, d_down, d_middle, m_low, d_mg = mlp_backward(
            grad, normed_mlp, middle, mg[layer], pre, gate_ups[layer] + (downs[layer],), layer > 0
        )
        rest, d_normed, d_away, d_st, d_ct = mixer_backward(
            scalars, m_low, sibling(m_low), st[layer], ct[layer], mixer_w[layer], normed, normed_far, gated, branches,
            decay, fwd, inv, q, key, conv, fh, uh,
        )
        d_part, d_ng = norm_back(x, ng[layer], d_normed + sibling(d_away).astype(F32))
        grad = d_middle + d_part

        if layer > 0:
            early[layer] = lax.psum_scatter(d_gu, AXES, scatter_dimension=0, tiled=True)
        summed.append((d_gu, d_down, rest, d_ng, d_mg, d_ct, d_st))
    token_grad = swap_rows(grad[None])
    d_gus, d_downs, rests, *smalls = zip(*summed[::-1])
    d_ng, d_mg, d_ct, d_st = [jnp.stack(x) for x in smalls]
    other = jnp.zeros_like(d_ct)
    d_ct = beside(d_ct, other, 2)
    d_st = d_st.reshape(layers, 5, 3, width)
    d_st = beside(d_st, jnp.zeros_like(d_st), 3).reshape(layers, 5, features, 3)
    d_st = d_st.transpose(0, 3, 1, 2).reshape(layers, 15, features)
    small = jnp.concatenate([d_ng, d_mg, d_ct, d_st, jnp.zeros((layers, LANES - 22, features), F32)], axis=1)
    small = small.astype(BF).transpose(0, 2, 1)
    pieces = [d_gus[0].reshape((2,) + grid + (share, hidden))]
    pieces += [x.reshape((2,) + grid + (hidden // features, share, width)) for x in d_downs]
    pieces += [x.reshape((2,) + grid + (share, 4 * width)) for x in rests]
    pieces.append(small.reshape((2,) + grid + (share, LANES)))
    outs = scatter_grads(pieces, dp_count, 1)

    def joined(x):
        parts = x.shape[-1] // width
        x = jnp.moveaxis(x.reshape(x.shape[:-1] + (parts, width)), 0, -2)
        return x.reshape(x.shape[:-3] + (parts * features,))

    early[0] = outs[0].transpose(1, 0, 2)
    for layer in range(1, layers):
        early[layer] = early[layer].reshape(share, hidden // TILE, 2, TILE).transpose(0, 2, 1, 3)
    g_gu = jnp.stack([x.reshape(share, 2 * hidden) for x in early]).astype(F32)
    g_down = jnp.stack([joined(x.reshape(2, -1, width)) for x in outs[1 : 1 + layers]]).astype(F32)
    rest = outs[1 + layers : 1 + 2 * layers]
    g_in = jnp.stack([joined(x[:, :, : 3 * width]) for x in rest]).astype(F32)
    g_out = jnp.stack([joined(x[:, :, 3 * width :]) for x in rest]).astype(F32)
    small = outs[-1].astype(F32)
    g_ng, g_mg, g_ct = small[:, :, 0], small[:, :, 1], small[:, :, 2:7].transpose(0, 2, 1)
    g_st = small[:, :, 7:22].reshape(layers, share, 3, 5).transpose(0, 3, 1, 2)
    return (
        activations,
        token_grad,
        g_ng,
        g_in,
        g_st.reshape(layers, 5, 3 * share),
        g_ct,
        g_out,
        g_mg,
        g_gu,
        g_down,
    )


def solution(mesh):
    every = ("dp", "seq")
    rows, part = P("dp", "seq", None), P(None, every, None)
    vector, taps = P(None, every), P(None, None, every)
    return jax.shard_map(
        shards,
        mesh=mesh,
        in_specs=(rows, P("dp"), rows, vector, part, taps, taps, part, vector, part, part),
        out_specs=(rows, rows, vector, part, taps, taps, part, vector, part, part),
        check_vma=False,
    )
```

```python
import functools
import math

import numpy as np
import jax
import jax.numpy as jnp
from jax import lax
from jax.experimental import pallas as pl
from jax.experimental.pallas import tpu as pltpu
from jax.sharding import PartitionSpec as P

BF = jnp.bfloat16
F32 = jnp.float32
EPS = 1e-05
AXES = ("dp", "seq")
GAP = 128
VMEM_LIMIT = 60 * 2**20
STRIP = 128
LANES = 128
BINS = 224
ROWS = 256
CHUNK = 128


def transform_matrix(length):
    half = length - GAP
    freq = np.arange(half)[:, None]
    place = np.arange(length)[None, :]
    angle = ((2 * freq + 1) * place % (4 * half)).astype(np.float64) * (math.pi / (2 * half))
    both = np.stack([np.cos(angle), -np.sin(angle)])
    both = both.reshape(2, half // BINS, BINS, length).transpose(1, 0, 2, 3)
    return both.reshape(2 * half, length).astype(np.float32)


def decay_table(length, features):
    channels = jnp.arange(features).astype(F32)
    positions = jnp.arange(length).astype(F32)
    rates = jnp.exp(math.log(1.0 / length) + channels / (features - 1) * math.log(4.0))
    scales = lax.rsqrt(jnp.sum(jnp.exp(-2.0 * positions[:, None] * rates[None, :]), axis=0))
    return jnp.exp(-positions[:, None] * rates[None, :]) * scales[None, :]


def dot(a, b, dims=((1,), (0,))):
    return lax.dot_general(a, b, (dims, ((), ())), preferred_element_type=F32)


def tap_same(row0, split):
    t = row0 + lax.broadcasted_iota(jnp.int32, (CHUNK, STRIP), 0)
    here = t >= split
    return [
        None if off == 2 else jnp.where(((t + (off - 2)) >= split) == here, 1.0, 0.0)
        for off in range(5)
    ]


def shifted(ref, row0, cols, same):
    block = ref[pl.ds(row0, CHUNK + 16), cols]
    out = []
    for off in range(5):
        turned = pltpu.roll(block, (2 - off) % (CHUNK + 16), 0) if off != 2 else block
        rows = turned[8 : 8 + CHUNK]
        out.append(rows if same[off] is None else rows * same[off])
    return out


def over_chunks(length, split, body):
    @pl.loop(0, length // CHUNK)
    def _(i):
        row0 = pl.multiple_of(i * CHUNK, CHUNK)
        touched = (split > row0 - 2) & (split < row0 + CHUNK + 2)

        @pl.when(touched)
        def _():
            body(row0, tap_same(row0, split))

        @pl.when(jnp.logical_not(touched))
        def _():
            body(row0, [None] * 5)


def tap_loads(layer, core, ch_hbm, st_hbm, ct_ref, st_ref):
    width = ct_ref.shape[0]
    own = pl.multiple_of(core * width, STRIP)
    pairs = [(ch_hbm.at[layer, pl.ds(own, width), :], ct_ref)]
    for part in range(3):
        rows = pl.ds(pl.multiple_of(part * 2 * width + own, STRIP), width)
        pairs.append((st_hbm.at[layer, rows, :], st_ref.at[pl.ds(part * width, width), :]))
    return pairs


def weigh(rows, w_ref, base, cols, flip):
    total = None
    for off, x in enumerate(rows):
        tap = base + (4 - off if flip else off)
        term = x * w_ref[tap : tap + 1, cols]
        total = term if total is None else total + term
    return total


def by_corner(split, length, body):
    for corner in range(length // ROWS):
        spans = (slice(0, (corner + 1) * ROWS), slice(corner * ROWS, length))
        pl.when(split // ROWS == corner)(functools.partial(body, spans))


def clear_ends(ref, length):
    ref[0:8, :] = jnp.zeros((8, ref.shape[1]), F32)
    ref[8 + length : 16 + length, :] = jnp.zeros((8, ref.shape[1]), F32)


def fetch(pairs, sems):
    copies = [pltpu.make_async_copy(src, dst, sems.at[i]) for i, (src, dst) in enumerate(pairs)]
    for copy in copies:
        copy.start()
    return copies


def mixer_forward_kernel(
    layer, scalar_ref, own_ref, other_ref, ch_hbm, st_hbm, iw_hbm, decay_hbm, fwd_hbm, inv_hbm,
    gated_ref, mine_ref, send_ref, br_hbm, q_hbm, key_hbm, conv_hbm, fh_hbm, uh_hbm,
    iw_ref, decay_ref, fwd_ref, inv_ref, br_ref, q_ref, key_ref, conv_ref, fh_ref, uh_ref,
    ct_ref, st_ref, cw_ref, sw_ref, pad, kpad, filt, u, prod, in_sems, out_sems,
):
    length, width = q_ref.shape
    rows_own = own_ref.shape[0]
    half = length - GAP
    split, core = scalar_ref[0], scalar_ref[1]
    strips = width // STRIP
    loads = fetch(
        [
            (iw_hbm.at[core, :, pl.ds(0, 3 * width)], iw_ref),
            (decay_hbm, decay_ref),
            (fwd_hbm, fwd_ref),
            (inv_hbm, inv_ref),
        ]
        + tap_loads(layer, core, ch_hbm, st_hbm, ct_ref, st_ref),
        in_sems,
    )
    outs = [(br_ref, br_hbm), (q_ref, q_hbm), (key_ref, key_hbm), (fh_ref, fh_hbm), (uh_ref, uh_hbm), (conv_ref, conv_hbm)]
    stores = [pltpu.make_async_copy(src, dst, out_sems.at[i]) for i, (src, dst) in enumerate(outs)]
    clear_ends(pad, length)
    clear_ends(kpad, length)
    loads[0].wait()
    for ref, side in ((own_ref, core), (other_ref, 1 - core)):

        @pl.loop(0, rows_own // ROWS)
        def _(i):
            row0 = pl.multiple_of(side * rows_own + i * ROWS, ROWS)
            low = dot(ref[pl.ds(pl.multiple_of(i * ROWS, ROWS), ROWS), :], iw_ref[...]).astype(BF)
            br_ref[pl.ds(row0, ROWS), :] = low
            pad[pl.ds(row0 + 8, ROWS), :] = low.astype(F32)

    stores[0].start()
    for copy in loads[4:]:
        copy.wait()
    cw_ref[...] = ct_ref[...].astype(F32).T
    sw_ref[...] = st_ref[...].astype(F32).T

    def mix(row0, same):
        rows = pl.ds(row0, CHUNK)
        first = row0 + lax.broadcasted_iota(jnp.int32, (CHUNK, STRIP), 0) < split
        for part in range(3):
            for strip in range(strips):
                cols = pl.ds(part * width + strip * STRIP, STRIP)
                own = pl.ds(strip * STRIP, STRIP)
                low = weigh(shifted(pad, row0, cols, same), sw_ref, 0, cols, False).astype(BF)
                if part == 0:
                    q_ref[rows, own] = low
                elif part == 1:
                    key_ref[rows, own] = low
                    kpad[pl.ds(row0 + 8, CHUNK), own] = low.astype(F32)
                else:
                    low = low.astype(F32)
                    u[0, rows, own] = jnp.where(first, low, 0.0).astype(BF)
                    u[1, rows, own] = jnp.where(first, 0.0, low).astype(BF)

    over_chunks(length, split, mix)
    stores[1].start()
    stores[2].start()
    loads[1].wait()

    def make_filter(row0, same):
        rows = pl.ds(row0, CHUNK)
        for strip in range(strips):
            cols = pl.ds(strip * STRIP, STRIP)
            total = weigh(shifted(kpad, row0, cols, same), cw_ref, 2, cols, False)
            filt[rows, cols] = (total * decay_ref[rows, cols]).astype(BF)

    over_chunks(length, split, make_filter)
    scale = 1.0 / half
    loads[2].wait()

    def transform(spans):
        @pl.loop(0, half // BINS)
        def _(i):
            rows = pl.ds(pl.multiple_of(i * 2 * BINS, 2 * BINS), 2 * BINS)
            f = dot(fwd_ref[rows, 0:half], filt[0:half, :])
            fr, fi = f[:BINS], f[BINS:]
            fh_ref[rows, :] = f.astype(BF)
            for m in range(2):
                s = dot(fwd_ref[rows, spans[m]], u[m, spans[m], :])
                uh_ref[m, rows, :] = s.astype(BF)
                sr, si = s[:BINS], s[BINS:]
                prod[m, rows, :] = jnp.concatenate(
                    [(fr * sr - fi * si) * scale, (fr * si + fi * sr) * scale], axis=0
                ).astype(BF)

    by_corner(split, length, transform)
    stores[3].start()
    stores[4].start()
    corner = split // ROWS
    loads[3].wait()

    @pl.loop(0, length // ROWS)
    def _(i):
        rows = pl.ds(pl.multiple_of(i * ROWS, ROWS), ROWS)
        pick = (i > corner).astype(jnp.int32)
        conv_ref[rows, :] = dot(inv_ref[rows, :], prod[pick]).astype(BF)

        @pl.when(i == corner)
        def _():
            later = i * ROWS + lax.broadcasted_iota(jnp.int32, (ROWS, width), 0) >= split
            other = dot(inv_ref[rows, :], prod[1])
            conv_ref[rows, :] = jnp.where(later, other, conv_ref[rows, :].astype(F32)).astype(BF)

        gated_ref[rows, :] = (q_ref[rows, :].astype(F32) * conv_ref[rows, :].astype(F32)).astype(BF)

    stores[5].start()
    mine_ref[...] = gated_ref[pl.ds(pl.multiple_of(core * rows_own, ROWS), rows_own), :]
    send_ref[...] = gated_ref[pl.ds(pl.multiple_of((1 - core) * rows_own, ROWS), rows_own), :]
    for copy in stores:
        copy.wait()


def mixer_backward_kernel(
    layer, scalar_ref, mid_own_ref, mid_other_ref, dmg_ref, ch_hbm, st_hbm,
    w_hbm, own_hbm, other_hbm, gated_hbm, br_hbm, decay_hbm, fwd_hbm, inv_hbm, q_hbm, key_hbm, conv_hbm, fh_hbm, uh_hbm,
    rest_ref, dn_ref, dn_send_ref, dch_ref, dst_ref,
    ow_ref, iw_ref, own_ref, other_ref, gated_ref, br_ref, decay_ref, fwd_ref, inv_ref, q_ref, key_ref, conv_ref, fh_ref,
    uh_ref, ct_ref, st_ref, cw_ref, sw_ref, pad, epad, kpad, g, prod, mid_ref, dbr_ref, dsw_sum, dcw_sum, ch_rows, st_rows,
    in_sems,
):
    length, width = q_ref.shape
    rows_own, features = own_ref.shape
    half = length - GAP
    split, core = scalar_ref[0], scalar_ref[1]
    strips = width // STRIP
    part = pl.ds(pl.multiple_of(core * width, STRIP), width)
    apart = pl.ds(pl.multiple_of((1 - core) * width, STRIP), width)
    near = pl.ds(pl.multiple_of(core * rows_own, ROWS), rows_own)
    far = pl.ds(pl.multiple_of((1 - core) * rows_own, ROWS), rows_own)
    out_cols = pl.ds(3 * width, width)
    loads = fetch(
        [
            (w_hbm.at[0, part, out_cols], ow_ref.at[0]),
            (w_hbm.at[1, part, out_cols], ow_ref.at[1]),
            (conv_hbm, conv_ref),
            (q_hbm, q_ref),
            (fwd_hbm, fwd_ref),
            (fh_hbm, fh_ref),
            (uh_hbm, uh_ref),
            (inv_hbm, inv_ref),
            (decay_hbm, decay_ref),
            (key_hbm, key_ref),
            (br_hbm, br_ref),
            (gated_hbm, gated_ref),
            (own_hbm, own_ref),
            (other_hbm, other_ref),
            (w_hbm.at[core, :, pl.ds(0, 3 * width)], iw_ref),
        ]
        + tap_loads(layer, core, ch_hbm, st_hbm, ct_ref, st_ref),
        in_sems,
    )
    mid_ref[near, :] = mid_own_ref[...]
    mid_ref[far, :] = mid_other_ref[...]
    clear_ends(pad, length)
    clear_ends(epad, length)
    clear_ends(kpad, length)
    dsw_sum[...] = jnp.zeros(dsw_sum.shape, F32)
    dcw_sum[...] = jnp.zeros(dcw_sum.shape, F32)
    ch_rows[...] = jnp.zeros(ch_rows.shape, F32)
    st_rows[...] = jnp.zeros(st_rows.shape, F32)
    for p in range(3):
        rows = pl.ds(pl.multiple_of(p * features + (1 - core) * width, STRIP), width)
        dst_ref[rows, :] = jnp.zeros((width, LANES), BF)
    rest_ref[1 - core, :, pl.ds(0, 3 * width)] = jnp.zeros((features, 3 * width), BF)
    for h in range(2):
        rest_ref[h, apart, out_cols] = jnp.zeros((width, width), BF)
    for copy in loads[:4]:
        copy.wait()
    out_w = jnp.concatenate([ow_ref[0], ow_ref[1]], axis=1)

    @pl.loop(0, length // ROWS)
    def _(i):
        row0 = pl.multiple_of(i * ROWS, ROWS)
        rows = pl.ds(row0, ROWS)
        dg = dot(mid_ref[rows, :], out_w, ((1,), (1,)))
        first = row0 + lax.broadcasted_iota(jnp.int32, (ROWS, width), 0) < split
        pad[pl.ds(row0 + 8, ROWS), pl.ds(0, width)] = dg * conv_ref[rows, :].astype(F32)
        dc = dg * q_ref[rows, :].astype(F32)
        g[0, rows, :] = jnp.where(first, dc, 0.0).astype(BF)
        g[1, rows, :] = jnp.where(first, 0.0, dc).astype(BF)

    scale = 1.0 / half
    for copy in loads[4:7]:
        copy.wait()

    def transform(spans):
        @pl.loop(0, half // BINS)
        def _(i):
            rows = pl.ds(pl.multiple_of(i * 2 * BINS, 2 * BINS), 2 * BINS)
            f = fh_ref[rows, :].astype(F32)
            fr, fi = f[:BINS], f[BINS:]
            er = None
            for m in range(2):
                s = dot(fwd_ref[rows, spans[m]], g[m, spans[m], :])
                sr, si = s[:BINS], s[BINS:]
                prod[m, rows, 0:width] = jnp.concatenate(
                    [(fr * sr + fi * si) * scale, (fr * si - fi * sr) * scale], axis=0
                ).astype(BF)
                w = uh_ref[m, rows, :].astype(F32)
                wr, wi = w[:BINS], w[BINS:]
                tr = wr * sr + wi * si
                ti = wr * si - wi * sr
                er, ei = (tr, ti) if er is None else (er + tr, ei + ti)
            e = jnp.concatenate([er * scale, ei * scale], axis=0).astype(BF)
            for m in range(2):
                prod[m, rows, width : 2 * width] = e

    by_corner(split, length, transform)
    corner = split // ROWS
    value_cols = pl.ds(2 * width, width)
    for copy in loads[7:10]:
        copy.wait()
    kpad[pl.ds(8, length), :] = key_ref[...].astype(F32)

    @pl.loop(0, length // ROWS)
    def _(i):
        row0 = pl.multiple_of(i * ROWS, ROWS)
        rows = pl.ds(row0, ROWS)
        spot = pl.ds(row0 + 8, ROWS)
        pick = (i > corner).astype(jnp.int32)
        both = dot(inv_ref[rows, :], prod[pick])
        pad[spot, value_cols] = both[:, :width]

        @pl.when(i == corner)
        def _():
            later = i * ROWS + lax.broadcasted_iota(jnp.int32, (ROWS, width), 0) >= split
            other = dot(inv_ref[rows, :], prod[1, :, 0:width])
            pad[spot, value_cols] = jnp.where(later, other, pad[spot, value_cols])

        inside = row0 + lax.broadcasted_iota(jnp.int32, (ROWS, width), 0) < half
        epad[spot, :] = jnp.where(inside, both[:, width:], 0.0) * decay_ref[rows, :]

    def key_taps(row0, same):
        spot = pl.ds(row0 + 8, CHUNK)
        for strip in range(strips):
            cols = pl.ds(strip * STRIP, STRIP)
            e = epad[spot, cols]
            pad[spot, pl.ds(width + strip * STRIP, STRIP)] = weigh(shifted(epad, row0, cols, same), cw_ref, 2, cols, True)
            for off, x in enumerate(shifted(kpad, row0, cols, same)):
                dcw_sum[off, :, cols] += (x * e).reshape(CHUNK // 8, 8, STRIP).sum(0)

    for copy in loads[15:]:
        copy.wait()
    cw_ref[...] = ct_ref[...].astype(F32).T
    sw_ref[...] = st_ref[...].astype(F32).T
    over_chunks(length, split, key_taps)
    loads[10].wait()

    @pl.loop(0, 3 * strips)
    def _(strip):
        cols = pl.ds(pl.multiple_of(strip * STRIP, STRIP), STRIP)
        kpad[pl.ds(8, length), pl.ds(0, STRIP)] = br_ref[:, cols].astype(F32)

        def branch_taps(row0, same):
            e = pad[pl.ds(row0 + 8, CHUNK), cols]
            total = weigh(shifted(pad, row0, cols, same), sw_ref, 0, cols, True)
            dbr_ref[pl.ds(row0, CHUNK), cols] = total.astype(BF)
            for off, x in enumerate(shifted(kpad, row0, pl.ds(0, STRIP), same)):
                dsw_sum[off, :, cols] += (x * e).reshape(CHUNK // 8, 8, STRIP).sum(0)

        over_chunks(length, split, branch_taps)

    ch_rows[1:2, :] = dmg_ref[...]
    st_rows[0:5, :] = jnp.sum(dsw_sum[...], axis=1)
    ch_rows[2:7, part] = jnp.sum(dcw_sum[...], axis=1)
    dch_ref[...] = ch_rows[...].T.astype(BF)
    for p in range(3):
        rows = pl.ds(pl.multiple_of(p * features + core * width, STRIP), width)
        dst_ref[rows, :] = st_rows[:, p * width : (p + 1) * width].T.astype(BF)
    for copy in loads[11:15]:
        copy.wait()
    d_out = dot(gated_ref[...], mid_ref[...], ((0,), (0,))).astype(BF)
    for h in range(2):
        rest_ref[h, part, out_cols] = d_out[:, h * width : (h + 1) * width]
    for cols in (pl.ds(0, 2 * width), pl.ds(2 * width, width)):
        d_in = dot(own_ref[...], dbr_ref[near, cols], ((0,), (0,)))
        d_in += dot(other_ref[...], dbr_ref[far, cols], ((0,), (0,)))
        rest_ref[core, :, cols] = d_in.astype(BF)
    dn_ref[...] = dot(dbr_ref[near, :], iw_ref[...], ((1,), (1,))).astype(BF)
    dn_send_ref[...] = dot(dbr_ref[far, :], iw_ref[...], ((1,), (1,))).astype(BF)


def local_call(kernel, args, direct, outs, direct_outs, scratch):
    vmem, anywhere = pl.BlockSpec(memory_space=pltpu.VMEM), pl.BlockSpec(memory_space=pl.ANY)
    return pl.pallas_call(
        kernel,
        out_shape=[jax.ShapeDtypeStruct(shape, dtype) for shape, dtype in outs],
        in_specs=[pl.BlockSpec(memory_space=pltpu.SMEM)]
        + [vmem] * (direct - 1)
        + [anywhere] * (len(args) - direct),
        out_specs=[vmem] * direct_outs + [anywhere] * (len(outs) - direct_outs),
        scratch_shapes=scratch,
        compiler_params=pltpu.CompilerParams(vmem_limit_bytes=VMEM_LIMIT),
    )(*args)


def tap_scratch(width):
    return [((width, LANES), BF), ((3 * width, LANES), BF), ((LANES, width), F32), ((LANES, 3 * width), F32)]


def mixer_forward(layer, scalars, own, other, ch, st, weight, decay, fwd, inv):
    length, width = decay.shape
    features = own.shape[1]
    bins = fwd.shape[0]
    tall, short, wide = (length, width), (own.shape[0], width), (length, 3 * width)
    kept = [(wide, BF), (tall, BF), (tall, BF), (tall, BF), ((bins, width), BF), ((2, bins, width), BF)]
    scratch = [((features, 3 * width), BF), (tall, F32), (fwd.shape, BF), (inv.shape, BF)] + kept + tap_scratch(width)
    scratch += [
        ((length + 16, 3 * width), F32),
        ((length + 16, width), F32),
        (tall, BF),
        ((2,) + tall, BF),
        ((2, bins, width), BF),
    ]
    return local_call(
        functools.partial(mixer_forward_kernel, layer),
        (scalars, own, other, ch, st, weight, decay, fwd, inv),
        3,
        [(tall, BF), (short, BF), (short, BF)] + kept,
        3,
        [pltpu.VMEM(*x) for x in scratch] + [pltpu.SemaphoreType.DMA((8,)), pltpu.SemaphoreType.DMA((6,))],
    )


def mixer_backward(
    layer, scalars, mid_own, mid_other, dmg, ch, st, weight, own, other, gated, br, decay, fwd, inv, q, key, conv, fh, uh
):
    length, width = decay.shape
    bins = fwd.shape[0]
    rows, features = mid_own.shape
    held = (own, other, gated, br, decay, fwd, inv, q, key, conv, fh, uh)
    scratch = [((2, width, width), BF), ((features, 3 * width), BF)] + [(x.shape, x.dtype) for x in held] + tap_scratch(width)
    scratch += [
        ((length + 16, 3 * width), F32),
        ((length + 16, width), F32),
        ((length + 16, width), F32),
        ((2, length, width), BF),
        ((2, bins, 2 * width), BF),
        ((length, features), BF),
        ((length, 3 * width), BF),
        ((5, 8, 3 * width), F32),
        ((5, 8, width), F32),
        ((LANES, features), F32),
        ((LANES, 3 * width), F32),
    ]
    return local_call(
        functools.partial(mixer_backward_kernel, layer),
        (scalars, mid_own, mid_other, dmg, ch, st, weight) + held,
        4,
        [
            ((2, features, 4 * width), BF),
            ((rows, features), BF),
            ((rows, features), BF),
            ((features, LANES), BF),
            ((3 * features, LANES), BF),
        ],
        5,
        [pltpu.VMEM(*x) for x in scratch] + [pltpu.SemaphoreType.DMA((19,))],
    )


def cube(dp_count):
    bits = (dp_count // 2).bit_length() - 1
    core, seq = bits, bits + 1
    low, rest = [bits - 1], list(range(bits - 1))
    orders = (
        rest + [seq] + low, rest + low + [seq], low + [seq] + rest,
        low + rest + [seq], [seq] + rest + low, [seq] + low + rest,
    )
    return bits, core, seq, orders


def place(bits):
    dp, seq = lax.axis_index("dp"), lax.axis_index("seq")
    coords = [(dp // (2 << (bits - 1 - d))) % 2 for d in range(bits)] + [dp % 2, seq]

    def neighbour(d):
        if d == bits + 1:
            return dp, 1 - seq
        step = 1 if d == bits else 2 << (bits - 1 - d)
        return dp + step * (1 - 2 * coords[d]), seq

    return coords, neighbour


def region(fixed, dims):
    return tuple(fixed[d] if d in fixed else slice(None) for d in range(dims))


def across(coords, bits):
    dp = lax.axis_index("dp")
    core, seq = coords[bits], coords[bits + 1]
    return core != seq, (dp + 1 - 2 * core, 1 - seq)


def greet(neighbours):
    barrier = pltpu.get_barrier_semaphore()
    for device in neighbours:
        pl.semaphore_signal(barrier, inc=1, device_id=device, device_id_type=pl.DeviceIdType.MESH)
    pl.semaphore_wait(barrier, len(neighbours))


class Swap:
    def __init__(self, src, dst, send, recv, local, moves, partner):
        self.stays, self.moves = jnp.logical_not(moves), moves
        self.away = pltpu.make_async_remote_copy(
            src_ref=src, dst_ref=dst, send_sem=send, recv_sem=recv,
            device_id=partner, device_id_type=pl.DeviceIdType.MESH,
        )
        self.here = pltpu.make_async_copy(src, dst, local)

    def start(self):
        pl.when(self.moves)(lambda: self.away.start())
        pl.when(self.stays)(lambda: self.here.start())

    def wait(self):
        pl.when(self.moves)(lambda: self.away.wait())
        pl.when(self.stays)(lambda: self.here.wait())


def remote(src, dst, send, recv, device):
    copy = pltpu.make_async_remote_copy(
        src_ref=src, dst_ref=dst, send_sem=send, recv_sem=recv,
        device_id=device, device_id_type=pl.DeviceIdType.MESH,
    )
    copy.start()
    return copy


GATHER_UNITS = (
    (3, 0, 640, 0, 0), (3, 640, 512, 1, 0), (3, 1152, 384, 2, 0), (5, 0, 128, 2, 0), (6, 0, 128, 1, 0),
    (0, 0, 768, 0, 1), (0, 768, 768, 1, 1), (2, 2, 2, 2, 1),
    (0, 1536, 768, 0, 2), (0, 2304, 768, 1, 2),
    (1, 0, 2, 0, 3), (1, 2, 2, 1, 3), (4, 1280, 256, 2, 3),
    (4, 0, 640, 0, 4), (4, 640, 640, 1, 4),
    (2, 0, 1, 0, 5), (2, 1, 1, 1, 5),
)
SCATTER_UNITS = (
    (0, 0, 768, 0, 0), (0, 768, 768, 1, 0), (2, 2, 2, 2, 0),
    (0, 1536, 768, 0, 1), (0, 2304, 768, 1, 1), (3, 1280, 256, 2, 1),
    (1, 0, 2, 0, 2), (1, 2, 2, 1, 2), (4, 1280, 256, 2, 2),
    (3, 0, 640, 0, 3), (3, 640, 640, 2, 3), (5, 0, 128, 2, 3), (6, 0, 128, 2, 3),
    (4, 0, 640, 0, 4), (4, 640, 640, 1, 4), (7, 0, 128, 2, 4),
    (2, 0, 1, 0, 5), (2, 1, 1, 0, 5),
)


def piece_of(unit, slabs):
    span = pl.ds(unit[1], unit[2])
    return (span, slice(None), slice(None)) if slabs else (slice(None), span)


def ticks(units, stages, shrinking):
    steps = [max(2**t, 2 ** (stages - 2)) for t in range(stages)]
    if shrinking:
        steps = steps[::-1]
    spacing = 2**stages // 4
    due = []
    for i, unit in enumerate(units):
        if shrinking:
            due.append((spacing * (unit[4] - 1) - 1, i, -1))
        due += [(spacing * unit[4] + sum(steps[:t]), i, t) for t in range(stages + 1)]
    return [(i, t) for _, i, t in sorted(due)]


def gather_kernel(dp_count, units, rows_in, rows_out, own, full, sems):
    bits, core_dim, _, orders = cube(dp_count)
    dims = bits + 2
    stages = dims - 1
    coords, neighbour = place(bits)
    core = coords[core_dim]
    sibling = neighbour(core_dim)
    moves, partner = across(coords, bits)
    greet([neighbour(d) for d in range(dims)] + [partner])
    ici_send, ici_recv, core_send, core_recv, local, swap_send, swap_recv, swap_local = sems
    swaps = [
        Swap(src, dst, swap_send.at[i], swap_recv.at[i], swap_local.at[i], moves, partner)
        for i, (src, dst) in enumerate(zip(rows_in, rows_out))
    ]
    mine = region(dict(enumerate(coords)), dims)
    firsts, forwards, sends = [], [], []
    last = [None] * len(units)
    for u, unit in enumerate(units):
        array, tail = unit[0], piece_of(unit, len(own[unit[0]].shape) == 4)
        piece = own[array].at[(slice(None),) + tail]
        here = full[array].at[(slice(None),) + mine + tail]
        keep = pltpu.make_async_copy(piece, here, local.at[u])
        keep.start()
        firsts.append((keep, remote(piece, here, core_send.at[u, 0], core_recv.at[u, 0], sibling)))
    for number, (u, t) in enumerate(ticks(units, stages, False)):
        if number == 10:
            for swap in swaps:
                swap.start()
        unit = units[u]
        array, tail, order = unit[0], piece_of(unit, len(own[unit[0]].shape) == 4), orders[unit[3]]
        fixed = {e: coords[e] for e in order[t:]}
        if t == 0:
            firsts[u][0].wait()
            firsts[u][1].wait_recv()
        else:
            last[u].wait_recv()
            got = full[array].at[(core,) + region(fixed | {order[t - 1]: 1 - coords[order[t - 1]]}, dims) + tail]
        if t < stages:
            held = full[array].at[(core,) + region(fixed, dims) + tail]
            last[u] = remote(held, held, ici_send.at[u, t], ici_recv.at[u, t], neighbour(order[t]))
            sends.append(last[u])
        if t > 0:
            forwards.append(remote(got, got, core_send.at[u, t], core_recv.at[u, t], sibling))
    for swap in swaps:
        swap.wait()
    beside = remote(rows_out[0], rows_out[-1], swap_send.at[len(swaps)], swap_recv.at[len(swaps)], sibling)
    for keep, copy in firsts:
        copy.wait_send()
    for copy in forwards:
        copy.wait()
    for copy in sends:
        copy.wait_send()
    beside.wait()


def gather_weights(rows, own, dp_count, number):
    bits = cube(dp_count)[0]
    stages = bits + 1
    units = GATHER_UNITS
    arrays = len(own)
    count = len(units)

    def body(*refs):
        rows_in, refs = refs[: len(rows)], refs[len(rows) :]
        own_refs, refs = refs[:arrays], refs[arrays:]
        rows_out, refs = refs[: len(rows) + 1], refs[len(rows) + 1 :]
        gather_kernel(dp_count, units, rows_in, rows_out, own_refs, refs[:arrays], refs[arrays:])

    grid = (2,) * (bits + 2)
    anywhere = pl.BlockSpec(memory_space=pl.ANY)
    return pl.pallas_call(
        body,
        out_shape=[jax.ShapeDtypeStruct(x.shape, x.dtype) for x in (*rows, rows[0])]
        + [jax.ShapeDtypeStruct(x.shape[:1] + grid + x.shape[1:], x.dtype) for x in own],
        in_specs=[anywhere] * (len(rows) + arrays),
        out_specs=[anywhere] * (len(rows) + 1 + arrays),
        scratch_shapes=[pltpu.SemaphoreType.DMA((count, stages))] * 2
        + [pltpu.SemaphoreType.DMA((count, stages + 1))] * 2
        + [pltpu.SemaphoreType.DMA((count,))]
        + [pltpu.SemaphoreType.DMA((len(rows) + 1,))] * 3,
        compiler_params=pltpu.CompilerParams(collective_id=number, has_side_effects=True),
    )(*rows, *own)


def scatter_kernel(dp_count, units, ends_in, token_ref, grads, outs, held, first, arrived, final, work, sems):
    bits, core_dim, _, orders = cube(dp_count)
    dims = bits + 2
    stages = dims - 1
    coords, neighbour = place(bits)
    core = coords[core_dim]
    sibling = neighbour(core_dim)
    moves, partner = across(coords, bits)
    greet([neighbour(d) for d in range(dims)] + [partner])
    ici_send, ici_recv, core_send, core_recv, local, end_send, end_recv, end_local = sems
    x_ref, dn_ref, away_ref, dmid_ref, gain_ref, dng_ref = ends_in
    other_ref, grad_ref, sum_ref, flat_ref, tall_ref, slab_ref = work
    grads = list(grads) + [slab_ref]
    exchange = remote(away_ref, other_ref, end_send.at[0], end_recv.at[0], sibling)
    begin = pltpu.make_async_copy(dmid_ref, grad_ref, end_local.at[1])
    begin.start()
    swap = Swap(grad_ref, token_ref, end_send.at[1], end_recv.at[1], end_local.at[0], moves, partner)

    def finish_rows():
        exchange.wait()
        begin.wait()
        sum_ref[...] = jnp.zeros(sum_ref.shape, F32)
        share = slab_ref.shape[-2]

        @pl.loop(0, x_ref.shape[0] // 128)
        def _(i):
            rows = pl.ds(pl.multiple_of(i * 128, 128), 128)
            d = dn_ref[rows, :].astype(F32) + other_ref[rows, :].astype(F32)
            dx, dg = norm_back(x_ref[rows, :].astype(F32), gain_ref[...], d)
            grad_ref[rows, :] += dx
            sum_ref[0:1, :] += dg

        swap.start()
        flat_ref[...] = jnp.zeros(flat_ref.shape, F32)
        for layer, row in enumerate((sum_ref, dng_ref)):
            for c in range(tall_ref.shape[0] // LANES):
                cols = slice(c * LANES, (c + 1) * LANES)
                flat_ref[0:1, :] = row[0:1, cols]
                tall_ref[cols, :] = flat_ref[...].T
            for i in range(2**dims):
                at = tuple((i >> (dims - 1 - d)) % 2 for d in range(dims))
                slab_ref[(layer,) + at] = tall_ref[i * share : (i + 1) * share, :].astype(BF)

    everything = region({}, dims)

    def add(u, fixed, extra):
        free = [d for d in range(dims) if d not in fixed]

        @pl.loop(0, 2 ** len(free))
        def _(i):
            at = {d: (i // 2 ** (len(free) - 1 - j)) % 2 for j, d in enumerate(free)}
            index = tuple(at[d] if d in at else fixed[d] for d in range(dims))
            held[u][index] += extra[tuple(at[d] for d in free)]

    starts, sends = [None] * len(units), []
    last = [None] * len(units)
    for u, t in ticks(units, stages, True):
        if t < 0 and units[u][0] == len(grads) - 1:
            finish_rows()
        if t < 0:
            array, tail = units[u][0], piece_of(units[u], len(outs[units[u][0]].shape) == 4)
            load = pltpu.make_async_copy(grads[array].at[(core,) + everything + tail], held[u], local.at[u, 0])
            load.start()
            other = grads[array].at[(1 - core,) + everything + tail]
            starts[u] = (load, remote(other, first[u], core_send.at[u, 0], core_recv.at[u, 0], sibling))
            continue
        order = orders[units[u][3]][::-1]
        fixed = {d: coords[d] for d in order[:t]}
        if t == 0:
            starts[u][0].wait()
            starts[u][1].wait_recv()
            add(u, fixed, first[u])
        else:
            last[u].wait_recv()
            add(u, fixed, arrived[u][t - 1])
        if t < stages:
            away = held[u].at[region(fixed | {order[t]: 1 - coords[order[t]]}, dims)]
            last[u] = remote(away, arrived[u][t], ici_send.at[u, t], ici_recv.at[u, t], neighbour(order[t]))
            sends.append(last[u])
        else:
            away = held[u].at[region(fixed | {core_dim: 1 - core}, dims)]
            last[u] = remote(away, final[u], core_send.at[u, 1], core_recv.at[u, 1], sibling)
    ends = []
    mine = region(dict(enumerate(coords)), dims)
    for u, unit in enumerate(units):
        array, tail = unit[0], piece_of(unit, len(outs[unit[0]].shape) == 4)
        own = pltpu.make_async_copy(held[u].at[mine], outs[array].at[(core,) + tail], local.at[u, 1])
        own.start()
        last[u].wait_recv()
        other = pltpu.make_async_copy(final[u], outs[array].at[(1 - core,) + tail], local.at[u, 2])
        other.start()
        ends += [own, other]
    swap.wait()
    for copy in ends:
        copy.wait()
    for copy in sends + last + [s[1] for s in starts]:
        copy.wait_send()


def scatter_grads(ends, grads, units, dp_count, number):
    bits = cube(dp_count)[0]
    dims = bits + 2
    stages = dims - 1
    count = len(units)
    grid = (2,) * dims
    rows, features = ends[0].shape
    share = grads[0].shape[1 + dims]
    tails = [x.shape[1 + dims :] for x in grads] + [(share, LANES)]
    arrays = len(tails)
    slabs = []
    for array, _, size, _, _ in units:
        shape = tails[array]
        slabs.append((size,) + shape[1:] if len(shape) == 3 else shape[:-1] + (size,))
    work = [((rows, features), BF), ((rows, features), F32), ((8, features), F32), ((LANES, LANES), F32)]
    work += [((features, LANES), F32), ((2,) + grid + (share, LANES), BF)]

    def body(*refs):
        ends_in, refs = refs[: len(ends)], refs[len(ends) :]
        grads_in, refs = refs[: len(grads)], refs[len(grads) :]
        token, outs, refs = refs[0], refs[1 : 1 + arrays], refs[1 + arrays :]
        held, first, final = refs[:count], refs[count : 2 * count], refs[2 * count : 3 * count]
        refs = refs[3 * count :]
        arrived = [refs[u * stages : (u + 1) * stages] for u in range(count)]
        refs = refs[count * stages :]
        scatter_kernel(
            dp_count, units, ends_in, token, grads_in, outs, held, first, arrived, final,
            refs[: len(work)], refs[len(work) :],
        )

    anywhere, vmem = pl.BlockSpec(memory_space=pl.ANY), pl.BlockSpec(memory_space=pltpu.VMEM)
    return pl.pallas_call(
        body,
        out_shape=[jax.ShapeDtypeStruct((rows, features), F32)]
        + [jax.ShapeDtypeStruct((2,) + tail, BF) for tail in tails],
        in_specs=[vmem, vmem, anywhere, anywhere, vmem, vmem] + [anywhere] * len(grads),
        out_specs=[anywhere] * (1 + arrays),
        scratch_shapes=[pltpu.VMEM(grid + slab, BF) for slab in slabs] * 2
        + [pltpu.VMEM(slab, BF) for slab in slabs]
        + [pltpu.VMEM((2,) * (dims - 1 - t) + slab, BF) for slab in slabs for t in range(stages)]
        + [pltpu.VMEM(*x) for x in work]
        + [pltpu.SemaphoreType.DMA((count, stages))] * 2
        + [pltpu.SemaphoreType.DMA((count, 2))] * 2
        + [pltpu.SemaphoreType.DMA((count, 3))]
        + [pltpu.SemaphoreType.DMA((2,))] * 2
        + [pltpu.SemaphoreType.DMA((2,))],
        compiler_params=pltpu.CompilerParams(
            collective_id=number, has_side_effects=True, vmem_limit_bytes=VMEM_LIMIT
        ),
    )(*ends, *grads)


def norm_parts(x):
    center = x - jnp.mean(x, axis=-1, keepdims=True)
    r = lax.rsqrt(jnp.mean(center * center, axis=-1, keepdims=True) + EPS)
    return center * r, r


def norm_back(x, gain, d):
    xhat, r = norm_parts(x)
    h = d * gain
    dx = r * (h - jnp.mean(h, axis=-1, keepdims=True) - xhat * jnp.mean(h * xhat, axis=-1, keepdims=True))
    return dx, jnp.sum(d * xhat, axis=0, keepdims=True)


SLOPE = math.sqrt(2.0 / math.pi)
CUBE = 0.044715


def gelu_parts(x):
    square = x * x
    t = jnp.tanh(SLOPE * (x + CUBE * square * x))
    flat = 0.5 + 0.5 * t
    return x * flat, flat + 0.5 * x * (1.0 - t * t) * (SLOPE + 3.0 * SLOPE * CUBE * square)


def mlp_forward_kernel(
    gain, next_gain, scalar_ref, x_ref, g0_ref, g1_ref, o0_ref, o1_ref, gains_ref, wg_ref, wu_ref, d0_ref, d1_ref,
    mid_ref, hm_ref, pre_ref, out_ref, next_ref,
):
    j = pl.program_id(0)

    @pl.when(j == 0)
    def _():
        width = g0_ref.shape[1]
        mid = x_ref[...]
        for ref, side in ((g0_ref, scalar_ref[1]), (g1_ref, 1 - scalar_ref[1])):
            rows = pl.ds(pl.multiple_of(side * width, STRIP), width)
            mid += dot(ref[...], jnp.concatenate([o0_ref[rows, :], o1_ref[rows, :]], axis=1))
        mid_ref[...] = mid
        out_ref[...] = mid
        hm_ref[...] = (norm_parts(mid)[0] * gains_ref[gain : gain + 1, :]).astype(BF)

    hm = hm_ref[...]
    total = out_ref[...]
    for i in range(TILE // PART_F):
        part = slice(i * PART_F, (i + 1) * PART_F)
        gate = dot(hm, wg_ref[:, part])
        up = dot(hm, wu_ref[:, part])
        pre_ref[0, :, part] = gate.astype(BF)
        pre_ref[1, :, part] = up.astype(BF)
        hid = (gelu_parts(gate)[0] * up).astype(BF)
        total += dot(hid, jnp.concatenate([d0_ref[part, :], d1_ref[part, :]], axis=1))
    out_ref[...] = total

    @pl.when(j == pl.num_programs(0) - 1)
    def _():
        next_ref[...] = (norm_parts(out_ref[...])[0] * gains_ref[next_gain : next_gain + 1, :]).astype(BF)


def mlp_backward_kernel(
    gain, g_ref, hm_ref, mid_ref, gains_ref, pre_ref, wg_ref, wu_ref, d0_ref, d1_ref,
    dgu_ref, ddn_ref, dmid_ref, mlow_ref, dmg_ref,
    glow, hm_t, acc,
):
    j = pl.program_id(0)
    width = d0_ref.shape[1]

    @pl.when(j == 0)
    def _():
        glow[...] = g_ref[...].astype(BF)
        hm_t[...] = hm_ref[...].T
        acc[...] = jnp.zeros(acc.shape, F32)

    low, hm = glow[...], hm_t[...]
    total = acc[...]
    for i in range(TILE // PART_B):
        part = slice(i * PART_B, (i + 1) * PART_B)
        dh = dot(low, jnp.concatenate([d0_ref[part, :], d1_ref[part, :]], axis=1), ((1,), (1,)))
        value, slope = gelu_parts(pre_ref[0, :, part].astype(F32))
        up = pre_ref[1, :, part].astype(F32)
        hid = (value * up).astype(BF)
        d_gate = (dh * up * slope).astype(BF)
        d_up = (dh * value).astype(BF)
        d_down = dot(hid, low, ((0,), (0,))).astype(BF)
        ddn_ref[0, part, :] = d_down[:, :width]
        ddn_ref[1, part, :] = d_down[:, width:]
        for h, d in enumerate((d_gate, d_up)):
            grad = dot(hm, d).astype(BF)
            if len(dgu_ref.shape) == 3:
                dgu_ref[h, :, part] = grad
            else:
                dgu_ref[:, h * TILE + i * PART_B : h * TILE + (i + 1) * PART_B] = grad
        total += dot(d_gate, wg_ref[:, part], ((1,), (1,))) + dot(d_up, wu_ref[:, part], ((1,), (1,)))
    acc[...] = total

    @pl.when(j == pl.num_programs(0) - 1)
    def _():
        dx, dg = norm_back(mid_ref[...], gains_ref[gain : gain + 1, :], acc[...])
        dmid = g_ref[...] + dx
        dmid_ref[...] = dmid
        mlow_ref[...] = dmid.astype(BF)
        dmg_ref[...] = dg


TILE = 512
PART_F = 512
PART_B = 512


def whole(shape):
    return pl.BlockSpec(shape, lambda j: (0,) * len(shape))


def weight_specs(layout, hidden, features):
    steps = hidden // TILE
    gate_up = pl.BlockSpec((features, TILE), lambda j: (0, j))
    up = pl.BlockSpec((features, TILE), lambda j: (1, j) if layout == "halves" else (0, steps + j))
    down = [
        pl.BlockSpec((TILE, features // 2), lambda j: (j, 0)),
        pl.BlockSpec((TILE, features // 2), lambda j: (steps + j, 0)),
    ]
    return [gate_up, up] + down


def mlp_forward(scalars, x, g0, g1, weight, gains, gain, next_gain, weights):
    layout, gu, dn = weights
    rows, features = x.shape
    hidden = dn.shape[0] // 2
    square = whole((rows, features))
    narrow = [whole(a.shape) for a in (g0, g1)]
    narrow += [pl.BlockSpec((features, features // 2), lambda j, h=h: (h, 3)) for h in range(2)]
    shapes = [((rows, features), F32), ((rows, features), BF), ((2, rows, hidden), BF), ((rows, features), F32), ((rows, features), BF)]
    return pl.pallas_call(
        functools.partial(mlp_forward_kernel, gain, next_gain),
        grid=(hidden // TILE,),
        out_shape=[jax.ShapeDtypeStruct(*s) for s in shapes],
        in_specs=[pl.BlockSpec(memory_space=pltpu.SMEM), square] + narrow + [whole(gains.shape)] + weight_specs(layout, hidden, features),
        out_specs=[square, square, pl.BlockSpec((2, rows, TILE), lambda j: (0, 0, j)), square, square],
        compiler_params=pltpu.CompilerParams(vmem_limit_bytes=VMEM_LIMIT),
    )(scalars, x, g0, g1, weight, weight, gains, gu, gu, dn, dn)


def mlp_backward(g, hm, mid, gains, gain, pre, weights, side_by_side):
    layout, gu, dn = weights
    rows, features = g.shape
    hidden = pre.shape[2]
    width = features // 2
    square, vector = whole((rows, features)), whole((1, features))
    both = (features, 2 * hidden) if side_by_side else (2, features, hidden)
    shapes = [(both, BF), ((2, hidden, width), BF), ((rows, features), F32), ((rows, features), BF), ((1, features), F32)]
    return pl.pallas_call(
        functools.partial(mlp_backward_kernel, gain),
        grid=(hidden // TILE,),
        out_shape=[jax.ShapeDtypeStruct(*s) for s in shapes],
        in_specs=[square] * 3
        + [whole(gains.shape), pl.BlockSpec((2, rows, TILE), lambda j: (0, 0, j))]
        + weight_specs(layout, hidden, features),
        out_specs=[
            pl.BlockSpec((features, 2 * TILE), lambda j: (0, j))
            if side_by_side
            else pl.BlockSpec((2, features, TILE), lambda j: (0, 0, j)),
            pl.BlockSpec((2, TILE, width), lambda j: (0, j, 0)),
            square, square, vector,
        ],
        scratch_shapes=[pltpu.VMEM((rows, features), BF), pltpu.VMEM((features, rows), BF), pltpu.VMEM((rows, features), F32)],
        compiler_params=pltpu.CompilerParams(vmem_limit_bytes=VMEM_LIMIT),
    )(g, hm, mid, gains, pre, gu, gu, dn, dn)


def shards(
    tokens, split_points, cotangent, norm_gain, in_weight, short_taps, cond_taps,
    out_weight, mlp_gain, gate_up, down_weight,
):
    rows, features = tokens.shape[1:]
    dp_count, seq_count = lax.axis_size("dp"), lax.axis_size("seq")
    devices = dp_count * seq_count
    length = rows * seq_count
    width = features // 2
    layers = in_weight.shape[0]
    share = norm_gain.shape[1]
    hidden = down_weight.shape[1] * devices
    core = lax.axis_index("dp") % 2
    seq = lax.axis_index("seq")

    swap = [(4 * k + a, 4 * k + 3 - a) for k in range(devices // 4) for a in (1, 2)]
    flip = [(i, i ^ 1) for i in range(dp_count)]

    def swap_rows(x):
        return jnp.where(core == seq, x, lax.ppermute(x, AXES, swap))

    def sibling(x):
        return lax.ppermute(x, "dp", flip)

    def beside(own, other, axis):
        return jnp.where(
            core == 0,
            jnp.concatenate([own, other], axis=axis),
            jnp.concatenate([other, own], axis=axis),
        )

    def half_of(x, which, axis):
        size = x.shape[axis] // 2
        return lax.dynamic_slice_in_dim(x, which * size, size, axis)

    def own_channels(x):
        parts = x.shape[-1] // features
        x = x.reshape(x.shape[:-1] + (parts, 2, width))
        x = lax.dynamic_index_in_dim(x, core, x.ndim - 2, keepdims=False)
        return x.reshape(x.shape[:-2] + (parts * width,))

    table = transform_matrix(length)
    fwd = jnp.asarray(table, BF)
    inv = jnp.asarray(np.ascontiguousarray(table.T), BF)
    decay = own_channels(decay_table(length, features))

    def halves(x):
        parts = x.shape[-1] // features
        x = x.reshape(x.shape[:-1] + (parts, 2, width))
        x = jnp.moveaxis(x, -2, 0)
        return x.reshape(x.shape[:-2] + (parts * width,))

    grid = (2,) * (cube(dp_count)[0] + 2)

    ch = jnp.concatenate([norm_gain[:, :, None], mlp_gain[:, :, None], cond_taps.transpose(0, 2, 1)], axis=2)
    ch = jnp.pad(ch, ((0, 0), (0, 0), (0, LANES - 7)))
    st = jnp.pad(short_taps.transpose(0, 2, 1), ((0, 0), (0, 0), (0, LANES - 5)))
    own = [gate_up[0].reshape(share, 2, hidden).transpose(1, 0, 2)]
    own += [halves(down_weight[layer]).reshape(2, hidden // features, share, width) for layer in range(layers)]
    for layer in range(layers):
        own.append(jnp.concatenate([halves(in_weight[layer]), halves(out_weight[layer])], axis=2))
    place_rows = [tokens[0], jnp.broadcast_to(split_points, (8, LANES))]
    x_low, split, x_far, *full = gather_weights(place_rows, own + [ch, st], dp_count, 0)
    downs = [x.reshape(2 * hidden, width) for x in full[1 : 1 + layers]]
    mixer_w = [x.reshape(2, features, 4 * width) for x in full[1 + layers : 1 + 2 * layers]]
    ch, st = full[-2].reshape(layers, features, LANES), full[-1].reshape(layers, 3 * features, LANES)
    late, _ = lax.optimization_barrier((gate_up[1:], full[0]))
    gate_ups = [("halves", full[0].reshape(2 * features, hidden))]
    gate_ups += [("plain", lax.all_gather(x, AXES, axis=0, tiled=True)) for x in late]
    gains = ch[:, :, :2].astype(F32).transpose(0, 2, 1).reshape(2 * layers, features)
    scalars = jnp.stack([split[0, 0], core.astype(jnp.int32)])
    stream, far = x_low.astype(F32), x_far.astype(F32)
    grad = swap_rows(cotangent)[0].astype(F32)
    normed, normed_far = [(norm_parts(x)[0] * gains[0]).astype(BF) for x in (stream, far)]
    kept = []
    for layer in range(layers):
        if layer > 0:
            normed_far = sibling(normed)
        gated, mine, away, branches, q, key, conv, fh, uh = mixer_forward(
            layer, scalars, normed, normed_far, ch, st, mixer_w[layer], decay, fwd, inv
        )
        middle, normed_mlp, pre, out, normed_next = mlp_forward(
            scalars, stream, mine, sibling(away), mixer_w[layer].reshape(2 * features, -1), gains,
            2 * layer + 1, (2 * layer + 2) % (2 * layers), gate_ups[layer] + (downs[layer],),
        )
        kept.append((stream, normed, normed_far, gated, branches, q, key, conv, fh, uh, middle, normed_mlp, pre))
        stream, normed = out, normed_next
    activations = swap_rows(stream.astype(BF)[None])

    summed = []
    early = [None] * layers
    for layer in reversed(range(layers)):
        x, normed, normed_far, gated, branches, q, key, conv, fh, uh, middle, normed_mlp, pre = kept[layer]
        d_gu, d_down, d_middle, m_low, d_mg = mlp_backward(
            grad, normed_mlp, middle, gains, 2 * layer + 1, pre, gate_ups[layer] + (downs[layer],), layer > 0
        )
        rest, d_normed, d_away, d_ch, d_st = mixer_backward(
            layer, scalars, m_low, sibling(m_low), d_mg, ch, st, mixer_w[layer], normed, normed_far, gated, branches,
            decay, fwd, inv, q, key, conv, fh, uh,
        )
        if layer > 0:
            early[layer] = lax.psum_scatter(d_gu, AXES, scatter_dimension=0, tiled=True)
            d_part, d_ng = norm_back(x, gains[2 * layer], d_normed.astype(F32) + sibling(d_away).astype(F32))
            grad = d_middle + d_part
        summed.append((d_gu, d_down, rest, d_ch, d_st))
    d_gus, d_downs, rests, *smalls = zip(*summed[::-1])
    pieces = [d_gus[0].reshape((2,) + grid + (share, hidden))]
    pieces += [x.reshape((2,) + grid + (hidden // features, share, width)) for x in d_downs]
    pieces += [x.reshape((2,) + grid + (share, 4 * width)) for x in rests]
    pieces += [jnp.stack(x).reshape((2,) + grid + (-1, LANES)) for x in smalls]
    ends = [x_low, d_normed, d_away, d_middle, gains[:1], d_ng]
    fits = share % 8 == 0
    units = tuple(unit for unit in SCATTER_UNITS if fits or unit[0] != 2)
    token_grad, *outs = scatter_grads(ends, pieces, units, dp_count, 1)
    if not fits:
        outs[2] = lax.psum_scatter(d_downs[1], AXES, scatter_dimension=1, tiled=True)
    token_grad = token_grad[None]

    def joined(x):
        parts = x.shape[-1] // width
        x = jnp.moveaxis(x.reshape(x.shape[:-1] + (parts, width)), 0, -2)
        return x.reshape(x.shape[:-3] + (parts * features,))

    early[0] = outs[0].transpose(1, 0, 2)
    for layer in range(1, layers):
        early[layer] = early[layer].reshape(share, hidden // TILE, 2, TILE).transpose(0, 2, 1, 3)
    g_gu = jnp.stack([x.reshape(share, 2 * hidden) for x in early]).astype(F32)
    g_down = jnp.stack([joined(x.reshape(2, -1, width)) for x in outs[1 : 1 + layers]]).astype(F32)
    rest = outs[1 + layers : 1 + 2 * layers]
    g_in = jnp.stack([joined(x[:, :, : 3 * width]) for x in rest]).astype(F32)
    g_out = jnp.stack([joined(x[:, :, 3 * width :]) for x in rest]).astype(F32)
    s_ch, s_st, s_ng = [x.astype(F32) for x in outs[1 + 2 * layers :]]
    g_ng, g_mg, g_ct, g_st = s_ng[:, :, 0], s_ch[:, :, 1], s_ch[:, :, 2:7].transpose(0, 2, 1), s_st[:, :, :5].transpose(0, 2, 1)
    return (
        activations,
        token_grad,
        g_ng,
        g_in,
        g_st,
        g_ct,
        g_out,
        g_mg,
        g_gu,
        g_down,
    )


def solution(mesh):
    every = ("dp", "seq")
    rows, part = P("dp", "seq", None), P(None, every, None)
    vector, taps = P(None, every), P(None, None, every)
    return jax.shard_map(
        shards,
        mesh=mesh,
        in_specs=(rows, P("dp"), rows, vector, part, taps, taps, part, vector, part, part),
        out_specs=(rows, rows, vector, part, taps, taps, part, vector, part, part),
        check_vma=False,
    )
```

```python
import functools
import math

import numpy as np
import jax
import jax.numpy as jnp
from jax import lax
from jax.experimental import pallas as pl
from jax.experimental.pallas import tpu as pltpu
from jax.sharding import PartitionSpec as P

BF = jnp.bfloat16
F32 = jnp.float32
EPS = 1e-05
AXES = ("dp", "seq")
GAP = 128
VMEM_LIMIT = 60 * 2**20
STRIP = 128
LANES = 128
BINS = 224
ROWS = 256
CHUNK = 128


def transform_matrix(length):
    half = length - GAP
    freq = np.arange(half)[:, None]
    place = np.arange(length)[None, :]
    angle = ((2 * freq + 1) * place % (4 * half)).astype(np.float64) * (math.pi / (2 * half))
    both = np.stack([np.cos(angle), -np.sin(angle)])
    both = both.reshape(2, half // BINS, BINS, length).transpose(1, 0, 2, 3)
    return both.reshape(2 * half, length).astype(np.float32)


def decay_table(length, features):
    channels = jnp.arange(features).astype(F32)
    positions = jnp.arange(length).astype(F32)
    rates = jnp.exp(math.log(1.0 / length) + channels / (features - 1) * math.log(4.0))
    scales = lax.rsqrt(jnp.sum(jnp.exp(-2.0 * positions[:, None] * rates[None, :]), axis=0))
    return jnp.exp(-positions[:, None] * rates[None, :]) * scales[None, :]


def dot(a, b, dims=((1,), (0,))):
    return lax.dot_general(a, b, (dims, ((), ())), preferred_element_type=F32)


def tap_same(row0, split):
    t = row0 + lax.broadcasted_iota(jnp.int32, (CHUNK, STRIP), 0)
    here = t >= split
    return [
        None if off == 2 else jnp.where(((t + (off - 2)) >= split) == here, 1.0, 0.0)
        for off in range(5)
    ]


def shifted(ref, row0, cols, same):
    block = ref[pl.ds(row0, CHUNK + 16), cols]
    out = []
    for off in range(5):
        turned = pltpu.roll(block, (2 - off) % (CHUNK + 16), 0) if off != 2 else block
        rows = turned[8 : 8 + CHUNK]
        out.append(rows if same[off] is None else rows * same[off])
    return out


def over_chunks(length, split, body):
    @pl.loop(0, length // CHUNK)
    def _(i):
        row0 = pl.multiple_of(i * CHUNK, CHUNK)
        touched = (split > row0 - 2) & (split < row0 + CHUNK + 2)

        @pl.when(touched)
        def _():
            body(row0, tap_same(row0, split))

        @pl.when(jnp.logical_not(touched))
        def _():
            body(row0, [None] * 5)


def tap_loads(layer, core, ch_hbm, st_hbm, ct_ref, st_ref):
    width = ct_ref.shape[0]
    own = pl.multiple_of(core * width, STRIP)
    pairs = [(ch_hbm.at[layer, pl.ds(own, width), :], ct_ref)]
    for part in range(3):
        rows = pl.ds(pl.multiple_of(part * 2 * width + own, STRIP), width)
        pairs.append((st_hbm.at[layer, rows, :], st_ref.at[pl.ds(part * width, width), :]))
    return pairs


def weigh(rows, w_ref, base, cols, flip):
    total = None
    for off, x in enumerate(rows):
        tap = base + (4 - off if flip else off)
        term = x * w_ref[tap : tap + 1, cols]
        total = term if total is None else total + term
    return total


def by_corner(split, length, body):
    for corner in range(length // ROWS):
        spans = (slice(0, (corner + 1) * ROWS), slice(corner * ROWS, length))
        pl.when(split // ROWS == corner)(functools.partial(body, spans))


def clear_ends(ref, length):
    ref[0:8, :] = jnp.zeros((8, ref.shape[1]), F32)
    ref[8 + length : 16 + length, :] = jnp.zeros((8, ref.shape[1]), F32)


def fetch(pairs, sems):
    copies = [pltpu.make_async_copy(src, dst, sems.at[i]) for i, (src, dst) in enumerate(pairs)]
    for copy in copies:
        copy.start()
    return copies


def mixer_forward_kernel(
    layer, scalar_ref, own_ref, other_ref, ch_hbm, st_hbm, iw_hbm, decay_hbm, fwd_hbm, inv_hbm,
    gated_ref, mine_ref, send_ref, br_hbm, q_hbm, key_hbm, conv_hbm, fh_hbm, uh_hbm,
    iw_ref, decay_ref, fwd_ref, inv_ref, br_ref, q_ref, key_ref, conv_ref, fh_ref, uh_ref,
    ct_ref, st_ref, cw_ref, sw_ref, pad, kpad, filt, u, prod, in_sems, out_sems,
):
    length, width = q_ref.shape
    rows_own = own_ref.shape[0]
    half = length - GAP
    split, core = scalar_ref[0], scalar_ref[1]
    strips = width // STRIP
    loads = fetch(
        [
            (iw_hbm.at[core, :, pl.ds(0, 3 * width)], iw_ref),
            (decay_hbm, decay_ref),
            (fwd_hbm, fwd_ref),
            (inv_hbm, inv_ref),
        ]
        + tap_loads(layer, core, ch_hbm, st_hbm, ct_ref, st_ref),
        in_sems,
    )
    outs = [(br_ref, br_hbm), (q_ref, q_hbm), (key_ref, key_hbm), (fh_ref, fh_hbm), (uh_ref, uh_hbm), (conv_ref, conv_hbm)]
    stores = [pltpu.make_async_copy(src, dst, out_sems.at[i]) for i, (src, dst) in enumerate(outs)]
    clear_ends(pad, length)
    clear_ends(kpad, length)
    loads[0].wait()
    for ref, side in ((own_ref, core), (other_ref, 1 - core)):

        @pl.loop(0, rows_own // ROWS)
        def _(i):
            row0 = pl.multiple_of(side * rows_own + i * ROWS, ROWS)
            low = dot(ref[pl.ds(pl.multiple_of(i * ROWS, ROWS), ROWS), :], iw_ref[...]).astype(BF)
            br_ref[pl.ds(row0, ROWS), :] = low
            pad[pl.ds(row0 + 8, ROWS), :] = low.astype(F32)

    stores[0].start()
    for copy in loads[4:]:
        copy.wait()
    cw_ref[...] = ct_ref[...].astype(F32).T
    sw_ref[...] = st_ref[...].astype(F32).T

    def mix(row0, same):
        rows = pl.ds(row0, CHUNK)
        first = row0 + lax.broadcasted_iota(jnp.int32, (CHUNK, STRIP), 0) < split
        for part in range(3):
            for strip in range(strips):
                cols = pl.ds(part * width + strip * STRIP, STRIP)
                own = pl.ds(strip * STRIP, STRIP)
                low = weigh(shifted(pad, row0, cols, same), sw_ref, 0, cols, False).astype(BF)
                if part == 0:
                    q_ref[rows, own] = low
                elif part == 1:
                    key_ref[rows, own] = low
                    kpad[pl.ds(row0 + 8, CHUNK), own] = low.astype(F32)
                else:
                    low = low.astype(F32)
                    u[0, rows, own] = jnp.where(first, low, 0.0).astype(BF)
                    u[1, rows, own] = jnp.where(first, 0.0, low).astype(BF)

    over_chunks(length, split, mix)
    stores[1].start()
    stores[2].start()
    loads[1].wait()

    def make_filter(row0, same):
        rows = pl.ds(row0, CHUNK)
        for strip in range(strips):
            cols = pl.ds(strip * STRIP, STRIP)
            total = weigh(shifted(kpad, row0, cols, same), cw_ref, 2, cols, False)
            filt[rows, cols] = (total * decay_ref[rows, cols]).astype(BF)

    over_chunks(length, split, make_filter)
    scale = 1.0 / half
    loads[2].wait()

    def transform(spans):
        @pl.loop(0, half // BINS)
        def _(i):
            rows = pl.ds(pl.multiple_of(i * 2 * BINS, 2 * BINS), 2 * BINS)
            f = dot(fwd_ref[rows, 0:half], filt[0:half, :])
            fr, fi = f[:BINS], f[BINS:]
            fh_ref[rows, :] = f.astype(BF)
            for m in range(2):
                s = dot(fwd_ref[rows, spans[m]], u[m, spans[m], :])
                uh_ref[m, rows, :] = s.astype(BF)
                sr, si = s[:BINS], s[BINS:]
                prod[m, rows, :] = jnp.concatenate(
                    [(fr * sr - fi * si) * scale, (fr * si + fi * sr) * scale], axis=0
                ).astype(BF)

    by_corner(split, length, transform)
    stores[3].start()
    stores[4].start()
    corner = split // ROWS
    loads[3].wait()

    @pl.loop(0, length // ROWS)
    def _(i):
        rows = pl.ds(pl.multiple_of(i * ROWS, ROWS), ROWS)
        pick = (i > corner).astype(jnp.int32)
        conv_ref[rows, :] = dot(inv_ref[rows, :], prod[pick]).astype(BF)

        @pl.when(i == corner)
        def _():
            later = i * ROWS + lax.broadcasted_iota(jnp.int32, (ROWS, width), 0) >= split
            other = dot(inv_ref[rows, :], prod[1])
            conv_ref[rows, :] = jnp.where(later, other, conv_ref[rows, :].astype(F32)).astype(BF)

        gated_ref[rows, :] = (q_ref[rows, :].astype(F32) * conv_ref[rows, :].astype(F32)).astype(BF)

    stores[5].start()
    mine_ref[...] = gated_ref[pl.ds(pl.multiple_of(core * rows_own, ROWS), rows_own), :]
    send_ref[...] = gated_ref[pl.ds(pl.multiple_of((1 - core) * rows_own, ROWS), rows_own), :]
    for copy in stores:
        copy.wait()


def mixer_backward_kernel(
    layer, scalar_ref, mid_own_ref, mid_other_ref, dmg_ref, ch_hbm, st_hbm,
    w_hbm, own_hbm, other_hbm, gated_hbm, br_hbm, decay_hbm, fwd_hbm, inv_hbm, q_hbm, key_hbm, conv_hbm, fh_hbm, uh_hbm,
    rest_ref, dn_ref, dn_send_ref, dch_ref, dst_ref,
    ow_ref, iw_ref, own_ref, other_ref, gated_ref, br_ref, decay_ref, fwd_ref, inv_ref, q_ref, key_ref, conv_ref, fh_ref,
    uh_ref, ct_ref, st_ref, cw_ref, sw_ref, pad, epad, kpad, g, prod, mid_ref, dbr_ref, dsw_sum, dcw_sum, ch_rows, st_rows,
    in_sems,
):
    length, width = q_ref.shape
    rows_own, features = own_ref.shape
    half = length - GAP
    split, core = scalar_ref[0], scalar_ref[1]
    strips = width // STRIP
    part = pl.ds(pl.multiple_of(core * width, STRIP), width)
    apart = pl.ds(pl.multiple_of((1 - core) * width, STRIP), width)
    near = pl.ds(pl.multiple_of(core * rows_own, ROWS), rows_own)
    far = pl.ds(pl.multiple_of((1 - core) * rows_own, ROWS), rows_own)
    out_cols = pl.ds(3 * width, width)
    loads = fetch(
        [
            (w_hbm.at[0, part, out_cols], ow_ref.at[0]),
            (w_hbm.at[1, part, out_cols], ow_ref.at[1]),
            (conv_hbm, conv_ref),
            (q_hbm, q_ref),
            (fwd_hbm, fwd_ref),
            (fh_hbm, fh_ref),
            (uh_hbm, uh_ref),
            (inv_hbm, inv_ref),
            (decay_hbm, decay_ref),
            (key_hbm, key_ref),
            (br_hbm, br_ref),
            (gated_hbm, gated_ref),
            (own_hbm, own_ref),
            (other_hbm, other_ref),
            (w_hbm.at[core, :, pl.ds(0, 3 * width)], iw_ref),
        ]
        + tap_loads(layer, core, ch_hbm, st_hbm, ct_ref, st_ref),
        in_sems,
    )
    mid_ref[near, :] = mid_own_ref[...]
    mid_ref[far, :] = mid_other_ref[...]
    clear_ends(pad, length)
    clear_ends(epad, length)
    clear_ends(kpad, length)
    dsw_sum[...] = jnp.zeros(dsw_sum.shape, F32)
    dcw_sum[...] = jnp.zeros(dcw_sum.shape, F32)
    ch_rows[...] = jnp.zeros(ch_rows.shape, F32)
    st_rows[...] = jnp.zeros(st_rows.shape, F32)
    for p in range(3):
        rows = pl.ds(pl.multiple_of(p * features + (1 - core) * width, STRIP), width)
        dst_ref[rows, :] = jnp.zeros((width, LANES), BF)
    rest_ref[1 - core, :, pl.ds(0, 3 * width)] = jnp.zeros((features, 3 * width), BF)
    for h in range(2):
        rest_ref[h, apart, out_cols] = jnp.zeros((width, width), BF)
    for copy in loads[:4]:
        copy.wait()
    out_w = jnp.concatenate([ow_ref[0], ow_ref[1]], axis=1)

    @pl.loop(0, length // ROWS)
    def _(i):
        row0 = pl.multiple_of(i * ROWS, ROWS)
        rows = pl.ds(row0, ROWS)
        dg = dot(mid_ref[rows, :], out_w, ((1,), (1,)))
        first = row0 + lax.broadcasted_iota(jnp.int32, (ROWS, width), 0) < split
        pad[pl.ds(row0 + 8, ROWS), pl.ds(0, width)] = dg * conv_ref[rows, :].astype(F32)
        dc = dg * q_ref[rows, :].astype(F32)
        g[0, rows, :] = jnp.where(first, dc, 0.0).astype(BF)
        g[1, rows, :] = jnp.where(first, 0.0, dc).astype(BF)

    scale = 1.0 / half
    for copy in loads[4:7]:
        copy.wait()

    def transform(spans):
        @pl.loop(0, half // BINS)
        def _(i):
            rows = pl.ds(pl.multiple_of(i * 2 * BINS, 2 * BINS), 2 * BINS)
            f = fh_ref[rows, :].astype(F32)
            fr, fi = f[:BINS], f[BINS:]
            er = None
            for m in range(2):
                s = dot(fwd_ref[rows, spans[m]], g[m, spans[m], :])
                sr, si = s[:BINS], s[BINS:]
                prod[m, rows, 0:width] = jnp.concatenate(
                    [(fr * sr + fi * si) * scale, (fr * si - fi * sr) * scale], axis=0
                ).astype(BF)
                w = uh_ref[m, rows, :].astype(F32)
                wr, wi = w[:BINS], w[BINS:]
                tr = wr * sr + wi * si
                ti = wr * si - wi * sr
                er, ei = (tr, ti) if er is None else (er + tr, ei + ti)
            e = jnp.concatenate([er * scale, ei * scale], axis=0).astype(BF)
            for m in range(2):
                prod[m, rows, width : 2 * width] = e

    by_corner(split, length, transform)
    corner = split // ROWS
    value_cols = pl.ds(2 * width, width)
    for copy in loads[7:10]:
        copy.wait()
    kpad[pl.ds(8, length), :] = key_ref[...].astype(F32)

    @pl.loop(0, length // ROWS)
    def _(i):
        row0 = pl.multiple_of(i * ROWS, ROWS)
        rows = pl.ds(row0, ROWS)
        spot = pl.ds(row0 + 8, ROWS)
        pick = (i > corner).astype(jnp.int32)
        both = dot(inv_ref[rows, :], prod[pick])
        pad[spot, value_cols] = both[:, :width]

        @pl.when(i == corner)
        def _():
            later = i * ROWS + lax.broadcasted_iota(jnp.int32, (ROWS, width), 0) >= split
            other = dot(inv_ref[rows, :], prod[1, :, 0:width])
            pad[spot, value_cols] = jnp.where(later, other, pad[spot, value_cols])

        inside = row0 + lax.broadcasted_iota(jnp.int32, (ROWS, width), 0) < half
        epad[spot, :] = jnp.where(inside, both[:, width:], 0.0) * decay_ref[rows, :]

    def key_taps(row0, same):
        spot = pl.ds(row0 + 8, CHUNK)
        for strip in range(strips):
            cols = pl.ds(strip * STRIP, STRIP)
            e = epad[spot, cols]
            pad[spot, pl.ds(width + strip * STRIP, STRIP)] = weigh(shifted(epad, row0, cols, same), cw_ref, 2, cols, True)
            for off, x in enumerate(shifted(kpad, row0, cols, same)):
                dcw_sum[off, :, cols] += (x * e).reshape(CHUNK // 8, 8, STRIP).sum(0)

    for copy in loads[15:]:
        copy.wait()
    cw_ref[...] = ct_ref[...].astype(F32).T
    sw_ref[...] = st_ref[...].astype(F32).T
    over_chunks(length, split, key_taps)
    loads[10].wait()

    @pl.loop(0, 3 * strips)
    def _(strip):
        cols = pl.ds(pl.multiple_of(strip * STRIP, STRIP), STRIP)
        kpad[pl.ds(8, length), pl.ds(0, STRIP)] = br_ref[:, cols].astype(F32)

        def branch_taps(row0, same):
            e = pad[pl.ds(row0 + 8, CHUNK), cols]
            total = weigh(shifted(pad, row0, cols, same), sw_ref, 0, cols, True)
            dbr_ref[pl.ds(row0, CHUNK), cols] = total.astype(BF)
            for off, x in enumerate(shifted(kpad, row0, pl.ds(0, STRIP), same)):
                dsw_sum[off, :, cols] += (x * e).reshape(CHUNK // 8, 8, STRIP).sum(0)

        over_chunks(length, split, branch_taps)

    ch_rows[1:2, :] = dmg_ref[...]
    st_rows[0:5, :] = jnp.sum(dsw_sum[...], axis=1)
    ch_rows[2:7, part] = jnp.sum(dcw_sum[...], axis=1)
    dch_ref[...] = ch_rows[...].T.astype(BF)
    for p in range(3):
        rows = pl.ds(pl.multiple_of(p * features + core * width, STRIP), width)
        dst_ref[rows, :] = st_rows[:, p * width : (p + 1) * width].T.astype(BF)
    for copy in loads[11:15]:
        copy.wait()
    d_out = dot(gated_ref[...], mid_ref[...], ((0,), (0,))).astype(BF)
    for h in range(2):
        rest_ref[h, part, out_cols] = d_out[:, h * width : (h + 1) * width]
    for cols in (pl.ds(0, 2 * width), pl.ds(2 * width, width)):
        d_in = dot(own_ref[...], dbr_ref[near, cols], ((0,), (0,)))
        d_in += dot(other_ref[...], dbr_ref[far, cols], ((0,), (0,)))
        rest_ref[core, :, cols] = d_in.astype(BF)
    dn_ref[...] = dot(dbr_ref[near, :], iw_ref[...], ((1,), (1,))).astype(BF)
    dn_send_ref[...] = dot(dbr_ref[far, :], iw_ref[...], ((1,), (1,))).astype(BF)


def local_call(kernel, args, direct, outs, direct_outs, scratch):
    vmem, anywhere = pl.BlockSpec(memory_space=pltpu.VMEM), pl.BlockSpec(memory_space=pl.ANY)
    return pl.pallas_call(
        kernel,
        out_shape=[jax.ShapeDtypeStruct(shape, dtype) for shape, dtype in outs],
        in_specs=[pl.BlockSpec(memory_space=pltpu.SMEM)]
        + [vmem] * (direct - 1)
        + [anywhere] * (len(args) - direct),
        out_specs=[vmem] * direct_outs + [anywhere] * (len(outs) - direct_outs),
        scratch_shapes=scratch,
        compiler_params=pltpu.CompilerParams(vmem_limit_bytes=VMEM_LIMIT),
    )(*args)


def tap_scratch(width):
    return [((width, LANES), BF), ((3 * width, LANES), BF), ((LANES, width), F32), ((LANES, 3 * width), F32)]


def mixer_forward(layer, scalars, own, other, ch, st, weight, decay, fwd, inv):
    length, width = decay.shape
    features = own.shape[1]
    bins = fwd.shape[0]
    tall, short, wide = (length, width), (own.shape[0], width), (length, 3 * width)
    kept = [(wide, BF), (tall, BF), (tall, BF), (tall, BF), ((bins, width), BF), ((2, bins, width), BF)]
    scratch = [((features, 3 * width), BF), (tall, F32), (fwd.shape, BF), (inv.shape, BF)] + kept + tap_scratch(width)
    scratch += [
        ((length + 16, 3 * width), F32),
        ((length + 16, width), F32),
        (tall, BF),
        ((2,) + tall, BF),
        ((2, bins, width), BF),
    ]
    return local_call(
        functools.partial(mixer_forward_kernel, layer),
        (scalars, own, other, ch, st, weight, decay, fwd, inv),
        3,
        [(tall, BF), (short, BF), (short, BF)] + kept,
        3,
        [pltpu.VMEM(*x) for x in scratch] + [pltpu.SemaphoreType.DMA((8,)), pltpu.SemaphoreType.DMA((6,))],
    )


def mixer_backward(
    layer, scalars, mid_own, mid_other, dmg, ch, st, weight, own, other, gated, br, decay, fwd, inv, q, key, conv, fh, uh
):
    length, width = decay.shape
    bins = fwd.shape[0]
    rows, features = mid_own.shape
    held = (own, other, gated, br, decay, fwd, inv, q, key, conv, fh, uh)
    scratch = [((2, width, width), BF), ((features, 3 * width), BF)] + [(x.shape, x.dtype) for x in held] + tap_scratch(width)
    scratch += [
        ((length + 16, 3 * width), F32),
        ((length + 16, width), F32),
        ((length + 16, width), F32),
        ((2, length, width), BF),
        ((2, bins, 2 * width), BF),
        ((length, features), BF),
        ((length, 3 * width), BF),
        ((5, 8, 3 * width), F32),
        ((5, 8, width), F32),
        ((LANES, features), F32),
        ((LANES, 3 * width), F32),
    ]
    return local_call(
        functools.partial(mixer_backward_kernel, layer),
        (scalars, mid_own, mid_other, dmg, ch, st, weight) + held,
        4,
        [
            ((2, features, 4 * width), BF),
            ((rows, features), BF),
            ((rows, features), BF),
            ((features, LANES), BF),
            ((3 * features, LANES), BF),
        ],
        5,
        [pltpu.VMEM(*x) for x in scratch] + [pltpu.SemaphoreType.DMA((19,))],
    )


def cube(dp_count):
    bits = (dp_count // 2).bit_length() - 1
    core, seq = bits, bits + 1
    low, rest = [bits - 1], list(range(bits - 1))
    orders = (
        rest + [seq] + low, rest + low + [seq], low + [seq] + rest,
        low + rest + [seq], [seq] + rest + low, [seq] + low + rest,
    )
    return bits, core, seq, orders


def place(bits):
    dp, seq = lax.axis_index("dp"), lax.axis_index("seq")
    coords = [(dp // (2 << (bits - 1 - d))) % 2 for d in range(bits)] + [dp % 2, seq]

    def neighbour(d):
        if d == bits + 1:
            return dp, 1 - seq
        step = 1 if d == bits else 2 << (bits - 1 - d)
        return dp + step * (1 - 2 * coords[d]), seq

    return coords, neighbour


def region(fixed, dims):
    return tuple(fixed[d] if d in fixed else slice(None) for d in range(dims))


def across(coords, bits):
    dp = lax.axis_index("dp")
    core, seq = coords[bits], coords[bits + 1]
    return core != seq, (dp + 1 - 2 * core, 1 - seq)


def greet(neighbours):
    barrier = pltpu.get_barrier_semaphore()
    for device in neighbours:
        pl.semaphore_signal(barrier, inc=1, device_id=device, device_id_type=pl.DeviceIdType.MESH)
    pl.semaphore_wait(barrier, len(neighbours))


class Swap:
    def __init__(self, src, dst, send, recv, local, moves, partner):
        self.stays, self.moves = jnp.logical_not(moves), moves
        self.away = pltpu.make_async_remote_copy(
            src_ref=src, dst_ref=dst, send_sem=send, recv_sem=recv,
            device_id=partner, device_id_type=pl.DeviceIdType.MESH,
        )
        self.here = pltpu.make_async_copy(src, dst, local)

    def start(self):
        pl.when(self.moves)(lambda: self.away.start())
        pl.when(self.stays)(lambda: self.here.start())

    def wait(self):
        pl.when(self.moves)(lambda: self.away.wait())
        pl.when(self.stays)(lambda: self.here.wait())


def remote(src, dst, send, recv, device):
    copy = pltpu.make_async_remote_copy(
        src_ref=src, dst_ref=dst, send_sem=send, recv_sem=recv,
        device_id=device, device_id_type=pl.DeviceIdType.MESH,
    )
    copy.start()
    return copy


GATHER_UNITS = (
    (3, 0, 640, 0, 0), (3, 640, 512, 1, 0), (3, 1152, 384, 2, 0), (5, 0, 128, 2, 0), (6, 0, 128, 1, 0),
    (0, 0, 768, 0, 1), (0, 768, 768, 1, 1), (2, 2, 2, 2, 1),
    (0, 1536, 768, 0, 2), (0, 2304, 768, 1, 2),
    (1, 0, 2, 0, 3), (1, 2, 2, 1, 3), (4, 1280, 256, 2, 3),
    (4, 0, 640, 0, 4), (4, 640, 640, 1, 4),
    (2, 0, 1, 0, 5), (2, 1, 1, 1, 5),
)
SCATTER_UNITS = (
    (0, 0, 768, 0, 0), (0, 768, 768, 1, 0), (2, 2, 2, 2, 0),
    (0, 1536, 768, 0, 1), (0, 2304, 768, 1, 1), (3, 1280, 256, 2, 1),
    (1, 0, 2, 0, 2), (1, 2, 2, 1, 2), (4, 1280, 256, 2, 2),
    (3, 0, 640, 0, 3), (3, 640, 640, 1, 3), (5, 0, 128, 2, 3), (6, 0, 128, 2, 3),
    (4, 0, 640, 0, 4), (4, 640, 640, 1, 4), (7, 0, 128, 2, 4),
    (2, 0, 1, 0, 5), (2, 1, 1, 0, 5),
)


def piece_of(unit, slabs):
    span = pl.ds(unit[1], unit[2])
    return (span, slice(None), slice(None)) if slabs else (slice(None), span)


def ticks(units, stages, shrinking):
    steps = [max(2**t, 2 ** (stages - 2)) for t in range(stages)]
    if shrinking:
        steps = steps[::-1]
    spacing = 2**stages // 4
    due = []
    for i, unit in enumerate(units):
        if shrinking:
            due.append((spacing * (unit[4] - 1) - 1, i, -1))
        due += [(spacing * unit[4] + sum(steps[:t]), i, t) for t in range(stages + 1)]
    return [(i, t) for _, i, t in sorted(due)]


def gather_kernel(dp_count, units, rows_in, rows_out, own, full, sems):
    bits, core_dim, _, orders = cube(dp_count)
    dims = bits + 2
    stages = dims - 1
    coords, neighbour = place(bits)
    core = coords[core_dim]
    sibling = neighbour(core_dim)
    moves, partner = across(coords, bits)
    greet([neighbour(d) for d in range(dims)] + [partner])
    ici_send, ici_recv, core_send, core_recv, local, swap_send, swap_recv, swap_local = sems
    swaps = [
        Swap(src, dst, swap_send.at[i], swap_recv.at[i], swap_local.at[i], moves, partner)
        for i, (src, dst) in enumerate(zip(rows_in, rows_out))
    ]
    mine = region(dict(enumerate(coords)), dims)
    firsts, forwards, sends = [], [], []
    last = [None] * len(units)
    for u, unit in enumerate(units):
        array, tail = unit[0], piece_of(unit, len(own[unit[0]].shape) == 4)
        piece = own[array].at[(slice(None),) + tail]
        here = full[array].at[(slice(None),) + mine + tail]
        keep = pltpu.make_async_copy(piece, here, local.at[u])
        keep.start()
        firsts.append((keep, remote(piece, here, core_send.at[u, 0], core_recv.at[u, 0], sibling)))
    for number, (u, t) in enumerate(ticks(units, stages, False)):
        if number == 4:
            for swap in swaps:
                swap.start()
        unit = units[u]
        array, tail, order = unit[0], piece_of(unit, len(own[unit[0]].shape) == 4), orders[unit[3]]
        fixed = {e: coords[e] for e in order[t:]}
        if t == 0:
            firsts[u][0].wait()
            firsts[u][1].wait_recv()
        else:
            last[u].wait_recv()
            got = full[array].at[(core,) + region(fixed | {order[t - 1]: 1 - coords[order[t - 1]]}, dims) + tail]
        if t < stages:
            held = full[array].at[(core,) + region(fixed, dims) + tail]
            last[u] = remote(held, held, ici_send.at[u, t], ici_recv.at[u, t], neighbour(order[t]))
            sends.append(last[u])
        if t > 0:
            forwards.append(remote(got, got, core_send.at[u, t], core_recv.at[u, t], sibling))
    for swap in swaps:
        swap.wait()
    beside = remote(rows_out[0], rows_out[-1], swap_send.at[len(swaps)], swap_recv.at[len(swaps)], sibling)
    for keep, copy in firsts:
        copy.wait_send()
    for copy in forwards:
        copy.wait()
    for copy in sends:
        copy.wait_send()
    beside.wait()


def gather_weights(rows, own, dp_count, number):
    bits = cube(dp_count)[0]
    stages = bits + 1
    units = GATHER_UNITS
    arrays = len(own)
    count = len(units)

    def body(*refs):
        rows_in, refs = refs[: len(rows)], refs[len(rows) :]
        own_refs, refs = refs[:arrays], refs[arrays:]
        rows_out, refs = refs[: len(rows) + 1], refs[len(rows) + 1 :]
        gather_kernel(dp_count, units, rows_in, rows_out, own_refs, refs[:arrays], refs[arrays:])

    grid = (2,) * (bits + 2)
    anywhere = pl.BlockSpec(memory_space=pl.ANY)
    return pl.pallas_call(
        body,
        out_shape=[jax.ShapeDtypeStruct(x.shape, x.dtype) for x in (*rows, rows[0])]
        + [jax.ShapeDtypeStruct(x.shape[:1] + grid + x.shape[1:], x.dtype) for x in own],
        in_specs=[anywhere] * (len(rows) + arrays),
        out_specs=[anywhere] * (len(rows) + 1 + arrays),
        scratch_shapes=[pltpu.SemaphoreType.DMA((count, stages))] * 2
        + [pltpu.SemaphoreType.DMA((count, stages + 1))] * 2
        + [pltpu.SemaphoreType.DMA((count,))]
        + [pltpu.SemaphoreType.DMA((len(rows) + 1,))] * 3,
        compiler_params=pltpu.CompilerParams(collective_id=number, has_side_effects=True),
    )(*rows, *own)


def scatter_kernel(dp_count, units, ends_in, token_ref, grads, outs, held, first, arrived, final, work, sems):
    bits, core_dim, _, orders = cube(dp_count)
    dims = bits + 2
    stages = dims - 1
    coords, neighbour = place(bits)
    core = coords[core_dim]
    sibling = neighbour(core_dim)
    moves, partner = across(coords, bits)
    greet([neighbour(d) for d in range(dims)] + [partner])
    ici_send, ici_recv, core_send, core_recv, local, end_send, end_recv, end_local = sems
    x_ref, dn_ref, away_ref, dmid_ref, gain_ref, dng_ref = ends_in
    other_ref, grad_ref, sum_ref, flat_ref, tall_ref, slab_ref = work
    grads = list(grads) + [slab_ref]
    exchange = remote(away_ref, other_ref, end_send.at[0], end_recv.at[0], sibling)
    begin = pltpu.make_async_copy(dmid_ref, grad_ref, end_local.at[1])
    begin.start()
    swap = Swap(other_ref, token_ref, end_send.at[1], end_recv.at[1], end_local.at[0], moves, partner)

    def finish_rows():
        exchange.wait()
        begin.wait()
        sum_ref[...] = jnp.zeros(sum_ref.shape, F32)
        share = slab_ref.shape[-2]

        @pl.loop(0, x_ref.shape[0] // 128)
        def _(i):
            rows = pl.ds(pl.multiple_of(i * 128, 128), 128)
            d = dn_ref[rows, :].astype(F32) + other_ref[rows, :].astype(F32)
            dx, dg = norm_back(x_ref[rows, :].astype(F32), gain_ref[...], d)
            other_ref[rows, :] = (grad_ref[rows, :] + dx).astype(BF)
            sum_ref[0:1, :] += dg

        swap.start()
        flat_ref[...] = jnp.zeros(flat_ref.shape, F32)
        for layer, row in enumerate((sum_ref, dng_ref)):
            for c in range(tall_ref.shape[0] // LANES):
                cols = slice(c * LANES, (c + 1) * LANES)
                flat_ref[0:1, :] = row[0:1, cols]
                tall_ref[cols, :] = flat_ref[...].T
            for i in range(2**dims):
                at = tuple((i >> (dims - 1 - d)) % 2 for d in range(dims))
                slab_ref[(layer,) + at] = tall_ref[i * share : (i + 1) * share, :].astype(BF)

    everything = region({}, dims)

    def add(u, fixed, extra):
        free = [d for d in range(dims) if d not in fixed]

        @pl.loop(0, 2 ** len(free))
        def _(i):
            at = {d: (i // 2 ** (len(free) - 1 - j)) % 2 for j, d in enumerate(free)}
            index = tuple(at[d] if d in at else fixed[d] for d in range(dims))
            held[u][index] += extra[tuple(at[d] for d in free)]

    starts, sends = [None] * len(units), []
    last = [None] * len(units)
    for u, t in ticks(units, stages, True):
        if t < 0 and units[u][0] == len(grads) - 1:
            finish_rows()
        if t < 0:
            array, tail = units[u][0], piece_of(units[u], len(outs[units[u][0]].shape) == 4)
            load = pltpu.make_async_copy(grads[array].at[(core,) + everything + tail], held[u], local.at[u, 0])
            load.start()
            other = grads[array].at[(1 - core,) + everything + tail]
            starts[u] = (load, remote(other, first[u], core_send.at[u, 0], core_recv.at[u, 0], sibling))
            continue
        order = orders[units[u][3]][::-1]
        fixed = {d: coords[d] for d in order[:t]}
        if t == 0:
            starts[u][0].wait()
            starts[u][1].wait_recv()
            add(u, fixed, first[u])
        else:
            last[u].wait_recv()
            add(u, fixed, arrived[u][t - 1])
        if t < stages:
            away = held[u].at[region(fixed | {order[t]: 1 - coords[order[t]]}, dims)]
            last[u] = remote(away, arrived[u][t], ici_send.at[u, t], ici_recv.at[u, t], neighbour(order[t]))
            sends.append(last[u])
        else:
            away = held[u].at[region(fixed | {core_dim: 1 - core}, dims)]
            last[u] = remote(away, final[u], core_send.at[u, 1], core_recv.at[u, 1], sibling)
    ends = []
    mine = region(dict(enumerate(coords)), dims)
    for u, unit in enumerate(units):
        array, tail = unit[0], piece_of(unit, len(outs[unit[0]].shape) == 4)
        own = pltpu.make_async_copy(held[u].at[mine], outs[array].at[(core,) + tail], local.at[u, 1])
        own.start()
        last[u].wait_recv()
        other = pltpu.make_async_copy(final[u], outs[array].at[(1 - core,) + tail], local.at[u, 2])
        other.start()
        ends += [own, other]
    swap.wait()
    for copy in ends:
        copy.wait()
    for copy in sends + last + [s[1] for s in starts]:
        copy.wait_send()


def scatter_grads(ends, grads, units, dp_count, number):
    bits = cube(dp_count)[0]
    dims = bits + 2
    stages = dims - 1
    count = len(units)
    grid = (2,) * dims
    rows, features = ends[0].shape
    share = grads[0].shape[1 + dims]
    tails = [x.shape[1 + dims :] for x in grads] + [(share, LANES)]
    arrays = len(tails)
    slabs = []
    for array, _, size, _, _ in units:
        shape = tails[array]
        slabs.append((size,) + shape[1:] if len(shape) == 3 else shape[:-1] + (size,))
    work = [((rows, features), BF), ((rows, features), F32), ((8, features), F32), ((LANES, LANES), F32)]
    work += [((features, LANES), F32), ((2,) + grid + (share, LANES), BF)]

    def body(*refs):
        ends_in, refs = refs[: len(ends)], refs[len(ends) :]
        grads_in, refs = refs[: len(grads)], refs[len(grads) :]
        token, outs, refs = refs[0], refs[1 : 1 + arrays], refs[1 + arrays :]
        held, first, final = refs[:count], refs[count : 2 * count], refs[2 * count : 3 * count]
        refs = refs[3 * count :]
        arrived = [refs[u * stages : (u + 1) * stages] for u in range(count)]
        refs = refs[count * stages :]
        scatter_kernel(
            dp_count, units, ends_in, token, grads_in, outs, held, first, arrived, final,
            refs[: len(work)], refs[len(work) :],
        )

    anywhere, vmem = pl.BlockSpec(memory_space=pl.ANY), pl.BlockSpec(memory_space=pltpu.VMEM)
    return pl.pallas_call(
        body,
        out_shape=[jax.ShapeDtypeStruct((rows, features), BF)]
        + [jax.ShapeDtypeStruct((2,) + tail, BF) for tail in tails],
        in_specs=[vmem, vmem, anywhere, anywhere, vmem, vmem] + [anywhere] * len(grads),
        out_specs=[anywhere] * (1 + arrays),
        scratch_shapes=[pltpu.VMEM(grid + slab, BF) for slab in slabs] * 2
        + [pltpu.VMEM(slab, BF) for slab in slabs]
        + [pltpu.VMEM((2,) * (dims - 1 - t) + slab, BF) for slab in slabs for t in range(stages)]
        + [pltpu.VMEM(*x) for x in work]
        + [pltpu.SemaphoreType.DMA((count, stages))] * 2
        + [pltpu.SemaphoreType.DMA((count, 2))] * 2
        + [pltpu.SemaphoreType.DMA((count, 3))]
        + [pltpu.SemaphoreType.DMA((2,))] * 2
        + [pltpu.SemaphoreType.DMA((2,))],
        compiler_params=pltpu.CompilerParams(
            collective_id=number, has_side_effects=True, vmem_limit_bytes=VMEM_LIMIT
        ),
    )(*ends, *grads)


def norm_parts(x):
    center = x - jnp.mean(x, axis=-1, keepdims=True)
    r = lax.rsqrt(jnp.mean(center * center, axis=-1, keepdims=True) + EPS)
    return center * r, r


def norm_back(x, gain, d):
    xhat, r = norm_parts(x)
    h = d * gain
    dx = r * (h - jnp.mean(h, axis=-1, keepdims=True) - xhat * jnp.mean(h * xhat, axis=-1, keepdims=True))
    return dx, jnp.sum(d * xhat, axis=0, keepdims=True)


SLOPE = math.sqrt(2.0 / math.pi)
CUBE = 0.044715


def gelu_parts(x):
    square = x * x
    t = jnp.tanh(SLOPE * (x + CUBE * square * x))
    flat = 0.5 + 0.5 * t
    return x * flat, flat + 0.5 * x * (1.0 - t * t) * (SLOPE + 3.0 * SLOPE * CUBE * square)


def mlp_forward_kernel(
    gain, next_gain, scalar_ref, x_ref, g0_ref, g1_ref, o0_ref, o1_ref, gains_ref, wg_ref, wu_ref, d0_ref, d1_ref,
    mid_ref, hm_ref, pre_ref, out_ref, next_ref,
):
    j = pl.program_id(0)

    @pl.when(j == 0)
    def _():
        width = g0_ref.shape[1]
        mid = x_ref[...]
        for ref, side in ((g0_ref, scalar_ref[1]), (g1_ref, 1 - scalar_ref[1])):
            rows = pl.ds(pl.multiple_of(side * width, STRIP), width)
            mid += dot(ref[...], jnp.concatenate([o0_ref[rows, :], o1_ref[rows, :]], axis=1))
        mid_ref[...] = mid
        out_ref[...] = mid
        hm_ref[...] = (norm_parts(mid)[0] * gains_ref[gain : gain + 1, :]).astype(BF)

    hm = hm_ref[...]
    total = out_ref[...]
    for i in range(TILE // PART_F):
        part = slice(i * PART_F, (i + 1) * PART_F)
        gate = dot(hm, wg_ref[:, part])
        up = dot(hm, wu_ref[:, part])
        pre_ref[0, :, part] = gate.astype(BF)
        pre_ref[1, :, part] = up.astype(BF)
        hid = (gelu_parts(gate)[0] * up).astype(BF)
        total += dot(hid, jnp.concatenate([d0_ref[part, :], d1_ref[part, :]], axis=1))
    out_ref[...] = total

    @pl.when(j == pl.num_programs(0) - 1)
    def _():
        next_ref[...] = (norm_parts(out_ref[...])[0] * gains_ref[next_gain : next_gain + 1, :]).astype(BF)


def mlp_backward_kernel(
    gain, g_ref, hm_ref, mid_ref, gains_ref, pre_ref, wg_ref, wu_ref, d0_ref, d1_ref,
    dgu_ref, ddn_ref, dmid_ref, mlow_ref, dmg_ref,
    glow, hm_t, acc,
):
    j = pl.program_id(0)
    width = d0_ref.shape[1]

    @pl.when(j == 0)
    def _():
        glow[...] = g_ref[...].astype(BF)
        hm_t[...] = hm_ref[...].T
        acc[...] = jnp.zeros(acc.shape, F32)

    low, hm = glow[...], hm_t[...]
    total = acc[...]
    for i in range(TILE // PART_B):
        part = slice(i * PART_B, (i + 1) * PART_B)
        dh = dot(low, jnp.concatenate([d0_ref[part, :], d1_ref[part, :]], axis=1), ((1,), (1,)))
        value, slope = gelu_parts(pre_ref[0, :, part].astype(F32))
        up = pre_ref[1, :, part].astype(F32)
        hid = (value * up).astype(BF)
        d_gate = (dh * up * slope).astype(BF)
        d_up = (dh * value).astype(BF)
        d_down = dot(hid, low, ((0,), (0,))).astype(BF)
        ddn_ref[0, part, :] = d_down[:, :width]
        ddn_ref[1, part, :] = d_down[:, width:]
        for h, d in enumerate((d_gate, d_up)):
            grad = dot(hm, d).astype(BF)
            if len(dgu_ref.shape) == 3:
                dgu_ref[h, :, part] = grad
            else:
                dgu_ref[:, h * TILE + i * PART_B : h * TILE + (i + 1) * PART_B] = grad
        total += dot(d_gate, wg_ref[:, part], ((1,), (1,))) + dot(d_up, wu_ref[:, part], ((1,), (1,)))
    acc[...] = total

    @pl.when(j == pl.num_programs(0) - 1)
    def _():
        dx, dg = norm_back(mid_ref[...], gains_ref[gain : gain + 1, :], acc[...])
        dmid = g_ref[...] + dx
        dmid_ref[...] = dmid
        mlow_ref[...] = dmid.astype(BF)
        dmg_ref[...] = dg


TILE = 512
PART_F = 512
PART_B = 512


def whole(shape):
    return pl.BlockSpec(shape, lambda j: (0,) * len(shape))


def weight_specs(layout, hidden, features):
    steps = hidden // TILE
    gate_up = pl.BlockSpec((features, TILE), lambda j: (0, j))
    up = pl.BlockSpec((features, TILE), lambda j: (1, j) if layout == "halves" else (0, steps + j))
    down = [
        pl.BlockSpec((TILE, features // 2), lambda j: (j, 0)),
        pl.BlockSpec((TILE, features // 2), lambda j: (steps + j, 0)),
    ]
    return [gate_up, up] + down


def mlp_forward(scalars, x, g0, g1, weight, gains, gain, next_gain, weights):
    layout, gu, dn = weights
    rows, features = x.shape
    hidden = dn.shape[0] // 2
    square = whole((rows, features))
    narrow = [whole(a.shape) for a in (g0, g1)]
    narrow += [pl.BlockSpec((features, features // 2), lambda j, h=h: (h, 3)) for h in range(2)]
    shapes = [((rows, features), F32), ((rows, features), BF), ((2, rows, hidden), BF), ((rows, features), F32), ((rows, features), BF)]
    return pl.pallas_call(
        functools.partial(mlp_forward_kernel, gain, next_gain),
        grid=(hidden // TILE,),
        out_shape=[jax.ShapeDtypeStruct(*s) for s in shapes],
        in_specs=[pl.BlockSpec(memory_space=pltpu.SMEM), square] + narrow + [whole(gains.shape)] + weight_specs(layout, hidden, features),
        out_specs=[square, square, pl.BlockSpec((2, rows, TILE), lambda j: (0, 0, j)), square, square],
        compiler_params=pltpu.CompilerParams(vmem_limit_bytes=VMEM_LIMIT),
    )(scalars, x, g0, g1, weight, weight, gains, gu, gu, dn, dn)


def mlp_backward(g, hm, mid, gains, gain, pre, weights, side_by_side):
    layout, gu, dn = weights
    rows, features = g.shape
    hidden = pre.shape[2]
    width = features // 2
    square, vector = whole((rows, features)), whole((1, features))
    both = (features, 2 * hidden) if side_by_side else (2, features, hidden)
    shapes = [(both, BF), ((2, hidden, width), BF), ((rows, features), F32), ((rows, features), BF), ((1, features), F32)]
    return pl.pallas_call(
        functools.partial(mlp_backward_kernel, gain),
        grid=(hidden // TILE,),
        out_shape=[jax.ShapeDtypeStruct(*s) for s in shapes],
        in_specs=[square] * 3
        + [whole(gains.shape), pl.BlockSpec((2, rows, TILE), lambda j: (0, 0, j))]
        + weight_specs(layout, hidden, features),
        out_specs=[
            pl.BlockSpec((features, 2 * TILE), lambda j: (0, j))
            if side_by_side
            else pl.BlockSpec((2, features, TILE), lambda j: (0, 0, j)),
            pl.BlockSpec((2, TILE, width), lambda j: (0, j, 0)),
            square, square, vector,
        ],
        scratch_shapes=[pltpu.VMEM((rows, features), BF), pltpu.VMEM((features, rows), BF), pltpu.VMEM((rows, features), F32)],
        compiler_params=pltpu.CompilerParams(vmem_limit_bytes=VMEM_LIMIT),
    )(g, hm, mid, gains, pre, gu, gu, dn, dn)


def shards(
    tokens, split_points, cotangent, norm_gain, in_weight, short_taps, cond_taps,
    out_weight, mlp_gain, gate_up, down_weight,
):
    rows, features = tokens.shape[1:]
    dp_count, seq_count = lax.axis_size("dp"), lax.axis_size("seq")
    devices = dp_count * seq_count
    length = rows * seq_count
    width = features // 2
    layers = in_weight.shape[0]
    share = norm_gain.shape[1]
    hidden = down_weight.shape[1] * devices
    core = lax.axis_index("dp") % 2
    seq = lax.axis_index("seq")

    swap = [(4 * k + a, 4 * k + 3 - a) for k in range(devices // 4) for a in (1, 2)]
    flip = [(i, i ^ 1) for i in range(dp_count)]

    def swap_rows(x):
        return jnp.where(core == seq, x, lax.ppermute(x, AXES, swap))

    def sibling(x):
        return lax.ppermute(x, "dp", flip)

    def beside(own, other, axis):
        return jnp.where(
            core == 0,
            jnp.concatenate([own, other], axis=axis),
            jnp.concatenate([other, own], axis=axis),
        )

    def half_of(x, which, axis):
        size = x.shape[axis] // 2
        return lax.dynamic_slice_in_dim(x, which * size, size, axis)

    def own_channels(x):
        parts = x.shape[-1] // features
        x = x.reshape(x.shape[:-1] + (parts, 2, width))
        x = lax.dynamic_index_in_dim(x, core, x.ndim - 2, keepdims=False)
        return x.reshape(x.shape[:-2] + (parts * width,))

    table = transform_matrix(length)
    fwd = jnp.asarray(table, BF)
    inv = jnp.asarray(np.ascontiguousarray(table.T), BF)
    decay = own_channels(decay_table(length, features))

    def halves(x):
        parts = x.shape[-1] // features
        x = x.reshape(x.shape[:-1] + (parts, 2, width))
        x = jnp.moveaxis(x, -2, 0)
        return x.reshape(x.shape[:-2] + (parts * width,))

    grid = (2,) * (cube(dp_count)[0] + 2)

    ch = jnp.concatenate([norm_gain[:, :, None], mlp_gain[:, :, None], cond_taps.transpose(0, 2, 1)], axis=2)
    ch = jnp.pad(ch, ((0, 0), (0, 0), (0, LANES - 7)))
    st = jnp.pad(short_taps.transpose(0, 2, 1), ((0, 0), (0, 0), (0, LANES - 5)))
    own = [gate_up[0].reshape(share, 2, hidden).transpose(1, 0, 2)]
    own += [halves(down_weight[layer]).reshape(2, hidden // features, share, width) for layer in range(layers)]
    for layer in range(layers):
        own.append(jnp.concatenate([halves(in_weight[layer]), halves(out_weight[layer])], axis=2))
    place_rows = [tokens[0], jnp.broadcast_to(split_points, (8, LANES))]
    x_low, split, x_far, *full = gather_weights(place_rows, own + [ch, st], dp_count, 0)
    downs = [x.reshape(2 * hidden, width) for x in full[1 : 1 + layers]]
    mixer_w = [x.reshape(2, features, 4 * width) for x in full[1 + layers : 1 + 2 * layers]]
    ch, st = full[-2].reshape(layers, features, LANES), full[-1].reshape(layers, 3 * features, LANES)
    late, _ = lax.optimization_barrier((gate_up[1:], full[0]))
    gate_ups = [("halves", full[0].reshape(2 * features, hidden))]
    gate_ups += [("plain", lax.all_gather(x, AXES, axis=0, tiled=True)) for x in late]
    gains = ch[:, :, :2].astype(F32).transpose(0, 2, 1).reshape(2 * layers, features)
    scalars = jnp.stack([split[0, 0], core.astype(jnp.int32)])
    stream, far = x_low.astype(F32), x_far.astype(F32)
    grad = swap_rows(cotangent)[0].astype(F32)
    normed, normed_far = [(norm_parts(x)[0] * gains[0]).astype(BF) for x in (stream, far)]
    kept = []
    for layer in range(layers):
        if layer > 0:
            normed_far = sibling(normed)
        gated, mine, away, branches, q, key, conv, fh, uh = mixer_forward(
            layer, scalars, normed, normed_far, ch, st, mixer_w[layer], decay, fwd, inv
        )
        middle, normed_mlp, pre, out, normed_next = mlp_forward(
            scalars, stream, mine, sibling(away), mixer_w[layer].reshape(2 * features, -1), gains,
            2 * layer + 1, (2 * layer + 2) % (2 * layers), gate_ups[layer] + (downs[layer],),
        )
        kept.append((stream, normed, normed_far, gated, branches, q, key, conv, fh, uh, middle, normed_mlp, pre))
        stream, normed = out, normed_next
    activations = swap_rows(stream.astype(BF)[None])

    summed = []
    early = [None] * layers
    for layer in reversed(range(layers)):
        x, normed, normed_far, gated, branches, q, key, conv, fh, uh, middle, normed_mlp, pre = kept[layer]
        d_gu, d_down, d_middle, m_low, d_mg = mlp_backward(
            grad, normed_mlp, middle, gains, 2 * layer + 1, pre, gate_ups[layer] + (downs[layer],), layer > 0
        )
        rest, d_normed, d_away, d_ch, d_st = mixer_backward(
            layer, scalars, m_low, sibling(m_low), d_mg, ch, st, mixer_w[layer], normed, normed_far, gated, branches,
            decay, fwd, inv, q, key, conv, fh, uh,
        )
        if layer > 0:
            early[layer] = lax.psum_scatter(d_gu, AXES, scatter_dimension=0, tiled=True)
            d_part, d_ng = norm_back(x, gains[2 * layer], d_normed.astype(F32) + sibling(d_away).astype(F32))
            grad = d_middle + d_part
        summed.append((d_gu, d_down, rest, d_ch, d_st))
    d_gus, d_downs, rests, *smalls = zip(*summed[::-1])
    pieces = [d_gus[0].reshape((2,) + grid + (share, hidden))]
    pieces += [x.reshape((2,) + grid + (hidden // features, share, width)) for x in d_downs]
    pieces += [x.reshape((2,) + grid + (share, 4 * width)) for x in rests]
    pieces += [jnp.stack(x).reshape((2,) + grid + (-1, LANES)) for x in smalls]
    ends = [x_low, d_normed, d_away, d_middle, gains[:1], d_ng]
    fits = share % 8 == 0
    units = tuple(unit for unit in SCATTER_UNITS if fits or unit[0] != 2)
    token_grad, *outs = scatter_grads(ends, pieces, units, dp_count, 1)
    if not fits:
        outs[2] = lax.psum_scatter(d_downs[1], AXES, scatter_dimension=1, tiled=True)
    token_grad = token_grad[None].astype(F32)

    def joined(x):
        parts = x.shape[-1] // width
        x = jnp.moveaxis(x.reshape(x.shape[:-1] + (parts, width)), 0, -2)
        return x.reshape(x.shape[:-3] + (parts * features,))

    early[0] = outs[0].transpose(1, 0, 2)
    for layer in range(1, layers):
        early[layer] = early[layer].reshape(share, hidden // TILE, 2, TILE).transpose(0, 2, 1, 3)
    g_gu = jnp.stack([x.reshape(share, 2 * hidden) for x in early]).astype(F32)
    g_down = jnp.stack([joined(x.reshape(2, -1, width)) for x in outs[1 : 1 + layers]]).astype(F32)
    rest = outs[1 + layers : 1 + 2 * layers]
    g_in = jnp.stack([joined(x[:, :, : 3 * width]) for x in rest]).astype(F32)
    g_out = jnp.stack([joined(x[:, :, 3 * width :]) for x in rest]).astype(F32)
    s_ch, s_st, s_ng = [x.astype(F32) for x in outs[1 + 2 * layers :]]
    g_ng, g_mg, g_ct, g_st = s_ng[:, :, 0], s_ch[:, :, 1], s_ch[:, :, 2:7].transpose(0, 2, 1), s_st[:, :, :5].transpose(0, 2, 1)
    return (
        activations,
        token_grad,
        g_ng,
        g_in,
        g_st,
        g_ct,
        g_out,
        g_mg,
        g_gu,
        g_down,
    )


def solution(mesh):
    every = ("dp", "seq")
    rows, part = P("dp", "seq", None), P(None, every, None)
    vector, taps = P(None, every), P(None, None, every)
    return jax.shard_map(
        shards,
        mesh=mesh,
        in_specs=(rows, P("dp"), rows, vector, part, taps, taps, part, vector, part, part),
        out_specs=(rows, rows, vector, part, taps, taps, part, vector, part, part),
        check_vma=False,
    )
```

```python
import functools
import math

import numpy as np
import jax
import jax.numpy as jnp
from jax import lax
from jax.experimental import pallas as pl
from jax.experimental.pallas import tpu as pltpu
from jax.sharding import PartitionSpec as P

BF = jnp.bfloat16
F32 = jnp.float32
EPS = 1e-05
AXES = ("dp", "seq")
GAP = 128
VMEM_LIMIT = 60 * 2**20
STRIP = 128
LANES = 128
BINS = 224
ROWS = 256
CHUNK = 128


def transform_matrix(length):
    half = length - GAP
    freq = np.arange(half)[:, None]
    place = np.arange(length)[None, :]
    angle = ((2 * freq + 1) * place % (4 * half)).astype(np.float64) * (math.pi / (2 * half))
    both = np.stack([np.cos(angle), -np.sin(angle)])
    both = both.reshape(2, half // BINS, BINS, length).transpose(1, 0, 2, 3)
    return both.reshape(2 * half, length).astype(np.float32)


def decay_table(length, features):
    positions = np.arange(length)
    rates = np.exp(math.log(1.0 / length) + np.arange(features) / (features - 1) * math.log(4.0))
    scales = np.sum(np.exp(-2.0 * positions[:, None] * rates[None, :]), axis=0) ** -0.5
    table = np.exp(-positions[:, None] * rates[None, :]) * scales[None, :]
    return np.stack(np.split(table, 2, axis=1)).astype(np.float32)


def dot(a, b, dims=((1,), (0,))):
    return lax.dot_general(a, b, (dims, ((), ())), preferred_element_type=F32)


def tap_same(row0, split):
    t = row0 + lax.broadcasted_iota(jnp.int32, (CHUNK, STRIP), 0)
    here = t >= split
    return [
        None if off == 2 else jnp.where(((t + (off - 2)) >= split) == here, 1.0, 0.0)
        for off in range(5)
    ]


def shifted(ref, row0, cols, same):
    block = ref[pl.ds(row0, CHUNK + 16), cols]
    out = []
    for off in range(5):
        turned = pltpu.roll(block, (2 - off) % (CHUNK + 16), 0) if off != 2 else block
        rows = turned[8 : 8 + CHUNK]
        out.append(rows if same[off] is None else rows * same[off])
    return out


def over_chunks(length, split, body):
    @pl.loop(0, length // CHUNK)
    def _(i):
        row0 = pl.multiple_of(i * CHUNK, CHUNK)
        touched = (split > row0 - 2) & (split < row0 + CHUNK + 2)

        @pl.when(touched)
        def _():
            body(row0, tap_same(row0, split))

        @pl.when(jnp.logical_not(touched))
        def _():
            body(row0, [None] * 5)


def tap_loads(layer, core, ch_hbm, st_hbm, ct_ref, st_ref):
    width = ct_ref.shape[0]
    own = pl.multiple_of(core * width, STRIP)
    pairs = [(ch_hbm.at[layer, pl.ds(own, width), :], ct_ref)]
    for part in range(3):
        rows = pl.ds(pl.multiple_of(part * 2 * width + own, STRIP), width)
        pairs.append((st_hbm.at[layer, rows, :], st_ref.at[pl.ds(part * width, width), :]))
    return pairs


def weigh(rows, w_ref, base, cols, flip):
    total = None
    for off, x in enumerate(rows):
        tap = base + (4 - off if flip else off)
        term = x * w_ref[tap : tap + 1, cols]
        total = term if total is None else total + term
    return total


def by_corner(split, length, body):
    for corner in range(length // ROWS):
        spans = (slice(0, (corner + 1) * ROWS), slice(corner * ROWS, length))
        pl.when(split // ROWS == corner)(functools.partial(body, spans))


def clear_ends(ref, length):
    ref[0:8, :] = jnp.zeros((8, ref.shape[1]), F32)
    ref[8 + length : 16 + length, :] = jnp.zeros((8, ref.shape[1]), F32)


def fetch(pairs, sems):
    copies = [pltpu.make_async_copy(src, dst, sems.at[i]) for i, (src, dst) in enumerate(pairs)]
    for copy in copies:
        copy.start()
    return copies


def mixer_forward_kernel(
    layer, split_ref, own_ref, other_ref, ch_hbm, st_hbm, iw_hbm, decay_hbm, fwd_hbm, inv_hbm,
    gated_ref, mine_ref, send_ref, br_hbm, q_hbm, key_hbm, conv_hbm, fh_hbm, uh_hbm,
    iw_ref, decay_ref, fwd_ref, inv_ref, br_ref, q_ref, key_ref, conv_ref, fh_ref, uh_ref,
    ct_ref, st_ref, cw_ref, sw_ref, pad, kpad, filt, u, prod, in_sems, out_sems,
):
    length, width = q_ref.shape
    rows_own = own_ref.shape[0]
    half = length - GAP
    split, core = split_ref[0, 0], lax.axis_index("dp") % 2
    strips = width // STRIP
    loads = fetch(
        [
            (iw_hbm.at[core, :, pl.ds(0, 3 * width)], iw_ref),
            (decay_hbm.at[core], decay_ref),
            (fwd_hbm, fwd_ref),
            (inv_hbm, inv_ref),
        ]
        + tap_loads(layer, core, ch_hbm, st_hbm, ct_ref, st_ref),
        in_sems,
    )
    outs = [(br_ref, br_hbm), (q_ref, q_hbm), (key_ref, key_hbm), (fh_ref, fh_hbm), (uh_ref, uh_hbm), (conv_ref, conv_hbm)]
    stores = [pltpu.make_async_copy(src, dst, out_sems.at[i]) for i, (src, dst) in enumerate(outs)]
    clear_ends(pad, length)
    clear_ends(kpad, length)
    loads[0].wait()
    for ref, side in ((own_ref, core), (other_ref, 1 - core)):

        @pl.loop(0, rows_own // ROWS)
        def _(i):
            row0 = pl.multiple_of(side * rows_own + i * ROWS, ROWS)
            low = dot(ref[pl.ds(pl.multiple_of(i * ROWS, ROWS), ROWS), :], iw_ref[...]).astype(BF)
            br_ref[pl.ds(row0, ROWS), :] = low
            pad[pl.ds(row0 + 8, ROWS), :] = low.astype(F32)

    stores[0].start()
    for copy in loads[4:]:
        copy.wait()
    cw_ref[...] = ct_ref[...].astype(F32).T
    sw_ref[...] = st_ref[...].astype(F32).T

    def mix(row0, same):
        rows = pl.ds(row0, CHUNK)
        first = row0 + lax.broadcasted_iota(jnp.int32, (CHUNK, STRIP), 0) < split
        for part in range(3):
            for strip in range(strips):
                cols = pl.ds(part * width + strip * STRIP, STRIP)
                own = pl.ds(strip * STRIP, STRIP)
                low = weigh(shifted(pad, row0, cols, same), sw_ref, 0, cols, False).astype(BF)
                if part == 0:
                    q_ref[rows, own] = low
                elif part == 1:
                    key_ref[rows, own] = low
                    kpad[pl.ds(row0 + 8, CHUNK), own] = low.astype(F32)
                else:
                    low = low.astype(F32)
                    u[0, rows, own] = jnp.where(first, low, 0.0).astype(BF)
                    u[1, rows, own] = jnp.where(first, 0.0, low).astype(BF)

    over_chunks(length, split, mix)
    stores[1].start()
    stores[2].start()
    loads[1].wait()

    def make_filter(row0, same):
        rows = pl.ds(row0, CHUNK)
        for strip in range(strips):
            cols = pl.ds(strip * STRIP, STRIP)
            total = weigh(shifted(kpad, row0, cols, same), cw_ref, 2, cols, False)
            filt[rows, cols] = (total * decay_ref[rows, cols]).astype(BF)

    over_chunks(length, split, make_filter)
    scale = 1.0 / half
    loads[2].wait()

    def transform(spans):
        @pl.loop(0, half // BINS)
        def _(i):
            rows = pl.ds(pl.multiple_of(i * 2 * BINS, 2 * BINS), 2 * BINS)
            f = dot(fwd_ref[rows, 0:half], filt[0:half, :])
            fr, fi = f[:BINS], f[BINS:]
            fh_ref[rows, :] = f.astype(BF)
            for m in range(2):
                s = dot(fwd_ref[rows, spans[m]], u[m, spans[m], :])
                uh_ref[m, rows, :] = s.astype(BF)
                sr, si = s[:BINS], s[BINS:]
                prod[m, rows, :] = jnp.concatenate(
                    [(fr * sr - fi * si) * scale, (fr * si + fi * sr) * scale], axis=0
                ).astype(BF)

    by_corner(split, length, transform)
    stores[3].start()
    stores[4].start()
    corner = split // ROWS
    loads[3].wait()

    @pl.loop(0, length // ROWS)
    def _(i):
        rows = pl.ds(pl.multiple_of(i * ROWS, ROWS), ROWS)
        pick = (i > corner).astype(jnp.int32)
        conv_ref[rows, :] = dot(inv_ref[rows, :], prod[pick]).astype(BF)

        @pl.when(i == corner)
        def _():
            later = i * ROWS + lax.broadcasted_iota(jnp.int32, (ROWS, width), 0) >= split
            other = dot(inv_ref[rows, :], prod[1])
            conv_ref[rows, :] = jnp.where(later, other, conv_ref[rows, :].astype(F32)).astype(BF)

        gated_ref[rows, :] = (q_ref[rows, :].astype(F32) * conv_ref[rows, :].astype(F32)).astype(BF)

    stores[5].start()
    mine_ref[...] = gated_ref[pl.ds(pl.multiple_of(core * rows_own, ROWS), rows_own), :]
    send_ref[...] = gated_ref[pl.ds(pl.multiple_of((1 - core) * rows_own, ROWS), rows_own), :]
    for copy in stores:
        copy.wait()


def mixer_backward_kernel(
    layer, split_ref, mid_own_ref, mid_other_ref, dmg_ref, ch_hbm, st_hbm,
    w_hbm, own_hbm, other_hbm, gated_hbm, br_hbm, decay_hbm, fwd_hbm, inv_hbm, q_hbm, key_hbm, conv_hbm, fh_hbm, uh_hbm,
    rest_ref, dn_ref, dn_send_ref, dch_ref, dst_ref,
    ow_ref, iw_ref, own_ref, other_ref, gated_ref, br_ref, decay_ref, fwd_ref, inv_ref, q_ref, key_ref, conv_ref, fh_ref,
    uh_ref, ct_ref, st_ref, cw_ref, sw_ref, pad, epad, kpad, g, prod, mid_ref, dbr_ref, dsw_sum, dcw_sum, ch_rows, st_rows,
    in_sems,
):
    length, width = q_ref.shape
    rows_own, features = own_ref.shape
    half = length - GAP
    split, core = split_ref[0, 0], lax.axis_index("dp") % 2
    strips = width // STRIP
    part = pl.ds(pl.multiple_of(core * width, STRIP), width)
    apart = pl.ds(pl.multiple_of((1 - core) * width, STRIP), width)
    near = pl.ds(pl.multiple_of(core * rows_own, ROWS), rows_own)
    far = pl.ds(pl.multiple_of((1 - core) * rows_own, ROWS), rows_own)
    out_cols = pl.ds(3 * width, width)
    loads = fetch(
        [
            (w_hbm.at[0, part, out_cols], ow_ref.at[0]),
            (w_hbm.at[1, part, out_cols], ow_ref.at[1]),
            (conv_hbm, conv_ref),
            (q_hbm, q_ref),
            (fwd_hbm, fwd_ref),
            (fh_hbm, fh_ref),
            (uh_hbm, uh_ref),
            (inv_hbm, inv_ref),
            (decay_hbm.at[core], decay_ref),
            (key_hbm, key_ref),
            (br_hbm, br_ref),
            (gated_hbm, gated_ref),
            (own_hbm, own_ref),
            (other_hbm, other_ref),
            (w_hbm.at[core, :, pl.ds(0, 3 * width)], iw_ref),
        ]
        + tap_loads(layer, core, ch_hbm, st_hbm, ct_ref, st_ref),
        in_sems,
    )
    mid_ref[near, :] = mid_own_ref[...]
    mid_ref[far, :] = mid_other_ref[...]
    clear_ends(pad, length)
    clear_ends(epad, length)
    clear_ends(kpad, length)
    dsw_sum[...] = jnp.zeros(dsw_sum.shape, F32)
    dcw_sum[...] = jnp.zeros(dcw_sum.shape, F32)
    ch_rows[...] = jnp.zeros(ch_rows.shape, F32)
    st_rows[...] = jnp.zeros(st_rows.shape, F32)
    for p in range(3):
        rows = pl.ds(pl.multiple_of(p * features + (1 - core) * width, STRIP), width)
        dst_ref[rows, :] = jnp.zeros((width, LANES), BF)
    rest_ref[1 - core, :, pl.ds(0, 3 * width)] = jnp.zeros((features, 3 * width), BF)
    for h in range(2):
        rest_ref[h, apart, out_cols] = jnp.zeros((width, width), BF)
    for copy in loads[:4]:
        copy.wait()
    out_w = jnp.concatenate([ow_ref[0], ow_ref[1]], axis=1)

    @pl.loop(0, length // ROWS)
    def _(i):
        row0 = pl.multiple_of(i * ROWS, ROWS)
        rows = pl.ds(row0, ROWS)
        dg = dot(mid_ref[rows, :], out_w, ((1,), (1,)))
        first = row0 + lax.broadcasted_iota(jnp.int32, (ROWS, width), 0) < split
        pad[pl.ds(row0 + 8, ROWS), pl.ds(0, width)] = dg * conv_ref[rows, :].astype(F32)
        dc = dg * q_ref[rows, :].astype(F32)
        g[0, rows, :] = jnp.where(first, dc, 0.0).astype(BF)
        g[1, rows, :] = jnp.where(first, 0.0, dc).astype(BF)

    scale = 1.0 / half
    for copy in loads[4:7]:
        copy.wait()

    def transform(spans):
        @pl.loop(0, half // BINS)
        def _(i):
            rows = pl.ds(pl.multiple_of(i * 2 * BINS, 2 * BINS), 2 * BINS)
            f = fh_ref[rows, :].astype(F32)
            fr, fi = f[:BINS], f[BINS:]
            er = None
            for m in range(2):
                s = dot(fwd_ref[rows, spans[m]], g[m, spans[m], :])
                sr, si = s[:BINS], s[BINS:]
                prod[m, rows, 0:width] = jnp.concatenate(
                    [(fr * sr + fi * si) * scale, (fr * si - fi * sr) * scale], axis=0
                ).astype(BF)
                w = uh_ref[m, rows, :].astype(F32)
                wr, wi = w[:BINS], w[BINS:]
                tr = wr * sr + wi * si
                ti = wr * si - wi * sr
                er, ei = (tr, ti) if er is None else (er + tr, ei + ti)
            e = jnp.concatenate([er * scale, ei * scale], axis=0).astype(BF)
            for m in range(2):
                prod[m, rows, width : 2 * width] = e

    by_corner(split, length, transform)
    corner = split // ROWS
    value_cols = pl.ds(2 * width, width)
    for copy in loads[7:10]:
        copy.wait()
    kpad[pl.ds(8, length), :] = key_ref[...].astype(F32)

    @pl.loop(0, length // ROWS)
    def _(i):
        row0 = pl.multiple_of(i * ROWS, ROWS)
        rows = pl.ds(row0, ROWS)
        spot = pl.ds(row0 + 8, ROWS)
        pick = (i > corner).astype(jnp.int32)
        both = dot(inv_ref[rows, :], prod[pick])
        pad[spot, value_cols] = both[:, :width]

        @pl.when(i == corner)
        def _():
            later = i * ROWS + lax.broadcasted_iota(jnp.int32, (ROWS, width), 0) >= split
            other = dot(inv_ref[rows, :], prod[1, :, 0:width])
            pad[spot, value_cols] = jnp.where(later, other, pad[spot, value_cols])

        inside = row0 + lax.broadcasted_iota(jnp.int32, (ROWS, width), 0) < half
        epad[spot, :] = jnp.where(inside, both[:, width:], 0.0) * decay_ref[rows, :]

    def key_taps(row0, same):
        spot = pl.ds(row0 + 8, CHUNK)
        for strip in range(strips):
            cols = pl.ds(strip * STRIP, STRIP)
            e = epad[spot, cols]
            pad[spot, pl.ds(width + strip * STRIP, STRIP)] = weigh(shifted(epad, row0, cols, same), cw_ref, 2, cols, True)
            for off, x in enumerate(shifted(kpad, row0, cols, same)):
                dcw_sum[off, :, cols] += (x * e).reshape(CHUNK // 8, 8, STRIP).sum(0)

    for copy in loads[15:]:
        copy.wait()
    cw_ref[...] = ct_ref[...].astype(F32).T
    sw_ref[...] = st_ref[...].astype(F32).T
    over_chunks(length, split, key_taps)
    loads[10].wait()

    @pl.loop(0, 3 * strips)
    def _(strip):
        cols = pl.ds(pl.multiple_of(strip * STRIP, STRIP), STRIP)
        kpad[pl.ds(8, length), pl.ds(0, STRIP)] = br_ref[:, cols].astype(F32)

        def branch_taps(row0, same):
            e = pad[pl.ds(row0 + 8, CHUNK), cols]
            total = weigh(shifted(pad, row0, cols, same), sw_ref, 0, cols, True)
            dbr_ref[pl.ds(row0, CHUNK), cols] = total.astype(BF)
            for off, x in enumerate(shifted(kpad, row0, pl.ds(0, STRIP), same)):
                dsw_sum[off, :, cols] += (x * e).reshape(CHUNK // 8, 8, STRIP).sum(0)

        over_chunks(length, split, branch_taps)

    ch_rows[1:2, :] = dmg_ref[...]
    st_rows[0:5, :] = jnp.sum(dsw_sum[...], axis=1)
    ch_rows[2:7, part] = jnp.sum(dcw_sum[...], axis=1)
    dch_ref[...] = ch_rows[...].T.astype(BF)
    for p in range(3):
        rows = pl.ds(pl.multiple_of(p * features + core * width, STRIP), width)
        dst_ref[rows, :] = st_rows[:, p * width : (p + 1) * width].T.astype(BF)
    for copy in loads[11:15]:
        copy.wait()
    d_out = dot(gated_ref[...], mid_ref[...], ((0,), (0,))).astype(BF)
    for h in range(2):
        rest_ref[h, part, out_cols] = d_out[:, h * width : (h + 1) * width]
    for cols in (pl.ds(0, 2 * width), pl.ds(2 * width, width)):
        d_in = dot(own_ref[...], dbr_ref[near, cols], ((0,), (0,)))
        d_in += dot(other_ref[...], dbr_ref[far, cols], ((0,), (0,)))
        rest_ref[core, :, cols] = d_in.astype(BF)
    dn_ref[...] = dot(dbr_ref[near, :], iw_ref[...], ((1,), (1,))).astype(BF)
    dn_send_ref[...] = dot(dbr_ref[far, :], iw_ref[...], ((1,), (1,))).astype(BF)


def local_call(kernel, args, direct, outs, direct_outs, scratch):
    vmem, anywhere = pl.BlockSpec(memory_space=pltpu.VMEM), pl.BlockSpec(memory_space=pl.ANY)
    return pl.pallas_call(
        kernel,
        out_shape=[jax.ShapeDtypeStruct(shape, dtype) for shape, dtype in outs],
        in_specs=[pl.BlockSpec(memory_space=pltpu.SMEM)]
        + [vmem] * (direct - 1)
        + [anywhere] * (len(args) - direct),
        out_specs=[vmem] * direct_outs + [anywhere] * (len(outs) - direct_outs),
        scratch_shapes=scratch,
        compiler_params=pltpu.CompilerParams(vmem_limit_bytes=VMEM_LIMIT),
    )(*args)


def tap_scratch(width):
    return [((width, LANES), BF), ((3 * width, LANES), BF), ((LANES, width), F32), ((LANES, 3 * width), F32)]


def mixer_forward(layer, split, own, other, ch, st, weight, decay, fwd, inv):
    _, length, width = decay.shape
    features = own.shape[1]
    bins = fwd.shape[0]
    tall, short, wide = (length, width), (own.shape[0], width), (length, 3 * width)
    kept = [(wide, BF), (tall, BF), (tall, BF), (tall, BF), ((bins, width), BF), ((2, bins, width), BF)]
    scratch = [((features, 3 * width), BF), (tall, F32), (fwd.shape, BF), (inv.shape, BF)] + kept + tap_scratch(width)
    scratch += [
        ((length + 16, 3 * width), F32),
        ((length + 16, width), F32),
        (tall, BF),
        ((2,) + tall, BF),
        ((2, bins, width), BF),
    ]
    return local_call(
        functools.partial(mixer_forward_kernel, layer),
        (split, own, other, ch, st, weight, decay, fwd, inv),
        3,
        [(tall, BF), (short, BF), (short, BF)] + kept,
        3,
        [pltpu.VMEM(*x) for x in scratch] + [pltpu.SemaphoreType.DMA((8,)), pltpu.SemaphoreType.DMA((6,))],
    )


def mixer_backward(
    layer, split, mid_own, mid_other, dmg, ch, st, weight, own, other, gated, br, decay, fwd, inv, q, key, conv, fh, uh
):
    _, length, width = decay.shape
    bins = fwd.shape[0]
    rows, features = mid_own.shape
    held = (own, other, gated, br, decay, fwd, inv, q, key, conv, fh, uh)
    scratch = [((2, width, width), BF), ((features, 3 * width), BF)]
    scratch += [(x.shape[1:] if x is decay else x.shape, x.dtype) for x in held] + tap_scratch(width)
    scratch += [
        ((length + 16, 3 * width), F32),
        ((length + 16, width), F32),
        ((length + 16, width), F32),
        ((2, length, width), BF),
        ((2, bins, 2 * width), BF),
        ((length, features), BF),
        ((length, 3 * width), BF),
        ((5, 8, 3 * width), F32),
        ((5, 8, width), F32),
        ((LANES, features), F32),
        ((LANES, 3 * width), F32),
    ]
    return local_call(
        functools.partial(mixer_backward_kernel, layer),
        (split, mid_own, mid_other, dmg, ch, st, weight) + held,
        4,
        [
            ((2, features, 4 * width), BF),
            ((rows, features), BF),
            ((rows, features), BF),
            ((features, LANES), BF),
            ((3 * features, LANES), BF),
        ],
        5,
        [pltpu.VMEM(*x) for x in scratch] + [pltpu.SemaphoreType.DMA((19,))],
    )


def cube(dp_count):
    bits = (dp_count // 2).bit_length() - 1
    core, seq = bits, bits + 1
    low, rest = [bits - 1], list(range(bits - 1))
    orders = (
        rest + [seq] + low, rest + low + [seq], low + [seq] + rest,
        low + rest + [seq], [seq] + rest + low, [seq] + low + rest,
    )
    return bits, core, seq, orders


def place(bits):
    dp, seq = lax.axis_index("dp"), lax.axis_index("seq")
    coords = [(dp // (2 << (bits - 1 - d))) % 2 for d in range(bits)] + [dp % 2, seq]

    def neighbour(d):
        if d == bits + 1:
            return dp, 1 - seq
        step = 1 if d == bits else 2 << (bits - 1 - d)
        return dp + step * (1 - 2 * coords[d]), seq

    return coords, neighbour


def region(fixed, dims):
    return tuple(fixed[d] if d in fixed else slice(None) for d in range(dims))


def across(coords, bits):
    dp = lax.axis_index("dp")
    core, seq = coords[bits], coords[bits + 1]
    return core != seq, (dp + 1 - 2 * core, 1 - seq)


def greet(neighbours):
    barrier = pltpu.get_barrier_semaphore()
    for device in neighbours:
        pl.semaphore_signal(barrier, inc=1, device_id=device, device_id_type=pl.DeviceIdType.MESH)
    pl.semaphore_wait(barrier, len(neighbours))


class Swap:
    def __init__(self, src, dst, send, recv, local, moves, partner):
        self.stays, self.moves = jnp.logical_not(moves), moves
        self.away = pltpu.make_async_remote_copy(
            src_ref=src, dst_ref=dst, send_sem=send, recv_sem=recv,
            device_id=partner, device_id_type=pl.DeviceIdType.MESH,
        )
        self.here = pltpu.make_async_copy(src, dst, local)

    def start(self):
        pl.when(self.moves)(lambda: self.away.start())
        pl.when(self.stays)(lambda: self.here.start())

    def wait(self):
        pl.when(self.moves)(lambda: self.away.wait())
        pl.when(self.stays)(lambda: self.here.wait())


def remote(src, dst, send, recv, device):
    copy = pltpu.make_async_remote_copy(
        src_ref=src, dst_ref=dst, send_sem=send, recv_sem=recv,
        device_id=device, device_id_type=pl.DeviceIdType.MESH,
    )
    copy.start()
    return copy


GATHER_UNITS = (
    (3, 0, 640, 0, 0), (3, 640, 512, 1, 0), (3, 1152, 384, 2, 0), (5, 0, 128, 2, 0), (6, 0, 128, 1, 0),
    (0, 0, 768, 0, 1), (0, 768, 768, 1, 1), (2, 2, 2, 2, 1),
    (0, 1536, 768, 0, 2), (0, 2304, 768, 1, 2),
    (1, 0, 2, 0, 3), (1, 2, 2, 1, 3), (4, 1280, 256, 2, 3),
    (4, 0, 640, 0, 4), (4, 640, 640, 1, 4),
    (2, 0, 1, 0, 5), (2, 1, 1, 1, 5),
)
SCATTER_UNITS = (
    (0, 0, 768, 0, 0), (0, 768, 768, 1, 0), (2, 2, 2, 2, 0),
    (0, 1536, 768, 0, 1), (0, 2304, 768, 1, 1), (3, 1280, 256, 2, 1),
    (1, 0, 2, 0, 2), (1, 2, 2, 1, 2), (4, 1280, 256, 2, 2),
    (3, 0, 640, 0, 3), (3, 640, 640, 1, 3), (5, 0, 128, 2, 3), (6, 0, 128, 2, 3),
    (4, 0, 640, 0, 4), (4, 640, 640, 1, 4), (7, 0, 128, 2, 4),
    (2, 0, 1, 0, 5), (2, 1, 1, 0, 5),
)


def piece_of(unit, slabs):
    span = pl.ds(unit[1], unit[2])
    return (span, slice(None), slice(None)) if slabs else (slice(None), span)


def ticks(units, stages, shrinking):
    steps = [max(2**t, 2 ** (stages - 2)) for t in range(stages)]
    if shrinking:
        steps = steps[::-1]
    spacing = 2**stages // 4
    due = []
    for i, unit in enumerate(units):
        if shrinking:
            due.append((spacing * (unit[4] - 1) - 1, i, -1))
        due += [(spacing * unit[4] + sum(steps[:t]), i, t) for t in range(stages + 1)]
    return [(i, t) for _, i, t in sorted(due)]


def gather_kernel(dp_count, units, rows_in, rows_out, own, full, sems):
    bits, core_dim, _, orders = cube(dp_count)
    dims = bits + 2
    stages = dims - 1
    coords, neighbour = place(bits)
    core = coords[core_dim]
    sibling = neighbour(core_dim)
    moves, partner = across(coords, bits)
    greet([neighbour(d) for d in range(dims)] + [partner])
    ici_send, ici_recv, core_send, core_recv, local, swap_send, swap_recv, swap_local = sems
    swaps = [
        Swap(src, dst, swap_send.at[i], swap_recv.at[i], swap_local.at[i], moves, partner)
        for i, (src, dst) in enumerate(zip(rows_in, rows_out))
    ]
    mine = region(dict(enumerate(coords)), dims)
    firsts, forwards, sends = [], [], []
    last = [None] * len(units)
    for u, unit in enumerate(units):
        array, tail = unit[0], piece_of(unit, len(own[unit[0]].shape) == 4)
        piece = own[array].at[(slice(None),) + tail]
        here = full[array].at[(slice(None),) + mine + tail]
        keep = pltpu.make_async_copy(piece, here, local.at[u])
        keep.start()
        firsts.append((keep, remote(piece, here, core_send.at[u, 0], core_recv.at[u, 0], sibling)))
    for number, (u, t) in enumerate(ticks(units, stages, False)):
        if number == 4:
            for swap in swaps:
                swap.start()
        unit = units[u]
        array, tail, order = unit[0], piece_of(unit, len(own[unit[0]].shape) == 4), orders[unit[3]]
        fixed = {e: coords[e] for e in order[t:]}
        if t == 0:
            firsts[u][0].wait()
            firsts[u][1].wait_recv()
        else:
            last[u].wait_recv()
            got = full[array].at[(core,) + region(fixed | {order[t - 1]: 1 - coords[order[t - 1]]}, dims) + tail]
        if t < stages:
            held = full[array].at[(core,) + region(fixed, dims) + tail]
            last[u] = remote(held, held, ici_send.at[u, t], ici_recv.at[u, t], neighbour(order[t]))
            sends.append(last[u])
        if t > 0:
            forwards.append(remote(got, got, core_send.at[u, t], core_recv.at[u, t], sibling))
    for swap in swaps:
        swap.wait()
    beside = remote(rows_out[0], rows_out[-1], swap_send.at[len(swaps)], swap_recv.at[len(swaps)], sibling)
    for keep, copy in firsts:
        copy.wait_send()
    for copy in forwards:
        copy.wait()
    for copy in sends:
        copy.wait_send()
    beside.wait()


def gather_weights(rows, own, dp_count, number):
    bits = cube(dp_count)[0]
    stages = bits + 1
    units = GATHER_UNITS
    arrays = len(own)
    count = len(units)

    def body(*refs):
        rows_in, refs = refs[: len(rows)], refs[len(rows) :]
        own_refs, refs = refs[:arrays], refs[arrays:]
        rows_out, refs = refs[: len(rows) + 1], refs[len(rows) + 1 :]
        gather_kernel(dp_count, units, rows_in, rows_out, own_refs, refs[:arrays], refs[arrays:])

    grid = (2,) * (bits + 2)
    anywhere = pl.BlockSpec(memory_space=pl.ANY)
    return pl.pallas_call(
        body,
        out_shape=[jax.ShapeDtypeStruct(x.shape, x.dtype) for x in (*rows, rows[0])]
        + [jax.ShapeDtypeStruct(x.shape[:1] + grid + x.shape[1:], x.dtype) for x in own],
        in_specs=[anywhere] * (len(rows) + arrays),
        out_specs=[anywhere] * (len(rows) + 1 + arrays),
        scratch_shapes=[pltpu.SemaphoreType.DMA((count, stages))] * 2
        + [pltpu.SemaphoreType.DMA((count, stages + 1))] * 2
        + [pltpu.SemaphoreType.DMA((count,))]
        + [pltpu.SemaphoreType.DMA((len(rows) + 1,))] * 3,
        compiler_params=pltpu.CompilerParams(collective_id=number, has_side_effects=True),
    )(*rows, *own)


def scatter_kernel(dp_count, units, ends_in, token_ref, grads, outs, held, first, arrived, final, work, sems):
    bits, core_dim, _, orders = cube(dp_count)
    dims = bits + 2
    stages = dims - 1
    coords, neighbour = place(bits)
    core = coords[core_dim]
    sibling = neighbour(core_dim)
    moves, partner = across(coords, bits)
    greet([neighbour(d) for d in range(dims)] + [partner])
    ici_send, ici_recv, core_send, core_recv, local, end_send, end_recv, end_local = sems
    x_ref, dn_ref, away_ref, dmid_ref, gain_ref, dng_ref = ends_in
    other_ref, grad_ref, sum_ref, flat_ref, tall_ref, slab_ref = work
    grads = list(grads) + [slab_ref]
    exchange = remote(away_ref, other_ref, end_send.at[0], end_recv.at[0], sibling)
    begin = pltpu.make_async_copy(dmid_ref, grad_ref, end_local.at[1])
    begin.start()
    swap = Swap(other_ref, token_ref, end_send.at[1], end_recv.at[1], end_local.at[0], moves, partner)

    def finish_rows():
        exchange.wait()
        begin.wait()
        sum_ref[...] = jnp.zeros(sum_ref.shape, F32)
        share = slab_ref.shape[-2]

        @pl.loop(0, x_ref.shape[0] // 128)
        def _(i):
            rows = pl.ds(pl.multiple_of(i * 128, 128), 128)
            d = dn_ref[rows, :].astype(F32) + other_ref[rows, :].astype(F32)
            dx, dg = norm_back(x_ref[rows, :].astype(F32), gain_ref[...], d)
            other_ref[rows, :] = (grad_ref[rows, :] + dx).astype(BF)
            sum_ref[0:1, :] += dg

        swap.start()
        flat_ref[...] = jnp.zeros(flat_ref.shape, F32)
        for layer, row in enumerate((sum_ref, dng_ref)):
            for c in range(tall_ref.shape[0] // LANES):
                cols = slice(c * LANES, (c + 1) * LANES)
                flat_ref[0:1, :] = row[0:1, cols]
                tall_ref[cols, :] = flat_ref[...].T
            for i in range(2**dims):
                at = tuple((i >> (dims - 1 - d)) % 2 for d in range(dims))
                slab_ref[(layer,) + at] = tall_ref[i * share : (i + 1) * share, :].astype(BF)

    everything = region({}, dims)

    def add(u, fixed, extra):
        free = [d for d in range(dims) if d not in fixed]

        @pl.loop(0, 2 ** len(free))
        def _(i):
            at = {d: (i // 2 ** (len(free) - 1 - j)) % 2 for j, d in enumerate(free)}
            index = tuple(at[d] if d in at else fixed[d] for d in range(dims))
            held[u][index] += extra[tuple(at[d] for d in free)]

    starts, sends = [None] * len(units), []
    last = [None] * len(units)
    for u, t in ticks(units, stages, True):
        if t < 0 and units[u][0] == len(grads) - 1:
            finish_rows()
        if t < 0:
            array, tail = units[u][0], piece_of(units[u], len(outs[units[u][0]].shape) == 4)
            load = pltpu.make_async_copy(grads[array].at[(core,) + everything + tail], held[u], local.at[u, 0])
            load.start()
            other = grads[array].at[(1 - core,) + everything + tail]
            starts[u] = (load, remote(other, first[u], core_send.at[u, 0], core_recv.at[u, 0], sibling))
            continue
        order = orders[units[u][3]][::-1]
        fixed = {d: coords[d] for d in order[:t]}
        if t == 0:
            starts[u][0].wait()
            starts[u][1].wait_recv()
            add(u, fixed, first[u])
        else:
            last[u].wait_recv()
            add(u, fixed, arrived[u][t - 1])
        if t < stages:
            away = held[u].at[region(fixed | {order[t]: 1 - coords[order[t]]}, dims)]
            last[u] = remote(away, arrived[u][t], ici_send.at[u, t], ici_recv.at[u, t], neighbour(order[t]))
            sends.append(last[u])
        else:
            away = held[u].at[region(fixed | {core_dim: 1 - core}, dims)]
            last[u] = remote(away, final[u], core_send.at[u, 1], core_recv.at[u, 1], sibling)
    ends = []
    mine = region(dict(enumerate(coords)), dims)
    for u, unit in enumerate(units):
        array, tail = unit[0], piece_of(unit, len(outs[unit[0]].shape) == 4)
        own = pltpu.make_async_copy(held[u].at[mine], outs[array].at[(core,) + tail], local.at[u, 1])
        own.start()
        last[u].wait_recv()
        other = pltpu.make_async_copy(final[u], outs[array].at[(1 - core,) + tail], local.at[u, 2])
        other.start()
        ends += [own, other]
    swap.wait()
    for copy in ends:
        copy.wait()
    for copy in sends + last + [s[1] for s in starts]:
        copy.wait_send()


def scatter_grads(ends, grads, units, dp_count, number):
    bits = cube(dp_count)[0]
    dims = bits + 2
    stages = dims - 1
    count = len(units)
    grid = (2,) * dims
    rows, features = ends[0].shape
    share = grads[0].shape[1 + dims]
    tails = [x.shape[1 + dims :] for x in grads] + [(share, LANES)]
    arrays = len(tails)
    slabs = []
    for array, _, size, _, _ in units:
        shape = tails[array]
        slabs.append((size,) + shape[1:] if len(shape) == 3 else shape[:-1] + (size,))
    work = [((rows, features), BF), ((rows, features), F32), ((8, features), F32), ((LANES, LANES), F32)]
    work += [((features, LANES), F32), ((2,) + grid + (share, LANES), BF)]

    def body(*refs):
        ends_in, refs = refs[: len(ends)], refs[len(ends) :]
        grads_in, refs = refs[: len(grads)], refs[len(grads) :]
        token, outs, refs = refs[0], refs[1 : 1 + arrays], refs[1 + arrays :]
        held, first, final = refs[:count], refs[count : 2 * count], refs[2 * count : 3 * count]
        refs = refs[3 * count :]
        arrived = [refs[u * stages : (u + 1) * stages] for u in range(count)]
        refs = refs[count * stages :]
        scatter_kernel(
            dp_count, units, ends_in, token, grads_in, outs, held, first, arrived, final,
            refs[: len(work)], refs[len(work) :],
        )

    anywhere, vmem = pl.BlockSpec(memory_space=pl.ANY), pl.BlockSpec(memory_space=pltpu.VMEM)
    return pl.pallas_call(
        body,
        out_shape=[jax.ShapeDtypeStruct((rows, features), BF)]
        + [jax.ShapeDtypeStruct((2,) + tail, BF) for tail in tails],
        in_specs=[vmem, vmem, anywhere, anywhere, vmem, vmem] + [anywhere] * len(grads),
        out_specs=[anywhere] * (1 + arrays),
        scratch_shapes=[pltpu.VMEM(grid + slab, BF) for slab in slabs] * 2
        + [pltpu.VMEM(slab, BF) for slab in slabs]
        + [pltpu.VMEM((2,) * (dims - 1 - t) + slab, BF) for slab in slabs for t in range(stages)]
        + [pltpu.VMEM(*x) for x in work]
        + [pltpu.SemaphoreType.DMA((count, stages))] * 2
        + [pltpu.SemaphoreType.DMA((count, 2))] * 2
        + [pltpu.SemaphoreType.DMA((count, 3))]
        + [pltpu.SemaphoreType.DMA((2,))] * 2
        + [pltpu.SemaphoreType.DMA((2,))],
        compiler_params=pltpu.CompilerParams(
            collective_id=number, has_side_effects=True, vmem_limit_bytes=VMEM_LIMIT
        ),
    )(*ends, *grads)


def norm_parts(x):
    center = x - jnp.mean(x, axis=-1, keepdims=True)
    r = lax.rsqrt(jnp.mean(center * center, axis=-1, keepdims=True) + EPS)
    return center * r, r


def norm_back(x, gain, d):
    xhat, r = norm_parts(x)
    h = d * gain
    dx = r * (h - jnp.mean(h, axis=-1, keepdims=True) - xhat * jnp.mean(h * xhat, axis=-1, keepdims=True))
    return dx, jnp.sum(d * xhat, axis=0, keepdims=True)


SLOPE = math.sqrt(2.0 / math.pi)
CUBE = 0.044715


def gelu_parts(x):
    square = x * x
    t = jnp.tanh(SLOPE * (x + CUBE * square * x))
    flat = 0.5 + 0.5 * t
    return x * flat, flat + 0.5 * x * (1.0 - t * t) * (SLOPE + 3.0 * SLOPE * CUBE * square)


def mlp_forward_kernel(
    gain, next_gain, x_ref, g0_ref, g1_ref, o0_ref, o1_ref, gains_ref, wg_ref, wu_ref, d0_ref, d1_ref,
    mid_ref, hm_ref, pre_ref, out_ref, next_ref,
):
    j = pl.program_id(0)

    @pl.when(j == 0)
    def _():
        width = g0_ref.shape[1]
        mid = x_ref[...]
        core = lax.axis_index("dp") % 2
        for ref, side in ((g0_ref, core), (g1_ref, 1 - core)):
            rows = pl.ds(pl.multiple_of(side * width, STRIP), width)
            mid += dot(ref[...], jnp.concatenate([o0_ref[rows, :], o1_ref[rows, :]], axis=1))
        mid_ref[...] = mid
        out_ref[...] = mid
        hm_ref[...] = (norm_parts(mid)[0] * gains_ref[gain : gain + 1, :]).astype(BF)

    hm = hm_ref[...]
    total = out_ref[...]
    for i in range(TILE // PART_F):
        part = slice(i * PART_F, (i + 1) * PART_F)
        gate = dot(hm, wg_ref[:, part])
        up = dot(hm, wu_ref[:, part])
        pre_ref[0, :, part] = gate.astype(BF)
        pre_ref[1, :, part] = up.astype(BF)
        hid = (gelu_parts(gate)[0] * up).astype(BF)
        total += dot(hid, jnp.concatenate([d0_ref[part, :], d1_ref[part, :]], axis=1))
    out_ref[...] = total

    @pl.when(j == pl.num_programs(0) - 1)
    def _():
        next_ref[...] = (norm_parts(out_ref[...])[0] * gains_ref[next_gain : next_gain + 1, :]).astype(BF)


def mlp_backward_kernel(
    gain, g_ref, hm_ref, mid_ref, gains_ref, pre_ref, wg_ref, wu_ref, d0_ref, d1_ref,
    dgu_ref, ddn_ref, dmid_ref, mlow_ref, dmg_ref,
    glow, hm_t, acc,
):
    j = pl.program_id(0)
    width = d0_ref.shape[1]

    @pl.when(j == 0)
    def _():
        glow[...] = g_ref[...].astype(BF)
        hm_t[...] = hm_ref[...].T
        acc[...] = jnp.zeros(acc.shape, F32)

    low, hm = glow[...], hm_t[...]
    total = acc[...]
    for i in range(TILE // PART_B):
        part = slice(i * PART_B, (i + 1) * PART_B)
        dh = dot(low, jnp.concatenate([d0_ref[part, :], d1_ref[part, :]], axis=1), ((1,), (1,)))
        value, slope = gelu_parts(pre_ref[0, :, part].astype(F32))
        up = pre_ref[1, :, part].astype(F32)
        hid = (value * up).astype(BF)
        d_gate = (dh * up * slope).astype(BF)
        d_up = (dh * value).astype(BF)
        d_down = dot(hid, low, ((0,), (0,))).astype(BF)
        ddn_ref[0, part, :] = d_down[:, :width]
        ddn_ref[1, part, :] = d_down[:, width:]
        for h, d in enumerate((d_gate, d_up)):
            grad = dot(hm, d).astype(BF)
            if len(dgu_ref.shape) == 3:
                dgu_ref[h, :, part] = grad
            else:
                dgu_ref[:, h * TILE + i * PART_B : h * TILE + (i + 1) * PART_B] = grad
        total += dot(d_gate, wg_ref[:, part], ((1,), (1,))) + dot(d_up, wu_ref[:, part], ((1,), (1,)))
    acc[...] = total

    @pl.when(j == pl.num_programs(0) - 1)
    def _():
        dx, dg = norm_back(mid_ref[...], gains_ref[gain : gain + 1, :], acc[...])
        dmid = g_ref[...] + dx
        dmid_ref[...] = dmid
        mlow_ref[...] = dmid.astype(BF)
        dmg_ref[...] = dg


TILE = 512
PART_F = 512
PART_B = 512


def whole(shape):
    return pl.BlockSpec(shape, lambda j: (0,) * len(shape))


def weight_specs(layout, hidden, features):
    steps = hidden // TILE
    gate_up = pl.BlockSpec((features, TILE), lambda j: (0, j))
    up = pl.BlockSpec((features, TILE), lambda j: (1, j) if layout == "halves" else (0, steps + j))
    down = [
        pl.BlockSpec((TILE, features // 2), lambda j: (j, 0)),
        pl.BlockSpec((TILE, features // 2), lambda j: (steps + j, 0)),
    ]
    return [gate_up, up] + down


def mlp_forward(x, g0, g1, weight, gains, gain, next_gain, weights):
    layout, gu, dn = weights
    rows, features = x.shape
    hidden = dn.shape[0] // 2
    square = whole((rows, features))
    narrow = [whole(a.shape) for a in (g0, g1)]
    narrow += [pl.BlockSpec((features, features // 2), lambda j, h=h: (h, 3)) for h in range(2)]
    shapes = [((rows, features), F32), ((rows, features), BF), ((2, rows, hidden), BF), ((rows, features), F32), ((rows, features), BF)]
    return pl.pallas_call(
        functools.partial(mlp_forward_kernel, gain, next_gain),
        grid=(hidden // TILE,),
        out_shape=[jax.ShapeDtypeStruct(*s) for s in shapes],
        in_specs=[square] + narrow + [whole(gains.shape)] + weight_specs(layout, hidden, features),
        out_specs=[square, square, pl.BlockSpec((2, rows, TILE), lambda j: (0, 0, j)), square, square],
        compiler_params=pltpu.CompilerParams(vmem_limit_bytes=VMEM_LIMIT),
    )(x, g0, g1, weight, weight, gains, gu, gu, dn, dn)


def mlp_backward(g, hm, mid, gains, gain, pre, weights, side_by_side):
    layout, gu, dn = weights
    rows, features = g.shape
    hidden = pre.shape[2]
    width = features // 2
    square, vector = whole((rows, features)), whole((1, features))
    both = (features, 2 * hidden) if side_by_side else (2, features, hidden)
    shapes = [(both, BF), ((2, hidden, width), BF), ((rows, features), F32), ((rows, features), BF), ((1, features), F32)]
    return pl.pallas_call(
        functools.partial(mlp_backward_kernel, gain),
        grid=(hidden // TILE,),
        out_shape=[jax.ShapeDtypeStruct(*s) for s in shapes],
        in_specs=[square] * 3
        + [whole(gains.shape), pl.BlockSpec((2, rows, TILE), lambda j: (0, 0, j))]
        + weight_specs(layout, hidden, features),
        out_specs=[
            pl.BlockSpec((features, 2 * TILE), lambda j: (0, j))
            if side_by_side
            else pl.BlockSpec((2, features, TILE), lambda j: (0, 0, j)),
            pl.BlockSpec((2, TILE, width), lambda j: (0, j, 0)),
            square, square, vector,
        ],
        scratch_shapes=[pltpu.VMEM((rows, features), BF), pltpu.VMEM((features, rows), BF), pltpu.VMEM((rows, features), F32)],
        compiler_params=pltpu.CompilerParams(vmem_limit_bytes=VMEM_LIMIT),
    )(g, hm, mid, gains, pre, gu, gu, dn, dn)


def shards(
    tokens, split_points, cotangent, norm_gain, in_weight, short_taps, cond_taps,
    out_weight, mlp_gain, gate_up, down_weight,
):
    rows, features = tokens.shape[1:]
    dp_count, seq_count = lax.axis_size("dp"), lax.axis_size("seq")
    devices = dp_count * seq_count
    length = rows * seq_count
    width = features // 2
    layers = in_weight.shape[0]
    share = norm_gain.shape[1]
    hidden = down_weight.shape[1] * devices
    core = lax.axis_index("dp") % 2
    seq = lax.axis_index("seq")

    swap = [(4 * k + a, 4 * k + 3 - a) for k in range(devices // 4) for a in (1, 2)]
    flip = [(i, i ^ 1) for i in range(dp_count)]

    def swap_rows(x):
        return jnp.where(core == seq, x, lax.ppermute(x, AXES, swap))

    def sibling(x):
        return lax.ppermute(x, "dp", flip)

    def beside(own, other, axis):
        return jnp.where(
            core == 0,
            jnp.concatenate([own, other], axis=axis),
            jnp.concatenate([other, own], axis=axis),
        )

    def half_of(x, which, axis):
        size = x.shape[axis] // 2
        return lax.dynamic_slice_in_dim(x, which * size, size, axis)

    table = transform_matrix(length)
    fwd = jnp.asarray(table, BF)
    inv = jnp.asarray(np.ascontiguousarray(table.T), BF)
    decay = jnp.asarray(decay_table(length, features))

    def halves(x):
        parts = x.shape[-1] // features
        x = x.reshape(x.shape[:-1] + (parts, 2, width))
        x = jnp.moveaxis(x, -2, 0)
        return x.reshape(x.shape[:-2] + (parts * width,))

    grid = (2,) * (cube(dp_count)[0] + 2)

    ch = jnp.concatenate([norm_gain[:, :, None], mlp_gain[:, :, None], cond_taps.transpose(0, 2, 1)], axis=2)
    ch = jnp.pad(ch, ((0, 0), (0, 0), (0, LANES - 7)))
    st = jnp.pad(short_taps.transpose(0, 2, 1), ((0, 0), (0, 0), (0, LANES - 5)))
    own = [gate_up[0].reshape(share, 2, hidden).transpose(1, 0, 2)]
    own += [halves(down_weight[layer]).reshape(2, hidden // features, share, width) for layer in range(layers)]
    for layer in range(layers):
        own.append(jnp.concatenate([halves(in_weight[layer]), halves(out_weight[layer])], axis=2))
    place_rows = [tokens[0], jnp.broadcast_to(split_points, (8, LANES))]
    x_low, split, x_far, *full = gather_weights(place_rows, own + [ch, st], dp_count, 0)
    downs = [x.reshape(2 * hidden, width) for x in full[1 : 1 + layers]]
    mixer_w = [x.reshape(2, features, 4 * width) for x in full[1 + layers : 1 + 2 * layers]]
    ch, st = full[-2].reshape(layers, features, LANES), full[-1].reshape(layers, 3 * features, LANES)
    late, _ = lax.optimization_barrier((gate_up[1:], full[0]))
    gate_ups = [("halves", full[0].reshape(2 * features, hidden))]
    gate_ups += [("plain", lax.all_gather(x, AXES, axis=0, tiled=True)) for x in late]
    gains = ch[:, :, :2].astype(F32).transpose(0, 2, 1).reshape(2 * layers, features)
    stream, far = x_low.astype(F32), x_far.astype(F32)
    grad = swap_rows(cotangent)[0].astype(F32)
    normed, normed_far = [(norm_parts(x)[0] * gains[0]).astype(BF) for x in (stream, far)]
    kept = []
    for layer in range(layers):
        if layer > 0:
            normed_far = sibling(normed)
        gated, mine, away, branches, q, key, conv, fh, uh = mixer_forward(
            layer, split, normed, normed_far, ch, st, mixer_w[layer], decay, fwd, inv
        )
        middle, normed_mlp, pre, out, normed_next = mlp_forward(
            stream, mine, sibling(away), mixer_w[layer].reshape(2 * features, -1), gains,
            2 * layer + 1, (2 * layer + 2) % (2 * layers), gate_ups[layer] + (downs[layer],),
        )
        kept.append((stream, normed, normed_far, gated, branches, q, key, conv, fh, uh, middle, normed_mlp, pre))
        stream, normed = out, normed_next
    activations = swap_rows(stream.astype(BF)[None])

    summed = []
    early = [None] * layers
    for layer in reversed(range(layers)):
        x, normed, normed_far, gated, branches, q, key, conv, fh, uh, middle, normed_mlp, pre = kept[layer]
        d_gu, d_down, d_middle, m_low, d_mg = mlp_backward(
            grad, normed_mlp, middle, gains, 2 * layer + 1, pre, gate_ups[layer] + (downs[layer],), layer > 0
        )
        rest, d_normed, d_away, d_ch, d_st = mixer_backward(
            layer, split, m_low, sibling(m_low), d_mg, ch, st, mixer_w[layer], normed, normed_far, gated, branches,
            decay, fwd, inv, q, key, conv, fh, uh,
        )
        if layer > 0:
            early[layer] = lax.psum_scatter(d_gu, AXES, scatter_dimension=0, tiled=True)
            d_part, d_ng = norm_back(x, gains[2 * layer], d_normed.astype(F32) + sibling(d_away).astype(F32))
            grad = d_middle + d_part
        summed.append((d_gu, d_down, rest, d_ch, d_st))
    d_gus, d_downs, rests, *smalls = zip(*summed[::-1])
    pieces = [d_gus[0].reshape((2,) + grid + (share, hidden))]
    pieces += [x.reshape((2,) + grid + (hidden // features, share, width)) for x in d_downs]
    pieces += [x.reshape((2,) + grid + (share, 4 * width)) for x in rests]
    pieces += [jnp.stack(x).reshape((2,) + grid + (-1, LANES)) for x in smalls]
    ends = [x_low, d_normed, d_away, d_middle, gains[:1], d_ng]
    fits = share % 8 == 0
    units = tuple(unit for unit in SCATTER_UNITS if fits or unit[0] != 2)
    token_grad, *outs = scatter_grads(ends, pieces, units, dp_count, 1)
    if not fits:
        outs[2] = lax.psum_scatter(d_downs[1], AXES, scatter_dimension=1, tiled=True)
    token_grad = token_grad[None].astype(F32)

    def joined(x):
        parts = x.shape[-1] // width
        x = jnp.moveaxis(x.reshape(x.shape[:-1] + (parts, width)), 0, -2)
        return x.reshape(x.shape[:-3] + (parts * features,))

    early[0] = outs[0].transpose(1, 0, 2)
    for layer in range(1, layers):
        early[layer] = early[layer].reshape(share, hidden // TILE, 2, TILE).transpose(0, 2, 1, 3)
    g_gu = jnp.stack([x.reshape(share, 2 * hidden) for x in early]).astype(F32)
    g_down = jnp.stack([joined(x.reshape(2, -1, width)) for x in outs[1 : 1 + layers]]).astype(F32)
    rest = outs[1 + layers : 1 + 2 * layers]
    g_in = jnp.stack([joined(x[:, :, : 3 * width]) for x in rest]).astype(F32)
    g_out = jnp.stack([joined(x[:, :, 3 * width :]) for x in rest]).astype(F32)
    s_ch, s_st, s_ng = [x.astype(F32) for x in outs[1 + 2 * layers :]]
    g_ng, g_mg, g_ct, g_st = s_ng[:, :, 0], s_ch[:, :, 1], s_ch[:, :, 2:7].transpose(0, 2, 1), s_st[:, :, :5].transpose(0, 2, 1)
    return (
        activations,
        token_grad,
        g_ng,
        g_in,
        g_st,
        g_ct,
        g_out,
        g_mg,
        g_gu,
        g_down,
    )


def solution(mesh):
    every = ("dp", "seq")
    rows, part = P("dp", "seq", None), P(None, every, None)
    vector, taps = P(None, every), P(None, None, every)
    return jax.shard_map(
        shards,
        mesh=mesh,
        in_specs=(rows, P("dp"), rows, vector, part, taps, taps, part, vector, part, part),
        out_specs=(rows, rows, vector, part, taps, taps, part, vector, part, part),
        check_vma=False,
    )
```

```python
import functools
import math

import numpy as np
import jax
import jax.numpy as jnp
from jax import lax
from jax.experimental import pallas as pl
from jax.experimental.pallas import tpu as pltpu
from jax.sharding import PartitionSpec as P

BF = jnp.bfloat16
F32 = jnp.float32
EPS = 1e-05
AXES = ("dp", "seq")
GAP = 128
VMEM_LIMIT = 60 * 2**20
STRIP = 128
LANES = 128
BINS = 224
ROWS = 256
CHUNK = 128


def transform_matrix(length):
    half = length - GAP
    freq = np.arange(half)[:, None]
    place = np.arange(length)[None, :]
    angle = ((2 * freq + 1) * place % (4 * half)).astype(np.float64) * (math.pi / (2 * half))
    both = np.stack([np.cos(angle), -np.sin(angle)])
    both = both.reshape(2, half // BINS, BINS, length).transpose(1, 0, 2, 3)
    return both.reshape(2 * half, length).astype(np.float32)


def decay_table(length, features):
    positions = np.arange(length)
    rates = np.exp(math.log(1.0 / length) + np.arange(features) / (features - 1) * math.log(4.0))
    scales = np.sum(np.exp(-2.0 * positions[:, None] * rates[None, :]), axis=0) ** -0.5
    table = np.exp(-positions[:, None] * rates[None, :]) * scales[None, :]
    return np.stack(np.split(table, 2, axis=1)).astype(np.float32)


def dot(a, b, dims=((1,), (0,))):
    return lax.dot_general(a, b, (dims, ((), ())), preferred_element_type=F32)


def tap_same(row0, split):
    t = row0 + lax.broadcasted_iota(jnp.int32, (CHUNK, STRIP), 0)
    here = t >= split
    return [
        None if off == 2 else jnp.where(((t + (off - 2)) >= split) == here, 1.0, 0.0)
        for off in range(5)
    ]


def shifted(ref, row0, cols, same):
    block = ref[pl.ds(row0, CHUNK + 16), cols]
    out = []
    for off in range(5):
        turned = pltpu.roll(block, (2 - off) % (CHUNK + 16), 0) if off != 2 else block
        rows = turned[8 : 8 + CHUNK]
        out.append(rows if same[off] is None else rows * same[off])
    return out


def over_chunks(length, split, body):
    @pl.loop(0, length // CHUNK)
    def _(i):
        row0 = pl.multiple_of(i * CHUNK, CHUNK)
        touched = (split > row0 - 2) & (split < row0 + CHUNK + 2)

        @pl.when(touched)
        def _():
            body(row0, tap_same(row0, split))

        @pl.when(jnp.logical_not(touched))
        def _():
            body(row0, [None] * 5)


def tap_loads(layer, core, ch_hbm, st_hbm, ct_ref, st_ref):
    width = ct_ref.shape[0]
    own = pl.multiple_of(core * width, STRIP)
    pairs = [(ch_hbm.at[layer, pl.ds(own, width), :], ct_ref)]
    for part in range(3):
        rows = pl.ds(pl.multiple_of(part * 2 * width + own, STRIP), width)
        pairs.append((st_hbm.at[layer, rows, :], st_ref.at[pl.ds(part * width, width), :]))
    return pairs


def weigh(rows, w_ref, base, cols, flip):
    total = None
    for off, x in enumerate(rows):
        tap = base + (4 - off if flip else off)
        term = x * w_ref[tap : tap + 1, cols]
        total = term if total is None else total + term
    return total


def by_corner(split, length, body):
    for corner in range(length // ROWS):
        spans = (slice(0, (corner + 1) * ROWS), slice(corner * ROWS, length))
        pl.when(split // ROWS == corner)(functools.partial(body, spans))


def clear_ends(ref, length):
    ref[0:8, :] = jnp.zeros((8, ref.shape[1]), F32)
    ref[8 + length : 16 + length, :] = jnp.zeros((8, ref.shape[1]), F32)


def fetch(pairs, sems):
    copies = [pltpu.make_async_copy(src, dst, sems.at[i]) for i, (src, dst) in enumerate(pairs)]
    for copy in copies:
        copy.start()
    return copies


def mixer_forward_kernel(
    layer, split_ref, own_ref, other_ref, ch_hbm, st_hbm, iw_hbm, decay_hbm, fwd_hbm, inv_hbm,
    gated_ref, mine_ref, send_ref, br_hbm, q_hbm, key_hbm, conv_hbm, fh_hbm, uh_hbm,
    iw_ref, decay_ref, fwd_ref, inv_ref, br_ref, q_ref, key_ref, conv_ref, fh_ref, uh_ref,
    ct_ref, st_ref, cw_ref, sw_ref, pad, kpad, filt, u, prod, in_sems, out_sems,
):
    length, width = q_ref.shape
    rows_own = own_ref.shape[0]
    half = length - GAP
    split, core = split_ref[0, 0], lax.axis_index("dp") % 2
    strips = width // STRIP
    loads = fetch(
        [
            (iw_hbm.at[core, :, pl.ds(0, 3 * width)], iw_ref),
            (decay_hbm.at[core], decay_ref),
            (fwd_hbm, fwd_ref),
            (inv_hbm, inv_ref),
        ]
        + tap_loads(layer, core, ch_hbm, st_hbm, ct_ref, st_ref),
        in_sems,
    )
    outs = [(br_ref, br_hbm), (q_ref, q_hbm), (key_ref, key_hbm), (fh_ref, fh_hbm), (uh_ref, uh_hbm), (conv_ref, conv_hbm)]
    stores = [pltpu.make_async_copy(src, dst, out_sems.at[i]) for i, (src, dst) in enumerate(outs)]
    clear_ends(pad, length)
    clear_ends(kpad, length)
    loads[0].wait()
    for ref, side in ((own_ref, core), (other_ref, 1 - core)):

        @pl.loop(0, rows_own // ROWS)
        def _(i):
            row0 = pl.multiple_of(side * rows_own + i * ROWS, ROWS)
            low = dot(ref[pl.ds(pl.multiple_of(i * ROWS, ROWS), ROWS), :], iw_ref[...]).astype(BF)
            br_ref[pl.ds(row0, ROWS), :] = low
            pad[pl.ds(row0 + 8, ROWS), :] = low.astype(F32)

    stores[0].start()
    for copy in loads[4:]:
        copy.wait()
    cw_ref[...] = ct_ref[...].astype(F32).T
    sw_ref[...] = st_ref[...].astype(F32).T

    def mix(row0, same):
        rows = pl.ds(row0, CHUNK)
        first = row0 + lax.broadcasted_iota(jnp.int32, (CHUNK, STRIP), 0) < split
        for part in range(3):
            for strip in range(strips):
                cols = pl.ds(part * width + strip * STRIP, STRIP)
                own = pl.ds(strip * STRIP, STRIP)
                low = weigh(shifted(pad, row0, cols, same), sw_ref, 0, cols, False).astype(BF)
                if part == 0:
                    q_ref[rows, own] = low
                elif part == 1:
                    key_ref[rows, own] = low
                    kpad[pl.ds(row0 + 8, CHUNK), own] = low.astype(F32)
                else:
                    low = low.astype(F32)
                    u[0, rows, own] = jnp.where(first, low, 0.0).astype(BF)
                    u[1, rows, own] = jnp.where(first, 0.0, low).astype(BF)

    over_chunks(length, split, mix)
    stores[1].start()
    stores[2].start()
    loads[1].wait()

    def make_filter(row0, same):
        rows = pl.ds(row0, CHUNK)
        for strip in range(strips):
            cols = pl.ds(strip * STRIP, STRIP)
            total = weigh(shifted(kpad, row0, cols, same), cw_ref, 2, cols, False)
            filt[rows, cols] = (total * decay_ref[rows, cols]).astype(BF)

    over_chunks(length, split, make_filter)
    scale = 1.0 / half
    loads[2].wait()

    def transform(spans):
        @pl.loop(0, half // BINS)
        def _(i):
            rows = pl.ds(pl.multiple_of(i * 2 * BINS, 2 * BINS), 2 * BINS)
            f = dot(fwd_ref[rows, 0:half], filt[0:half, :])
            fr, fi = f[:BINS], f[BINS:]
            fh_ref[rows, :] = f.astype(BF)
            for m in range(2):
                s = dot(fwd_ref[rows, spans[m]], u[m, spans[m], :])
                uh_ref[m, rows, :] = s.astype(BF)
                sr, si = s[:BINS], s[BINS:]
                prod[m, rows, :] = jnp.concatenate(
                    [(fr * sr - fi * si) * scale, (fr * si + fi * sr) * scale], axis=0
                ).astype(BF)

    by_corner(split, length, transform)
    stores[3].start()
    stores[4].start()
    corner = split // ROWS
    loads[3].wait()

    @pl.loop(0, length // ROWS)
    def _(i):
        rows = pl.ds(pl.multiple_of(i * ROWS, ROWS), ROWS)
        pick = (i > corner).astype(jnp.int32)
        conv_ref[rows, :] = dot(inv_ref[rows, :], prod[pick]).astype(BF)

        @pl.when(i == corner)
        def _():
            later = i * ROWS + lax.broadcasted_iota(jnp.int32, (ROWS, width), 0) >= split
            other = dot(inv_ref[rows, :], prod[1])
            conv_ref[rows, :] = jnp.where(later, other, conv_ref[rows, :].astype(F32)).astype(BF)

        gated_ref[rows, :] = (q_ref[rows, :].astype(F32) * conv_ref[rows, :].astype(F32)).astype(BF)

    stores[5].start()
    mine_ref[...] = gated_ref[pl.ds(pl.multiple_of(core * rows_own, ROWS), rows_own), :]
    send_ref[...] = gated_ref[pl.ds(pl.multiple_of((1 - core) * rows_own, ROWS), rows_own), :]
    for copy in stores:
        copy.wait()


def mixer_backward_kernel(
    layer, split_ref, mid_own_ref, mid_other_ref, dmg_ref, ch_hbm, st_hbm,
    w_hbm, own_hbm, other_hbm, gated_hbm, br_hbm, decay_hbm, fwd_hbm, inv_hbm, q_hbm, key_hbm, conv_hbm, fh_hbm, uh_hbm,
    rest_ref, dn_ref, dn_send_ref, dch_ref, dst_ref,
    ow_ref, iw_ref, own_ref, other_ref, gated_ref, br_ref, decay_ref, fwd_ref, inv_ref, q_ref, key_ref, conv_ref, fh_ref,
    uh_ref, ct_ref, st_ref, cw_ref, sw_ref, pad, epad, kpad, g, prod, mid_ref, dbr_ref, dsw_sum, dcw_sum, ch_rows, st_rows,
    in_sems,
):
    length, width = q_ref.shape
    rows_own, features = own_ref.shape
    half = length - GAP
    split, core = split_ref[0, 0], lax.axis_index("dp") % 2
    strips = width // STRIP
    part = pl.ds(pl.multiple_of(core * width, STRIP), width)
    apart = pl.ds(pl.multiple_of((1 - core) * width, STRIP), width)
    near = pl.ds(pl.multiple_of(core * rows_own, ROWS), rows_own)
    far = pl.ds(pl.multiple_of((1 - core) * rows_own, ROWS), rows_own)
    out_cols = pl.ds(3 * width, width)
    loads = fetch(
        [
            (w_hbm.at[0, part, out_cols], ow_ref.at[0]),
            (w_hbm.at[1, part, out_cols], ow_ref.at[1]),
            (conv_hbm, conv_ref),
            (q_hbm, q_ref),
            (fwd_hbm, fwd_ref),
            (fh_hbm, fh_ref),
            (uh_hbm, uh_ref),
            (inv_hbm, inv_ref),
            (decay_hbm.at[core], decay_ref),
            (key_hbm, key_ref),
            (br_hbm, br_ref),
            (gated_hbm, gated_ref),
            (own_hbm, own_ref),
            (other_hbm, other_ref),
            (w_hbm.at[core, :, pl.ds(0, 3 * width)], iw_ref),
        ]
        + tap_loads(layer, core, ch_hbm, st_hbm, ct_ref, st_ref),
        in_sems,
    )
    mid_ref[near, :] = mid_own_ref[...]
    mid_ref[far, :] = mid_other_ref[...]
    clear_ends(pad, length)
    clear_ends(epad, length)
    clear_ends(kpad, length)
    dsw_sum[...] = jnp.zeros(dsw_sum.shape, F32)
    dcw_sum[...] = jnp.zeros(dcw_sum.shape, F32)
    ch_rows[...] = jnp.zeros(ch_rows.shape, F32)
    st_rows[...] = jnp.zeros(st_rows.shape, F32)
    for p in range(3):
        rows = pl.ds(pl.multiple_of(p * features + (1 - core) * width, STRIP), width)
        dst_ref[rows, :] = jnp.zeros((width, LANES), BF)
    rest_ref[1 - core, :, pl.ds(0, 3 * width)] = jnp.zeros((features, 3 * width), BF)
    for h in range(2):
        rest_ref[h, apart, out_cols] = jnp.zeros((width, width), BF)
    for copy in loads[:4]:
        copy.wait()
    out_w = jnp.concatenate([ow_ref[0], ow_ref[1]], axis=1)

    @pl.loop(0, length // ROWS)
    def _(i):
        row0 = pl.multiple_of(i * ROWS, ROWS)
        rows = pl.ds(row0, ROWS)
        dg = dot(mid_ref[rows, :], out_w, ((1,), (1,)))
        first = row0 + lax.broadcasted_iota(jnp.int32, (ROWS, width), 0) < split
        pad[pl.ds(row0 + 8, ROWS), pl.ds(0, width)] = dg * conv_ref[rows, :].astype(F32)
        dc = dg * q_ref[rows, :].astype(F32)
        g[0, rows, :] = jnp.where(first, dc, 0.0).astype(BF)
        g[1, rows, :] = jnp.where(first, 0.0, dc).astype(BF)

    scale = 1.0 / half
    for copy in loads[4:7]:
        copy.wait()

    def transform(spans):
        @pl.loop(0, half // BINS)
        def _(i):
            rows = pl.ds(pl.multiple_of(i * 2 * BINS, 2 * BINS), 2 * BINS)
            f = fh_ref[rows, :].astype(F32)
            fr, fi = f[:BINS], f[BINS:]
            er = None
            for m in range(2):
                s = dot(fwd_ref[rows, spans[m]], g[m, spans[m], :])
                sr, si = s[:BINS], s[BINS:]
                prod[m, rows, 0:width] = jnp.concatenate(
                    [(fr * sr + fi * si) * scale, (fr * si - fi * sr) * scale], axis=0
                ).astype(BF)
                w = uh_ref[m, rows, :].astype(F32)
                wr, wi = w[:BINS], w[BINS:]
                tr = wr * sr + wi * si
                ti = wr * si - wi * sr
                er, ei = (tr, ti) if er is None else (er + tr, ei + ti)
            e = jnp.concatenate([er * scale, ei * scale], axis=0).astype(BF)
            for m in range(2):
                prod[m, rows, width : 2 * width] = e

    by_corner(split, length, transform)
    corner = split // ROWS
    value_cols = pl.ds(2 * width, width)
    for copy in loads[7:10]:
        copy.wait()
    kpad[pl.ds(8, length), :] = key_ref[...].astype(F32)

    @pl.loop(0, length // ROWS)
    def _(i):
        row0 = pl.multiple_of(i * ROWS, ROWS)
        rows = pl.ds(row0, ROWS)
        spot = pl.ds(row0 + 8, ROWS)
        pick = (i > corner).astype(jnp.int32)
        both = dot(inv_ref[rows, :], prod[pick])
        pad[spot, value_cols] = both[:, :width]

        @pl.when(i == corner)
        def _():
            later = i * ROWS + lax.broadcasted_iota(jnp.int32, (ROWS, width), 0) >= split
            other = dot(inv_ref[rows, :], prod[1, :, 0:width])
            pad[spot, value_cols] = jnp.where(later, other, pad[spot, value_cols])

        inside = row0 + lax.broadcasted_iota(jnp.int32, (ROWS, width), 0) < half
        epad[spot, :] = jnp.where(inside, both[:, width:], 0.0) * decay_ref[rows, :]

    def key_taps(row0, same):
        spot = pl.ds(row0 + 8, CHUNK)
        for strip in range(strips):
            cols = pl.ds(strip * STRIP, STRIP)
            e = epad[spot, cols]
            pad[spot, pl.ds(width + strip * STRIP, STRIP)] = weigh(shifted(epad, row0, cols, same), cw_ref, 2, cols, True)
            for off, x in enumerate(shifted(kpad, row0, cols, same)):
                dcw_sum[off, :, cols] += (x * e).reshape(CHUNK // 8, 8, STRIP).sum(0)

    for copy in loads[15:]:
        copy.wait()
    cw_ref[...] = ct_ref[...].astype(F32).T
    sw_ref[...] = st_ref[...].astype(F32).T
    over_chunks(length, split, key_taps)
    loads[10].wait()

    @pl.loop(0, 3 * strips)
    def _(strip):
        cols = pl.ds(pl.multiple_of(strip * STRIP, STRIP), STRIP)
        kpad[pl.ds(8, length), pl.ds(0, STRIP)] = br_ref[:, cols].astype(F32)

        def branch_taps(row0, same):
            e = pad[pl.ds(row0 + 8, CHUNK), cols]
            total = weigh(shifted(pad, row0, cols, same), sw_ref, 0, cols, True)
            dbr_ref[pl.ds(row0, CHUNK), cols] = total.astype(BF)
            for off, x in enumerate(shifted(kpad, row0, pl.ds(0, STRIP), same)):
                dsw_sum[off, :, cols] += (x * e).reshape(CHUNK // 8, 8, STRIP).sum(0)

        over_chunks(length, split, branch_taps)

    ch_rows[1:2, :] = dmg_ref[...]
    st_rows[0:5, :] = jnp.sum(dsw_sum[...], axis=1)
    ch_rows[2:7, part] = jnp.sum(dcw_sum[...], axis=1)
    dch_ref[...] = ch_rows[...].T.astype(BF)
    for p in range(3):
        rows = pl.ds(pl.multiple_of(p * features + core * width, STRIP), width)
        dst_ref[rows, :] = st_rows[:, p * width : (p + 1) * width].T.astype(BF)
    for copy in loads[11:15]:
        copy.wait()
    d_out = dot(gated_ref[...], mid_ref[...], ((0,), (0,))).astype(BF)
    for h in range(2):
        rest_ref[h, part, out_cols] = d_out[:, h * width : (h + 1) * width]
    for cols in (pl.ds(0, 2 * width), pl.ds(2 * width, width)):
        d_in = dot(own_ref[...], dbr_ref[near, cols], ((0,), (0,)))
        d_in += dot(other_ref[...], dbr_ref[far, cols], ((0,), (0,)))
        rest_ref[core, :, cols] = d_in.astype(BF)
    dn_ref[...] = dot(dbr_ref[near, :], iw_ref[...], ((1,), (1,))).astype(BF)
    dn_send_ref[...] = dot(dbr_ref[far, :], iw_ref[...], ((1,), (1,))).astype(BF)


def local_call(kernel, args, direct, outs, direct_outs, scratch):
    vmem, anywhere = pl.BlockSpec(memory_space=pltpu.VMEM), pl.BlockSpec(memory_space=pl.ANY)
    return pl.pallas_call(
        kernel,
        out_shape=[jax.ShapeDtypeStruct(shape, dtype) for shape, dtype in outs],
        in_specs=[pl.BlockSpec(memory_space=pltpu.SMEM)]
        + [vmem] * (direct - 1)
        + [anywhere] * (len(args) - direct),
        out_specs=[vmem] * direct_outs + [anywhere] * (len(outs) - direct_outs),
        scratch_shapes=scratch,
        compiler_params=pltpu.CompilerParams(vmem_limit_bytes=VMEM_LIMIT),
    )(*args)


def tap_scratch(width):
    return [((width, LANES), BF), ((3 * width, LANES), BF), ((LANES, width), F32), ((LANES, 3 * width), F32)]


def mixer_forward(layer, split, own, other, ch, st, weight, decay, fwd, inv):
    _, length, width = decay.shape
    features = own.shape[1]
    bins = fwd.shape[0]
    tall, short, wide = (length, width), (own.shape[0], width), (length, 3 * width)
    kept = [(wide, BF), (tall, BF), (tall, BF), (tall, BF), ((bins, width), BF), ((2, bins, width), BF)]
    scratch = [((features, 3 * width), BF), (tall, F32), (fwd.shape, BF), (inv.shape, BF)] + kept + tap_scratch(width)
    scratch += [
        ((length + 16, 3 * width), F32),
        ((length + 16, width), F32),
        (tall, BF),
        ((2,) + tall, BF),
        ((2, bins, width), BF),
    ]
    return local_call(
        functools.partial(mixer_forward_kernel, layer),
        (split, own, other, ch, st, weight, decay, fwd, inv),
        3,
        [(tall, BF), (short, BF), (short, BF)] + kept,
        3,
        [pltpu.VMEM(*x) for x in scratch] + [pltpu.SemaphoreType.DMA((8,)), pltpu.SemaphoreType.DMA((6,))],
    )


def mixer_backward(
    layer, split, mid_own, mid_other, dmg, ch, st, weight, own, other, gated, br, decay, fwd, inv, q, key, conv, fh, uh
):
    _, length, width = decay.shape
    bins = fwd.shape[0]
    rows, features = mid_own.shape
    held = (own, other, gated, br, decay, fwd, inv, q, key, conv, fh, uh)
    scratch = [((2, width, width), BF), ((features, 3 * width), BF)]
    scratch += [(x.shape[1:] if x is decay else x.shape, x.dtype) for x in held] + tap_scratch(width)
    scratch += [
        ((length + 16, 3 * width), F32),
        ((length + 16, width), F32),
        ((length + 16, width), F32),
        ((2, length, width), BF),
        ((2, bins, 2 * width), BF),
        ((length, features), BF),
        ((length, 3 * width), BF),
        ((5, 8, 3 * width), F32),
        ((5, 8, width), F32),
        ((LANES, features), F32),
        ((LANES, 3 * width), F32),
    ]
    return local_call(
        functools.partial(mixer_backward_kernel, layer),
        (split, mid_own, mid_other, dmg, ch, st, weight) + held,
        4,
        [
            ((2, features, 4 * width), BF),
            ((rows, features), BF),
            ((rows, features), BF),
            ((features, LANES), BF),
            ((3 * features, LANES), BF),
        ],
        5,
        [pltpu.VMEM(*x) for x in scratch] + [pltpu.SemaphoreType.DMA((19,))],
    )


def cube(dp_count):
    bits = (dp_count // 2).bit_length() - 1
    core, seq = bits, bits + 1
    low, rest = [bits - 1], list(range(bits - 1))
    orders = (
        rest + [seq] + low, rest + low + [seq], low + [seq] + rest,
        low + rest + [seq], [seq] + rest + low, [seq] + low + rest,
    )
    return bits, core, seq, orders


def place(bits):
    dp, seq = lax.axis_index("dp"), lax.axis_index("seq")
    coords = [(dp // (2 << (bits - 1 - d))) % 2 for d in range(bits)] + [dp % 2, seq]

    def neighbour(d):
        if d == bits + 1:
            return dp, 1 - seq
        step = 1 if d == bits else 2 << (bits - 1 - d)
        return dp + step * (1 - 2 * coords[d]), seq

    return coords, neighbour


def region(fixed, dims):
    return tuple(fixed[d] if d in fixed else slice(None) for d in range(dims))


def across(coords, bits):
    dp = lax.axis_index("dp")
    core, seq = coords[bits], coords[bits + 1]
    return core != seq, (dp + 1 - 2 * core, 1 - seq)


def greet(neighbours):
    barrier = pltpu.get_barrier_semaphore()
    for device in neighbours:
        pl.semaphore_signal(barrier, inc=1, device_id=device, device_id_type=pl.DeviceIdType.MESH)
    pl.semaphore_wait(barrier, len(neighbours))


class Swap:
    def __init__(self, src, dst, send, recv, local, moves, partner):
        self.stays, self.moves = jnp.logical_not(moves), moves
        self.away = pltpu.make_async_remote_copy(
            src_ref=src, dst_ref=dst, send_sem=send, recv_sem=recv,
            device_id=partner, device_id_type=pl.DeviceIdType.MESH,
        )
        self.here = pltpu.make_async_copy(src, dst, local)

    def start(self):
        pl.when(self.moves)(lambda: self.away.start())
        pl.when(self.stays)(lambda: self.here.start())

    def wait(self):
        pl.when(self.moves)(lambda: self.away.wait())
        pl.when(self.stays)(lambda: self.here.wait())


def remote(src, dst, send, recv, device):
    copy = pltpu.make_async_remote_copy(
        src_ref=src, dst_ref=dst, send_sem=send, recv_sem=recv,
        device_id=device, device_id_type=pl.DeviceIdType.MESH,
    )
    copy.start()
    return copy


GATHER_UNITS = (
    (3, 0, 640, 0, 0), (3, 640, 512, 1, 0), (3, 1152, 384, 2, 0), (5, 0, 128, 2, 0), (6, 0, 128, 1, 0),
    (0, 0, 768, 0, 1), (0, 768, 768, 1, 1), (2, 2, 2, 2, 1),
    (0, 1536, 768, 0, 2), (0, 2304, 768, 1, 2),
    (1, 0, 2, 0, 3), (1, 2, 2, 1, 3), (4, 1280, 256, 2, 3),
    (4, 0, 640, 0, 4), (4, 640, 640, 1, 4),
    (2, 0, 1, 0, 5), (2, 1, 1, 1, 5),
)
SCATTER_UNITS = (
    (0, 0, 768, 0, 0), (0, 768, 768, 1, 0), (2, 2, 2, 2, 0),
    (0, 1536, 768, 0, 1), (0, 2304, 768, 1, 1), (3, 1280, 256, 2, 1),
    (1, 0, 2, 0, 2), (1, 2, 2, 1, 2), (4, 1280, 256, 2, 2),
    (3, 0, 640, 0, 3), (3, 640, 640, 1, 3), (5, 0, 128, 2, 3), (6, 0, 128, 2, 3),
    (4, 0, 640, 0, 4), (4, 640, 640, 1, 4), (7, 0, 128, 2, 4),
    (2, 0, 1, 0, 5), (2, 1, 1, 0, 5),
)


def piece_of(unit, slabs):
    span = pl.ds(unit[1], unit[2])
    return (span, slice(None), slice(None)) if slabs else (slice(None), span)


def ticks(units, stages, shrinking):
    steps = [max(2**t, 2 ** (stages - 2)) for t in range(stages)]
    if shrinking:
        steps = steps[::-1]
    spacing = 2**stages // 4
    due = []
    for i, unit in enumerate(units):
        if shrinking:
            due.append((spacing * (unit[4] - 1) - 1, i, -1))
        due += [(spacing * unit[4] + sum(steps[:t]), i, t) for t in range(stages + 1)]
    return [(i, t) for _, i, t in sorted(due)]


def gather_kernel(dp_count, units, rows_in, rows_out, own, full, sems):
    bits, core_dim, _, orders = cube(dp_count)
    dims = bits + 2
    stages = dims - 1
    coords, neighbour = place(bits)
    core = coords[core_dim]
    sibling = neighbour(core_dim)
    moves, partner = across(coords, bits)
    greet([neighbour(d) for d in range(dims)] + [partner])
    ici_send, ici_recv, core_send, core_recv, local, swap_send, swap_recv, swap_local = sems
    swaps = [
        Swap(src, dst, swap_send.at[i], swap_recv.at[i], swap_local.at[i], moves, partner)
        for i, (src, dst) in enumerate(zip(rows_in, rows_out))
    ]
    mine = region(dict(enumerate(coords)), dims)
    firsts, forwards, sends = [], [], []
    last = [None] * len(units)
    for u, unit in enumerate(units):
        array, tail = unit[0], piece_of(unit, len(own[unit[0]].shape) == 4)
        piece = own[array].at[(slice(None),) + tail]
        here = full[array].at[(slice(None),) + mine + tail]
        keep = pltpu.make_async_copy(piece, here, local.at[u])
        keep.start()
        firsts.append((keep, remote(piece, here, core_send.at[u, 0], core_recv.at[u, 0], sibling)))
    for number, (u, t) in enumerate(ticks(units, stages, False)):
        if number == 4:
            for swap in swaps:
                swap.start()
        unit = units[u]
        array, tail, order = unit[0], piece_of(unit, len(own[unit[0]].shape) == 4), orders[unit[3]]
        fixed = {e: coords[e] for e in order[t:]}
        if t == 0:
            firsts[u][0].wait()
            firsts[u][1].wait_recv()
        else:
            last[u].wait_recv()
            got = full[array].at[(core,) + region(fixed | {order[t - 1]: 1 - coords[order[t - 1]]}, dims) + tail]
        if t < stages:
            held = full[array].at[(core,) + region(fixed, dims) + tail]
            last[u] = remote(held, held, ici_send.at[u, t], ici_recv.at[u, t], neighbour(order[t]))
            sends.append(last[u])
        if t > 0:
            forwards.append(remote(got, got, core_send.at[u, t], core_recv.at[u, t], sibling))
    for swap in swaps:
        swap.wait()
    beside = remote(rows_out[0], rows_out[-1], swap_send.at[len(swaps)], swap_recv.at[len(swaps)], sibling)
    for keep, copy in firsts:
        copy.wait_send()
    for copy in forwards:
        copy.wait()
    for copy in sends:
        copy.wait_send()
    beside.wait()


def gather_weights(rows, own, dp_count, number):
    bits = cube(dp_count)[0]
    stages = bits + 1
    units = GATHER_UNITS
    arrays = len(own)
    count = len(units)

    def body(*refs):
        rows_in, refs = refs[: len(rows)], refs[len(rows) :]
        own_refs, refs = refs[:arrays], refs[arrays:]
        rows_out, refs = refs[: len(rows) + 1], refs[len(rows) + 1 :]
        gather_kernel(dp_count, units, rows_in, rows_out, own_refs, refs[:arrays], refs[arrays:])

    grid = (2,) * (bits + 2)
    anywhere = pl.BlockSpec(memory_space=pl.ANY)
    return pl.pallas_call(
        body,
        out_shape=[jax.ShapeDtypeStruct(x.shape, x.dtype) for x in (*rows, rows[0])]
        + [jax.ShapeDtypeStruct(x.shape[:1] + grid + x.shape[1:], x.dtype) for x in own],
        in_specs=[anywhere] * (len(rows) + arrays),
        out_specs=[anywhere] * (len(rows) + 1 + arrays),
        scratch_shapes=[pltpu.SemaphoreType.DMA((count, stages))] * 2
        + [pltpu.SemaphoreType.DMA((count, stages + 1))] * 2
        + [pltpu.SemaphoreType.DMA((count,))]
        + [pltpu.SemaphoreType.DMA((len(rows) + 1,))] * 3,
        compiler_params=pltpu.CompilerParams(collective_id=number, has_side_effects=True),
    )(*rows, *own)


def scatter_kernel(dp_count, units, ends_in, token_ref, grads, outs, held, first, arrived, final, work, sems):
    bits, core_dim, _, orders = cube(dp_count)
    dims = bits + 2
    stages = dims - 1
    coords, neighbour = place(bits)
    core = coords[core_dim]
    sibling = neighbour(core_dim)
    moves, partner = across(coords, bits)
    greet([neighbour(d) for d in range(dims)] + [partner])
    ici_send, ici_recv, core_send, core_recv, local, end_send, end_recv, end_local = sems
    x_ref, dn_ref, away_ref, dmid_ref, gain_ref, dng_ref = ends_in
    other_ref, grad_ref, sum_ref, flat_ref, tall_ref, slab_ref = work
    grads = list(grads) + [slab_ref]
    exchange = remote(away_ref, other_ref, end_send.at[0], end_recv.at[0], sibling)
    begin = pltpu.make_async_copy(dmid_ref, grad_ref, end_local.at[1])
    begin.start()
    swap = Swap(other_ref, token_ref, end_send.at[1], end_recv.at[1], end_local.at[0], moves, partner)

    def finish_rows():
        exchange.wait()
        begin.wait()
        sum_ref[...] = jnp.zeros(sum_ref.shape, F32)
        share = slab_ref.shape[-2]

        @pl.loop(0, x_ref.shape[0] // 128)
        def _(i):
            rows = pl.ds(pl.multiple_of(i * 128, 128), 128)
            d = dn_ref[rows, :].astype(F32) + other_ref[rows, :].astype(F32)
            dx, dg = norm_back(x_ref[rows, :].astype(F32), gain_ref[...], d)
            other_ref[rows, :] = (grad_ref[rows, :] + dx).astype(BF)
            sum_ref[0:1, :] += dg

        swap.start()
        flat_ref[...] = jnp.zeros(flat_ref.shape, F32)
        for layer, row in enumerate((sum_ref, dng_ref)):
            for c in range(tall_ref.shape[0] // LANES):
                cols = slice(c * LANES, (c + 1) * LANES)
                flat_ref[0:1, :] = row[0:1, cols]
                tall_ref[cols, :] = flat_ref[...].T
            for i in range(2**dims):
                at = tuple((i >> (dims - 1 - d)) % 2 for d in range(dims))
                slab_ref[(layer,) + at] = tall_ref[i * share : (i + 1) * share, :].astype(BF)

    everything = region({}, dims)

    def add(u, fixed, extra):
        free = [d for d in range(dims) if d not in fixed]

        @pl.loop(0, 2 ** len(free))
        def _(i):
            at = {d: (i // 2 ** (len(free) - 1 - j)) % 2 for j, d in enumerate(free)}
            index = tuple(at[d] if d in at else fixed[d] for d in range(dims))
            held[u][index] += extra[tuple(at[d] for d in free)]

    starts, sends = [None] * len(units), []
    last = [None] * len(units)
    for u, t in ticks(units, stages, True):
        if t < 0 and units[u][0] == len(grads) - 1:
            finish_rows()
        if t < 0:
            array, tail = units[u][0], piece_of(units[u], len(outs[units[u][0]].shape) == 4)
            load = pltpu.make_async_copy(grads[array].at[(core,) + everything + tail], held[u], local.at[u, 0])
            load.start()
            other = grads[array].at[(1 - core,) + everything + tail]
            starts[u] = (load, remote(other, first[u], core_send.at[u, 0], core_recv.at[u, 0], sibling))
            continue
        order = orders[units[u][3]][::-1]
        fixed = {d: coords[d] for d in order[:t]}
        if t == 0:
            starts[u][0].wait()
            starts[u][1].wait_recv()
            add(u, fixed, first[u])
        else:
            last[u].wait_recv()
            add(u, fixed, arrived[u][t - 1])
        if t < stages:
            away = held[u].at[region(fixed | {order[t]: 1 - coords[order[t]]}, dims)]
            last[u] = remote(away, arrived[u][t], ici_send.at[u, t], ici_recv.at[u, t], neighbour(order[t]))
            sends.append(last[u])
        else:
            away = held[u].at[region(fixed | {core_dim: 1 - core}, dims)]
            last[u] = remote(away, final[u], core_send.at[u, 1], core_recv.at[u, 1], sibling)
    ends = []
    mine = region(dict(enumerate(coords)), dims)
    for u, unit in enumerate(units):
        array, tail = unit[0], piece_of(unit, len(outs[unit[0]].shape) == 4)
        own = pltpu.make_async_copy(held[u].at[mine], outs[array].at[(core,) + tail], local.at[u, 1])
        own.start()
        last[u].wait_recv()
        other = pltpu.make_async_copy(final[u], outs[array].at[(1 - core,) + tail], local.at[u, 2])
        other.start()
        ends += [own, other]
    swap.wait()
    for copy in ends:
        copy.wait()
    for copy in sends + last + [s[1] for s in starts]:
        copy.wait_send()


def scatter_grads(ends, grads, units, dp_count, number):
    bits = cube(dp_count)[0]
    dims = bits + 2
    stages = dims - 1
    count = len(units)
    grid = (2,) * dims
    rows, features = ends[0].shape
    share = grads[0].shape[1 + dims]
    tails = [x.shape[1 + dims :] for x in grads] + [(share, LANES)]
    arrays = len(tails)
    slabs = []
    for array, _, size, _, _ in units:
        shape = tails[array]
        slabs.append((size,) + shape[1:] if len(shape) == 3 else shape[:-1] + (size,))
    work = [((rows, features), BF), ((rows, features), F32), ((8, features), F32), ((LANES, LANES), F32)]
    work += [((features, LANES), F32), ((2,) + grid + (share, LANES), BF)]

    def body(*refs):
        ends_in, refs = refs[: len(ends)], refs[len(ends) :]
        grads_in, refs = refs[: len(grads)], refs[len(grads) :]
        token, outs, refs = refs[0], refs[1 : 1 + arrays], refs[1 + arrays :]
        held, first, final = refs[:count], refs[count : 2 * count], refs[2 * count : 3 * count]
        refs = refs[3 * count :]
        arrived = [refs[u * stages : (u + 1) * stages] for u in range(count)]
        refs = refs[count * stages :]
        scatter_kernel(
            dp_count, units, ends_in, token, grads_in, outs, held, first, arrived, final,
            refs[: len(work)], refs[len(work) :],
        )

    anywhere, vmem = pl.BlockSpec(memory_space=pl.ANY), pl.BlockSpec(memory_space=pltpu.VMEM)
    return pl.pallas_call(
        body,
        out_shape=[jax.ShapeDtypeStruct((rows, features), BF)]
        + [jax.ShapeDtypeStruct((2,) + tail, BF) for tail in tails],
        in_specs=[vmem, vmem, anywhere, anywhere, vmem, vmem] + [anywhere] * len(grads),
        out_specs=[anywhere] * (1 + arrays),
        scratch_shapes=[pltpu.VMEM(grid + slab, BF) for slab in slabs] * 2
        + [pltpu.VMEM(slab, BF) for slab in slabs]
        + [pltpu.VMEM((2,) * (dims - 1 - t) + slab, BF) for slab in slabs for t in range(stages)]
        + [pltpu.VMEM(*x) for x in work]
        + [pltpu.SemaphoreType.DMA((count, stages))] * 2
        + [pltpu.SemaphoreType.DMA((count, 2))] * 2
        + [pltpu.SemaphoreType.DMA((count, 3))]
        + [pltpu.SemaphoreType.DMA((2,))] * 2
        + [pltpu.SemaphoreType.DMA((2,))],
        compiler_params=pltpu.CompilerParams(
            collective_id=number, has_side_effects=True, vmem_limit_bytes=VMEM_LIMIT
        ),
    )(*ends, *grads)


def norm_parts(x):
    center = x - jnp.mean(x, axis=-1, keepdims=True)
    r = lax.rsqrt(jnp.mean(center * center, axis=-1, keepdims=True) + EPS)
    return center * r, r


def norm_back(x, gain, d):
    xhat, r = norm_parts(x)
    h = d * gain
    dx = r * (h - jnp.mean(h, axis=-1, keepdims=True) - xhat * jnp.mean(h * xhat, axis=-1, keepdims=True))
    return dx, jnp.sum(d * xhat, axis=0, keepdims=True)


SLOPE = math.sqrt(2.0 / math.pi)
CUBE = 0.044715


def gelu_parts(x):
    square = x * x
    t = jnp.tanh(SLOPE * (x + CUBE * square * x))
    flat = 0.5 + 0.5 * t
    return x * flat, flat + 0.5 * x * (1.0 - t * t) * (SLOPE + 3.0 * SLOPE * CUBE * square)


def mlp_forward_kernel(
    gain, next_gain, x_ref, g0_ref, g1_ref, o0_ref, o1_ref, gains_ref, wg_ref, wu_ref, d0_ref, d1_ref,
    mid_ref, hm_ref, pre_ref, out_ref, next_ref,
):
    j = pl.program_id(0)

    @pl.when(j == 0)
    def _():
        width = g0_ref.shape[1]
        mid = x_ref[...]
        core = lax.axis_index("dp") % 2
        for ref, side in ((g0_ref, core), (g1_ref, 1 - core)):
            rows = pl.ds(pl.multiple_of(side * width, STRIP), width)
            mid += dot(ref[...], jnp.concatenate([o0_ref[rows, :], o1_ref[rows, :]], axis=1))
        mid_ref[...] = mid
        out_ref[...] = mid
        hm_ref[...] = (norm_parts(mid)[0] * gains_ref[gain : gain + 1, :]).astype(BF)

    hm = hm_ref[...]
    total = out_ref[...]
    for i in range(TILE // PART_F):
        part = slice(i * PART_F, (i + 1) * PART_F)
        gate = dot(hm, wg_ref[:, part])
        up = dot(hm, wu_ref[:, part])
        pre_ref[0, :, part] = gate.astype(BF)
        pre_ref[1, :, part] = up.astype(BF)
        hid = (gelu_parts(gate)[0] * up).astype(BF)
        total += dot(hid, jnp.concatenate([d0_ref[part, :], d1_ref[part, :]], axis=1))
    out_ref[...] = total

    @pl.when(j == pl.num_programs(0) - 1)
    def _():
        next_ref[...] = (norm_parts(out_ref[...])[0] * gains_ref[next_gain : next_gain + 1, :]).astype(BF)


def mlp_backward_kernel(
    gain, g_ref, hm_ref, mid_ref, gains_ref, pre_ref, wg_ref, wu_ref, d0_ref, d1_ref,
    dgu_ref, ddn_ref, dmid_ref, mlow_ref, dmg_ref,
    glow, hm_t, acc,
):
    j = pl.program_id(0)
    width = d0_ref.shape[1]

    @pl.when(j == 0)
    def _():
        glow[...] = g_ref[...].astype(BF)
        hm_t[...] = hm_ref[...].T
        acc[...] = jnp.zeros(acc.shape, F32)

    low, hm = glow[...], hm_t[...]
    total = acc[...]
    for i in range(TILE // PART_B):
        part = slice(i * PART_B, (i + 1) * PART_B)
        dh = dot(low, jnp.concatenate([d0_ref[part, :], d1_ref[part, :]], axis=1), ((1,), (1,)))
        value, slope = gelu_parts(pre_ref[0, :, part].astype(F32))
        up = pre_ref[1, :, part].astype(F32)
        hid = (value * up).astype(BF)
        d_gate = (dh * up * slope).astype(BF)
        d_up = (dh * value).astype(BF)
        d_down = dot(hid, low, ((0,), (0,))).astype(BF)
        ddn_ref[0, part, :] = d_down[:, :width]
        ddn_ref[1, part, :] = d_down[:, width:]
        for h, d in enumerate((d_gate, d_up)):
            grad = dot(hm, d).astype(BF)
            if len(dgu_ref.shape) == 3:
                dgu_ref[h, :, part] = grad
            else:
                dgu_ref[:, h * TILE + i * PART_B : h * TILE + (i + 1) * PART_B] = grad
        total += dot(d_gate, wg_ref[:, part], ((1,), (1,))) + dot(d_up, wu_ref[:, part], ((1,), (1,)))
    acc[...] = total

    @pl.when(j == pl.num_programs(0) - 1)
    def _():
        dx, dg = norm_back(mid_ref[...], gains_ref[gain : gain + 1, :], acc[...])
        dmid = g_ref[...] + dx
        dmid_ref[...] = dmid
        mlow_ref[...] = dmid.astype(BF)
        dmg_ref[...] = dg


TILE = 512
PART_F = 512
PART_B = 512


def whole(shape):
    return pl.BlockSpec(shape, lambda j: (0,) * len(shape))


def weight_specs(layout, hidden, features):
    steps = hidden // TILE
    gate_up = pl.BlockSpec((features, TILE), lambda j: (0, j))
    up = pl.BlockSpec((features, TILE), lambda j: (1, j) if layout == "halves" else (0, steps + j))
    down = [
        pl.BlockSpec((TILE, features // 2), lambda j: (j, 0)),
        pl.BlockSpec((TILE, features // 2), lambda j: (steps + j, 0)),
    ]
    return [gate_up, up] + down


def mlp_forward(x, g0, g1, weight, gains, gain, next_gain, weights):
    layout, gu, dn = weights
    rows, features = x.shape
    hidden = dn.shape[0] // 2
    square = whole((rows, features))
    narrow = [whole(a.shape) for a in (g0, g1)]
    narrow += [pl.BlockSpec((features, features // 2), lambda j, h=h: (h, 3)) for h in range(2)]
    shapes = [((rows, features), F32), ((rows, features), BF), ((2, rows, hidden), BF), ((rows, features), F32), ((rows, features), BF)]
    return pl.pallas_call(
        functools.partial(mlp_forward_kernel, gain, next_gain),
        grid=(hidden // TILE,),
        out_shape=[jax.ShapeDtypeStruct(*s) for s in shapes],
        in_specs=[square] + narrow + [whole(gains.shape)] + weight_specs(layout, hidden, features),
        out_specs=[square, square, pl.BlockSpec((2, rows, TILE), lambda j: (0, 0, j)), square, square],
        compiler_params=pltpu.CompilerParams(vmem_limit_bytes=VMEM_LIMIT),
    )(x, g0, g1, weight, weight, gains, gu, gu, dn, dn)


def mlp_backward(g, hm, mid, gains, gain, pre, weights, side_by_side):
    layout, gu, dn = weights
    rows, features = g.shape
    hidden = pre.shape[2]
    width = features // 2
    square, vector = whole((rows, features)), whole((1, features))
    both = (features, 2 * hidden) if side_by_side else (2, features, hidden)
    shapes = [(both, BF), ((2, hidden, width), BF), ((rows, features), F32), ((rows, features), BF), ((1, features), F32)]
    return pl.pallas_call(
        functools.partial(mlp_backward_kernel, gain),
        grid=(hidden // TILE,),
        out_shape=[jax.ShapeDtypeStruct(*s) for s in shapes],
        in_specs=[square] * 3
        + [whole(gains.shape), pl.BlockSpec((2, rows, TILE), lambda j: (0, 0, j))]
        + weight_specs(layout, hidden, features),
        out_specs=[
            pl.BlockSpec((features, 2 * TILE), lambda j: (0, j))
            if side_by_side
            else pl.BlockSpec((2, features, TILE), lambda j: (0, 0, j)),
            pl.BlockSpec((2, TILE, width), lambda j: (0, j, 0)),
            square, square, vector,
        ],
        scratch_shapes=[pltpu.VMEM((rows, features), BF), pltpu.VMEM((features, rows), BF), pltpu.VMEM((rows, features), F32)],
        compiler_params=pltpu.CompilerParams(vmem_limit_bytes=VMEM_LIMIT),
    )(g, hm, mid, gains, pre, gu, gu, dn, dn)


def shards(
    tokens, split_points, cotangent, norm_gain, in_weight, short_taps, cond_taps,
    out_weight, mlp_gain, gate_up, down_weight,
):
    rows, features = tokens.shape[1:]
    dp_count, seq_count = lax.axis_size("dp"), lax.axis_size("seq")
    devices = dp_count * seq_count
    length = rows * seq_count
    width = features // 2
    layers = in_weight.shape[0]
    share = norm_gain.shape[1]
    hidden = down_weight.shape[1] * devices
    core = lax.axis_index("dp") % 2
    seq = lax.axis_index("seq")

    swap = [(4 * k + a, 4 * k + 3 - a) for k in range(devices // 4) for a in (1, 2)]
    flip = [(i, i ^ 1) for i in range(dp_count)]

    def swap_rows(x):
        return jnp.where(core == seq, x, lax.ppermute(x, AXES, swap))

    def sibling(x):
        return lax.ppermute(x, "dp", flip)

    def beside(own, other, axis):
        return jnp.where(
            core == 0,
            jnp.concatenate([own, other], axis=axis),
            jnp.concatenate([other, own], axis=axis),
        )

    def half_of(x, which, axis):
        size = x.shape[axis] // 2
        return lax.dynamic_slice_in_dim(x, which * size, size, axis)

    table = transform_matrix(length)
    fwd = jnp.asarray(table, BF)
    inv = jnp.asarray(np.ascontiguousarray(table.T), BF)
    decay = jnp.asarray(decay_table(length, features))

    def halves(x):
        parts = x.shape[-1] // features
        x = x.reshape(x.shape[:-1] + (parts, 2, width))
        x = jnp.moveaxis(x, -2, 0)
        return x.reshape(x.shape[:-2] + (parts * width,))

    grid = (2,) * (cube(dp_count)[0] + 2)

    ch = jnp.concatenate([norm_gain[:, :, None], mlp_gain[:, :, None], cond_taps.transpose(0, 2, 1)], axis=2)
    ch = jnp.pad(ch, ((0, 0), (0, 0), (0, LANES - 7)))
    st = jnp.pad(short_taps.transpose(0, 2, 1), ((0, 0), (0, 0), (0, LANES - 5)))
    own = [gate_up[0].reshape(share, 2, hidden).transpose(1, 0, 2)]
    own += [halves(down_weight[layer]).reshape(2, hidden // features, share, width) for layer in range(layers)]
    for layer in range(layers):
        own.append(jnp.concatenate([halves(in_weight[layer]), halves(out_weight[layer])], axis=2))
    place_rows = [tokens[0], jnp.broadcast_to(split_points, (8, LANES))]
    x_low, split, x_far, *full = gather_weights(place_rows, own + [ch, st], dp_count, 0)
    downs = [x.reshape(2 * hidden, width) for x in full[1 : 1 + layers]]
    mixer_w = [x.reshape(2, features, 4 * width) for x in full[1 + layers : 1 + 2 * layers]]
    ch, st = full[-2].reshape(layers, features, LANES), full[-1].reshape(layers, 3 * features, LANES)
    late, _ = lax.optimization_barrier((gate_up[1:], full[0]))
    gate_ups = [("halves", full[0].reshape(2 * features, hidden))]
    gate_ups += [("plain", lax.all_gather(x, AXES, axis=0, tiled=True)) for x in late]
    gains = ch[:, :, :2].astype(F32).transpose(0, 2, 1).reshape(2 * layers, features)
    stream, far = x_low.astype(F32), x_far.astype(F32)
    arrived, _ = lax.optimization_barrier((cotangent, gate_ups[-1][1]))
    grad = swap_rows(arrived)[0].astype(F32)
    normed, normed_far = [(norm_parts(x)[0] * gains[0]).astype(BF) for x in (stream, far)]
    kept = []
    for layer in range(layers):
        if layer > 0:
            normed_far = sibling(normed)
        gated, mine, away, branches, q, key, conv, fh, uh = mixer_forward(
            layer, split, normed, normed_far, ch, st, mixer_w[layer], decay, fwd, inv
        )
        middle, normed_mlp, pre, out, normed_next = mlp_forward(
            stream, mine, sibling(away), mixer_w[layer].reshape(2 * features, -1), gains,
            2 * layer + 1, (2 * layer + 2) % (2 * layers), gate_ups[layer] + (downs[layer],),
        )
        kept.append((stream, normed, normed_far, gated, branches, q, key, conv, fh, uh, middle, normed_mlp, pre))
        stream, normed = out, normed_next
    activations = swap_rows(stream.astype(BF)[None])

    summed = []
    early = [None] * layers
    for layer in reversed(range(layers)):
        x, normed, normed_far, gated, branches, q, key, conv, fh, uh, middle, normed_mlp, pre = kept[layer]
        d_gu, d_down, d_middle, m_low, d_mg = mlp_backward(
            grad, normed_mlp, middle, gains, 2 * layer + 1, pre, gate_ups[layer] + (downs[layer],), layer > 0
        )
        rest, d_normed, d_away, d_ch, d_st = mixer_backward(
            layer, split, m_low, sibling(m_low), d_mg, ch, st, mixer_w[layer], normed, normed_far, gated, branches,
            decay, fwd, inv, q, key, conv, fh, uh,
        )
        if layer > 0:
            early[layer] = lax.psum_scatter(d_gu, AXES, scatter_dimension=0, tiled=True)
            d_part, d_ng = norm_back(x, gains[2 * layer], d_normed.astype(F32) + sibling(d_away).astype(F32))
            grad = d_middle + d_part
        summed.append((d_gu, d_down, rest, d_ch, d_st))
    d_gus, d_downs, rests, *smalls = zip(*summed[::-1])
    pieces = [d_gus[0].reshape((2,) + grid + (share, hidden))]
    pieces += [x.reshape((2,) + grid + (hidden // features, share, width)) for x in d_downs]
    pieces += [x.reshape((2,) + grid + (share, 4 * width)) for x in rests]
    pieces += [jnp.stack(x).reshape((2,) + grid + (-1, LANES)) for x in smalls]
    ends = [x_low, d_normed, d_away, d_middle, gains[:1], d_ng]
    fits = share % 8 == 0
    units = tuple(unit for unit in SCATTER_UNITS if fits or unit[0] != 2)
    token_grad, *outs = scatter_grads(ends, pieces, units, dp_count, 1)
    if not fits:
        outs[2] = lax.psum_scatter(d_downs[1], AXES, scatter_dimension=1, tiled=True)
    token_grad = token_grad[None].astype(F32)

    def joined(x):
        parts = x.shape[-1] // width
        x = jnp.moveaxis(x.reshape(x.shape[:-1] + (parts, width)), 0, -2)
        return x.reshape(x.shape[:-3] + (parts * features,))

    early[0] = outs[0].transpose(1, 0, 2)
    for layer in range(1, layers):
        early[layer] = early[layer].reshape(share, hidden // TILE, 2, TILE).transpose(0, 2, 1, 3)
    g_gu = jnp.stack([x.reshape(share, 2 * hidden) for x in early]).astype(F32)
    g_down = jnp.stack([joined(x.reshape(2, -1, width)) for x in outs[1 : 1 + layers]]).astype(F32)
    rest = outs[1 + layers : 1 + 2 * layers]
    g_in = jnp.stack([joined(x[:, :, : 3 * width]) for x in rest]).astype(F32)
    g_out = jnp.stack([joined(x[:, :, 3 * width :]) for x in rest]).astype(F32)
    s_ch, s_st, s_ng = [x.astype(F32) for x in outs[1 + 2 * layers :]]
    g_ng, g_mg, g_ct, g_st = s_ng[:, :, 0], s_ch[:, :, 1], s_ch[:, :, 2:7].transpose(0, 2, 1), s_st[:, :, :5].transpose(0, 2, 1)
    return (
        activations,
        token_grad,
        g_ng,
        g_in,
        g_st,
        g_ct,
        g_out,
        g_mg,
        g_gu,
        g_down,
    )


def solution(mesh):
    every = ("dp", "seq")
    rows, part = P("dp", "seq", None), P(None, every, None)
    vector, taps = P(None, every), P(None, None, every)
    return jax.shard_map(
        shards,
        mesh=mesh,
        in_specs=(rows, P("dp"), rows, vector, part, taps, taps, part, vector, part, part),
        out_specs=(rows, rows, vector, part, taps, taps, part, vector, part, part),
        check_vma=False,
    )
```

```python
import functools
import math

import numpy as np
import jax
import jax.numpy as jnp
from jax import lax
from jax.experimental import pallas as pl
from jax.experimental.pallas import tpu as pltpu
from jax.sharding import PartitionSpec as P

BF = jnp.bfloat16
F32 = jnp.float32
EPS = 1e-05
AXES = ("dp", "seq")
GAP = 128
VMEM_LIMIT = 60 * 2**20
STRIP = 128
LANES = 128
BINS = 224
ROWS = 256
CHUNK = 128


def transform_matrix(length):
    half = length - GAP
    freq = np.arange(half)[:, None]
    place = np.arange(length)[None, :]
    angle = ((2 * freq + 1) * place % (4 * half)).astype(np.float64) * (math.pi / (2 * half))
    both = np.stack([np.cos(angle), -np.sin(angle)])
    both = both.reshape(2, half // BINS, BINS, length).transpose(1, 0, 2, 3)
    return both.reshape(2 * half, length).astype(np.float32)


def decay_table(length, features):
    positions = np.arange(length)
    rates = np.exp(math.log(1.0 / length) + np.arange(features) / (features - 1) * math.log(4.0))
    scales = np.sum(np.exp(-2.0 * positions[:, None] * rates[None, :]), axis=0) ** -0.5
    table = np.exp(-positions[:, None] * rates[None, :]) * scales[None, :]
    return np.stack(np.split(table, 2, axis=1)).astype(np.float32)


def dot(a, b, dims=((1,), (0,))):
    return lax.dot_general(a, b, (dims, ((), ())), preferred_element_type=F32)


def tap_same(row0, split):
    t = row0 + lax.broadcasted_iota(jnp.int32, (CHUNK, STRIP), 0)
    here = t >= split
    return [
        None if off == 2 else jnp.where(((t + (off - 2)) >= split) == here, 1.0, 0.0)
        for off in range(5)
    ]


def shifted(ref, row0, cols, same):
    block = ref[pl.ds(row0, CHUNK + 16), cols]
    out = []
    for off in range(5):
        turned = pltpu.roll(block, (2 - off) % (CHUNK + 16), 0) if off != 2 else block
        rows = turned[8 : 8 + CHUNK]
        out.append(rows if same[off] is None else rows * same[off])
    return out


def over_chunks(length, split, body):
    @pl.loop(0, length // CHUNK)
    def _(i):
        row0 = pl.multiple_of(i * CHUNK, CHUNK)
        touched = (split > row0 - 2) & (split < row0 + CHUNK + 2)

        @pl.when(touched)
        def _():
            body(row0, tap_same(row0, split))

        @pl.when(jnp.logical_not(touched))
        def _():
            body(row0, [None] * 5)


def tap_loads(layer, core, ch_hbm, st_hbm, ct_ref, st_ref):
    width = ct_ref.shape[0]
    own = pl.multiple_of(core * width, STRIP)
    pairs = [(ch_hbm.at[layer, pl.ds(own, width), :], ct_ref)]
    for part in range(3):
        rows = pl.ds(pl.multiple_of(part * 2 * width + own, STRIP), width)
        pairs.append((st_hbm.at[layer, rows, :], st_ref.at[pl.ds(part * width, width), :]))
    return pairs


def weigh(rows, w_ref, base, cols, flip):
    total = None
    for off, x in enumerate(rows):
        tap = base + (4 - off if flip else off)
        term = x * w_ref[tap : tap + 1, cols]
        total = term if total is None else total + term
    return total


def by_corner(split, length, body):
    for corner in range(length // ROWS):
        spans = (slice(0, (corner + 1) * ROWS), slice(corner * ROWS, length))
        pl.when(split // ROWS == corner)(functools.partial(body, spans))


def clear_ends(ref, length):
    ref[0:8, :] = jnp.zeros((8, ref.shape[1]), F32)
    ref[8 + length : 16 + length, :] = jnp.zeros((8, ref.shape[1]), F32)


def fetch(pairs, sems):
    copies = [pltpu.make_async_copy(src, dst, sems.at[i]) for i, (src, dst) in enumerate(pairs)]
    for copy in copies:
        copy.start()
    return copies


def mixer_forward_kernel(
    layer, split_ref, own_ref, other_ref, ch_hbm, st_hbm, iw_hbm, decay_hbm, fwd_hbm, inv_hbm,
    gated_ref, mine_ref, send_ref, br_hbm, q_hbm, key_hbm, conv_hbm, fh_hbm, uh_hbm,
    iw_ref, decay_ref, fwd_ref, inv_ref, br_ref, q_ref, key_ref, conv_ref, fh_ref, uh_ref,
    ct_ref, st_ref, cw_ref, sw_ref, pad, kpad, filt, u, prod, in_sems, out_sems,
):
    length, width = q_ref.shape
    rows_own = own_ref.shape[0]
    half = length - GAP
    split, core = split_ref[0, 0], lax.axis_index("dp") % 2
    strips = width // STRIP
    loads = fetch(
        [
            (iw_hbm.at[core, :, pl.ds(0, 3 * width)], iw_ref),
            (decay_hbm.at[core], decay_ref),
            (fwd_hbm, fwd_ref),
            (inv_hbm, inv_ref),
        ]
        + tap_loads(layer, core, ch_hbm, st_hbm, ct_ref, st_ref),
        in_sems,
    )
    outs = [(br_ref, br_hbm), (q_ref, q_hbm), (key_ref, key_hbm), (fh_ref, fh_hbm), (uh_ref, uh_hbm), (conv_ref, conv_hbm)]
    stores = [pltpu.make_async_copy(src, dst, out_sems.at[i]) for i, (src, dst) in enumerate(outs)]
    clear_ends(pad, length)
    clear_ends(kpad, length)
    loads[0].wait()
    for ref, side in ((own_ref, core), (other_ref, 1 - core)):

        @pl.loop(0, rows_own // ROWS)
        def _(i):
            row0 = pl.multiple_of(side * rows_own + i * ROWS, ROWS)
            low = dot(ref[pl.ds(pl.multiple_of(i * ROWS, ROWS), ROWS), :], iw_ref[...]).astype(BF)
            br_ref[pl.ds(row0, ROWS), :] = low
            pad[pl.ds(row0 + 8, ROWS), :] = low.astype(F32)

    stores[0].start()
    for copy in loads[4:]:
        copy.wait()
    cw_ref[...] = ct_ref[...].astype(F32).T
    sw_ref[...] = st_ref[...].astype(F32).T

    def mix(row0, same):
        rows = pl.ds(row0, CHUNK)
        first = row0 + lax.broadcasted_iota(jnp.int32, (CHUNK, STRIP), 0) < split
        for part in range(3):
            for strip in range(strips):
                cols = pl.ds(part * width + strip * STRIP, STRIP)
                own = pl.ds(strip * STRIP, STRIP)
                low = weigh(shifted(pad, row0, cols, same), sw_ref, 0, cols, False).astype(BF)
                if part == 0:
                    q_ref[rows, own] = low
                elif part == 1:
                    key_ref[rows, own] = low
                    kpad[pl.ds(row0 + 8, CHUNK), own] = low.astype(F32)
                else:
                    low = low.astype(F32)
                    u[0, rows, own] = jnp.where(first, low, 0.0).astype(BF)
                    u[1, rows, own] = jnp.where(first, 0.0, low).astype(BF)

    over_chunks(length, split, mix)
    stores[1].start()
    stores[2].start()
    loads[1].wait()

    def make_filter(row0, same):
        rows = pl.ds(row0, CHUNK)
        for strip in range(strips):
            cols = pl.ds(strip * STRIP, STRIP)
            total = weigh(shifted(kpad, row0, cols, same), cw_ref, 2, cols, False)
            filt[rows, cols] = (total * decay_ref[rows, cols]).astype(BF)

    over_chunks(length, split, make_filter)
    scale = 1.0 / half
    loads[2].wait()

    def transform(spans):
        @pl.loop(0, half // BINS)
        def _(i):
            rows = pl.ds(pl.multiple_of(i * 2 * BINS, 2 * BINS), 2 * BINS)
            f = dot(fwd_ref[rows, 0:half], filt[0:half, :])
            fr, fi = f[:BINS], f[BINS:]
            fh_ref[rows, :] = f.astype(BF)
            for m in range(2):
                s = dot(fwd_ref[rows, spans[m]], u[m, spans[m], :])
                uh_ref[m, rows, :] = s.astype(BF)
                sr, si = s[:BINS], s[BINS:]
                prod[m, rows, :] = jnp.concatenate(
                    [(fr * sr - fi * si) * scale, (fr * si + fi * sr) * scale], axis=0
                ).astype(BF)

    by_corner(split, length, transform)
    stores[3].start()
    stores[4].start()
    corner = split // ROWS
    loads[3].wait()

    @pl.loop(0, length // ROWS)
    def _(i):
        rows = pl.ds(pl.multiple_of(i * ROWS, ROWS), ROWS)
        pick = (i > corner).astype(jnp.int32)
        conv_ref[rows, :] = dot(inv_ref[rows, :], prod[pick]).astype(BF)

        @pl.when(i == corner)
        def _():
            later = i * ROWS + lax.broadcasted_iota(jnp.int32, (ROWS, width), 0) >= split
            other = dot(inv_ref[rows, :], prod[1])
            conv_ref[rows, :] = jnp.where(later, other, conv_ref[rows, :].astype(F32)).astype(BF)

        gated_ref[rows, :] = (q_ref[rows, :].astype(F32) * conv_ref[rows, :].astype(F32)).astype(BF)

    stores[5].start()
    mine_ref[...] = gated_ref[pl.ds(pl.multiple_of(core * rows_own, ROWS), rows_own), :]
    send_ref[...] = gated_ref[pl.ds(pl.multiple_of((1 - core) * rows_own, ROWS), rows_own), :]
    for copy in stores:
        copy.wait()


def mixer_backward_kernel(
    layer, split_ref, mid_own_ref, mid_other_ref, dmg_ref, ch_hbm, st_hbm,
    w_hbm, own_hbm, other_hbm, gated_hbm, br_hbm, decay_hbm, fwd_hbm, inv_hbm, q_hbm, key_hbm, conv_hbm, fh_hbm, uh_hbm,
    rest_ref, dn_ref, dn_send_ref, dch_ref, dst_ref,
    ow_ref, iw_ref, own_ref, other_ref, gated_ref, br_ref, decay_ref, fwd_ref, inv_ref, q_ref, key_ref, conv_ref, fh_ref,
    uh_ref, ct_ref, st_ref, cw_ref, sw_ref, pad, epad, kpad, g, prod, mid_ref, dbr_ref, dsw_sum, dcw_sum, ch_rows, st_rows,
    in_sems,
):
    length, width = q_ref.shape
    rows_own, features = own_ref.shape
    half = length - GAP
    split, core = split_ref[0, 0], lax.axis_index("dp") % 2
    strips = width // STRIP
    part = pl.ds(pl.multiple_of(core * width, STRIP), width)
    apart = pl.ds(pl.multiple_of((1 - core) * width, STRIP), width)
    near = pl.ds(pl.multiple_of(core * rows_own, ROWS), rows_own)
    far = pl.ds(pl.multiple_of((1 - core) * rows_own, ROWS), rows_own)
    out_cols = pl.ds(3 * width, width)
    loads = fetch(
        [
            (w_hbm.at[0, part, out_cols], ow_ref.at[0]),
            (w_hbm.at[1, part, out_cols], ow_ref.at[1]),
            (conv_hbm, conv_ref),
            (q_hbm, q_ref),
            (fwd_hbm, fwd_ref),
            (fh_hbm, fh_ref),
            (uh_hbm, uh_ref),
            (inv_hbm, inv_ref),
            (decay_hbm.at[core], decay_ref),
            (key_hbm, key_ref),
            (br_hbm, br_ref),
            (gated_hbm, gated_ref),
            (own_hbm, own_ref),
            (other_hbm, other_ref),
            (w_hbm.at[core, :, pl.ds(0, 3 * width)], iw_ref),
        ]
        + tap_loads(layer, core, ch_hbm, st_hbm, ct_ref, st_ref),
        in_sems,
    )
    mid_ref[near, :] = mid_own_ref[...]
    mid_ref[far, :] = mid_other_ref[...]
    clear_ends(pad, length)
    clear_ends(epad, length)
    clear_ends(kpad, length)
    dsw_sum[...] = jnp.zeros(dsw_sum.shape, F32)
    dcw_sum[...] = jnp.zeros(dcw_sum.shape, F32)
    ch_rows[...] = jnp.zeros(ch_rows.shape, F32)
    st_rows[...] = jnp.zeros(st_rows.shape, F32)
    for p in range(3):
        rows = pl.ds(pl.multiple_of(p * features + (1 - core) * width, STRIP), width)
        dst_ref[rows, :] = jnp.zeros((width, LANES), BF)
    rest_ref[1 - core, :, pl.ds(0, 3 * width)] = jnp.zeros((features, 3 * width), BF)
    for h in range(2):
        rest_ref[h, apart, out_cols] = jnp.zeros((width, width), BF)
    for copy in loads[:4]:
        copy.wait()
    out_w = jnp.concatenate([ow_ref[0], ow_ref[1]], axis=1)

    @pl.loop(0, length // ROWS)
    def _(i):
        row0 = pl.multiple_of(i * ROWS, ROWS)
        rows = pl.ds(row0, ROWS)
        dg = dot(mid_ref[rows, :], out_w, ((1,), (1,)))
        first = row0 + lax.broadcasted_iota(jnp.int32, (ROWS, width), 0) < split
        pad[pl.ds(row0 + 8, ROWS), pl.ds(0, width)] = dg * conv_ref[rows, :].astype(F32)
        dc = dg * q_ref[rows, :].astype(F32)
        g[0, rows, :] = jnp.where(first, dc, 0.0).astype(BF)
        g[1, rows, :] = jnp.where(first, 0.0, dc).astype(BF)

    scale = 1.0 / half
    for copy in loads[4:7]:
        copy.wait()

    def transform(spans):
        @pl.loop(0, half // BINS)
        def _(i):
            rows = pl.ds(pl.multiple_of(i * 2 * BINS, 2 * BINS), 2 * BINS)
            f = fh_ref[rows, :].astype(F32)
            fr, fi = f[:BINS], f[BINS:]
            er = None
            for m in range(2):
                s = dot(fwd_ref[rows, spans[m]], g[m, spans[m], :])
                sr, si = s[:BINS], s[BINS:]
                prod[m, rows, 0:width] = jnp.concatenate(
                    [(fr * sr + fi * si) * scale, (fr * si - fi * sr) * scale], axis=0
                ).astype(BF)
                w = uh_ref[m, rows, :].astype(F32)
                wr, wi = w[:BINS], w[BINS:]
                tr = wr * sr + wi * si
                ti = wr * si - wi * sr
                er, ei = (tr, ti) if er is None else (er + tr, ei + ti)
            e = jnp.concatenate([er * scale, ei * scale], axis=0).astype(BF)
            for m in range(2):
                prod[m, rows, width : 2 * width] = e

    by_corner(split, length, transform)
    corner = split // ROWS
    value_cols = pl.ds(2 * width, width)
    for copy in loads[7:10]:
        copy.wait()
    kpad[pl.ds(8, length), :] = key_ref[...].astype(F32)

    @pl.loop(0, length // ROWS)
    def _(i):
        row0 = pl.multiple_of(i * ROWS, ROWS)
        rows = pl.ds(row0, ROWS)
        spot = pl.ds(row0 + 8, ROWS)
        pick = (i > corner).astype(jnp.int32)
        both = dot(inv_ref[rows, :], prod[pick])
        pad[spot, value_cols] = both[:, :width]

        @pl.when(i == corner)
        def _():
            later = i * ROWS + lax.broadcasted_iota(jnp.int32, (ROWS, width), 0) >= split
            other = dot(inv_ref[rows, :], prod[1, :, 0:width])
            pad[spot, value_cols] = jnp.where(later, other, pad[spot, value_cols])

        inside = row0 + lax.broadcasted_iota(jnp.int32, (ROWS, width), 0) < half
        epad[spot, :] = jnp.where(inside, both[:, width:], 0.0) * decay_ref[rows, :]

    def key_taps(row0, same):
        spot = pl.ds(row0 + 8, CHUNK)
        for strip in range(strips):
            cols = pl.ds(strip * STRIP, STRIP)
            e = epad[spot, cols]
            pad[spot, pl.ds(width + strip * STRIP, STRIP)] = weigh(shifted(epad, row0, cols, same), cw_ref, 2, cols, True)
            for off, x in enumerate(shifted(kpad, row0, cols, same)):
                dcw_sum[off, :, cols] += (x * e).reshape(CHUNK // 8, 8, STRIP).sum(0)

    for copy in loads[15:]:
        copy.wait()
    cw_ref[...] = ct_ref[...].astype(F32).T
    sw_ref[...] = st_ref[...].astype(F32).T
    over_chunks(length, split, key_taps)
    loads[10].wait()

    @pl.loop(0, 3 * strips)
    def _(strip):
        cols = pl.ds(pl.multiple_of(strip * STRIP, STRIP), STRIP)
        kpad[pl.ds(8, length), pl.ds(0, STRIP)] = br_ref[:, cols].astype(F32)

        def branch_taps(row0, same):
            e = pad[pl.ds(row0 + 8, CHUNK), cols]
            total = weigh(shifted(pad, row0, cols, same), sw_ref, 0, cols, True)
            dbr_ref[pl.ds(row0, CHUNK), cols] = total.astype(BF)
            for off, x in enumerate(shifted(kpad, row0, pl.ds(0, STRIP), same)):
                dsw_sum[off, :, cols] += (x * e).reshape(CHUNK // 8, 8, STRIP).sum(0)

        over_chunks(length, split, branch_taps)

    ch_rows[1:2, :] = dmg_ref[...]
    st_rows[0:5, :] = jnp.sum(dsw_sum[...], axis=1)
    ch_rows[2:7, part] = jnp.sum(dcw_sum[...], axis=1)
    dch_ref[...] = ch_rows[...].T.astype(BF)
    for p in range(3):
        rows = pl.ds(pl.multiple_of(p * features + core * width, STRIP), width)
        dst_ref[rows, :] = st_rows[:, p * width : (p + 1) * width].T.astype(BF)
    for copy in loads[11:15]:
        copy.wait()
    d_out = dot(gated_ref[...], mid_ref[...], ((0,), (0,))).astype(BF)
    for h in range(2):
        rest_ref[h, part, out_cols] = d_out[:, h * width : (h + 1) * width]
    for cols in (pl.ds(0, 2 * width), pl.ds(2 * width, width)):
        d_in = dot(own_ref[...], dbr_ref[near, cols], ((0,), (0,)))
        d_in += dot(other_ref[...], dbr_ref[far, cols], ((0,), (0,)))
        rest_ref[core, :, cols] = d_in.astype(BF)
    dn_ref[...] = dot(dbr_ref[near, :], iw_ref[...], ((1,), (1,))).astype(BF)
    dn_send_ref[...] = dot(dbr_ref[far, :], iw_ref[...], ((1,), (1,))).astype(BF)


def local_call(kernel, args, direct, outs, direct_outs, scratch):
    vmem, anywhere = pl.BlockSpec(memory_space=pltpu.VMEM), pl.BlockSpec(memory_space=pl.ANY)
    return pl.pallas_call(
        kernel,
        out_shape=[jax.ShapeDtypeStruct(shape, dtype) for shape, dtype in outs],
        in_specs=[pl.BlockSpec(memory_space=pltpu.SMEM)]
        + [vmem] * (direct - 1)
        + [anywhere] * (len(args) - direct),
        out_specs=[vmem] * direct_outs + [anywhere] * (len(outs) - direct_outs),
        scratch_shapes=scratch,
        compiler_params=pltpu.CompilerParams(vmem_limit_bytes=VMEM_LIMIT),
    )(*args)


def tap_scratch(width):
    return [((width, LANES), BF), ((3 * width, LANES), BF), ((LANES, width), F32), ((LANES, 3 * width), F32)]


def mixer_forward(layer, split, own, other, ch, st, weight, decay, fwd, inv):
    _, length, width = decay.shape
    features = own.shape[1]
    bins = fwd.shape[0]
    tall, short, wide = (length, width), (own.shape[0], width), (length, 3 * width)
    kept = [(wide, BF), (tall, BF), (tall, BF), (tall, BF), ((bins, width), BF), ((2, bins, width), BF)]
    scratch = [((features, 3 * width), BF), (tall, F32), (fwd.shape, BF), (inv.shape, BF)] + kept + tap_scratch(width)
    scratch += [
        ((length + 16, 3 * width), F32),
        ((length + 16, width), F32),
        (tall, BF),
        ((2,) + tall, BF),
        ((2, bins, width), BF),
    ]
    return local_call(
        functools.partial(mixer_forward_kernel, layer),
        (split, own, other, ch, st, weight, decay, fwd, inv),
        3,
        [(tall, BF), (short, BF), (short, BF)] + kept,
        3,
        [pltpu.VMEM(*x) for x in scratch] + [pltpu.SemaphoreType.DMA((8,)), pltpu.SemaphoreType.DMA((6,))],
    )


def mixer_backward(
    layer, split, mid_own, mid_other, dmg, ch, st, weight, own, other, gated, br, decay, fwd, inv, q, key, conv, fh, uh
):
    _, length, width = decay.shape
    bins = fwd.shape[0]
    rows, features = mid_own.shape
    held = (own, other, gated, br, decay, fwd, inv, q, key, conv, fh, uh)
    scratch = [((2, width, width), BF), ((features, 3 * width), BF)]
    scratch += [(x.shape[1:] if x is decay else x.shape, x.dtype) for x in held] + tap_scratch(width)
    scratch += [
        ((length + 16, 3 * width), F32),
        ((length + 16, width), F32),
        ((length + 16, width), F32),
        ((2, length, width), BF),
        ((2, bins, 2 * width), BF),
        ((length, features), BF),
        ((length, 3 * width), BF),
        ((5, 8, 3 * width), F32),
        ((5, 8, width), F32),
        ((LANES, features), F32),
        ((LANES, 3 * width), F32),
    ]
    return local_call(
        functools.partial(mixer_backward_kernel, layer),
        (split, mid_own, mid_other, dmg, ch, st, weight) + held,
        4,
        [
            ((2, features, 4 * width), BF),
            ((rows, features), BF),
            ((rows, features), BF),
            ((features, LANES), BF),
            ((3 * features, LANES), BF),
        ],
        5,
        [pltpu.VMEM(*x) for x in scratch] + [pltpu.SemaphoreType.DMA((19,))],
    )


def cube(dp_count):
    bits = (dp_count // 2).bit_length() - 1
    core, seq = bits, bits + 1
    low, rest = [bits - 1], list(range(bits - 1))
    orders = (
        rest + [seq] + low, rest + low + [seq], low + [seq] + rest,
        low + rest + [seq], [seq] + rest + low, [seq] + low + rest,
    )
    return bits, core, seq, orders


def place(bits):
    dp, seq = lax.axis_index("dp"), lax.axis_index("seq")
    coords = [(dp // (2 << (bits - 1 - d))) % 2 for d in range(bits)] + [dp % 2, seq]

    def neighbour(d):
        if d == bits + 1:
            return dp, 1 - seq
        step = 1 if d == bits else 2 << (bits - 1 - d)
        return dp + step * (1 - 2 * coords[d]), seq

    return coords, neighbour


def region(fixed, dims):
    return tuple(fixed[d] if d in fixed else slice(None) for d in range(dims))


def across(coords, bits):
    dp = lax.axis_index("dp")
    core, seq = coords[bits], coords[bits + 1]
    return core != seq, (dp + 1 - 2 * core, 1 - seq)


def greet(neighbours):
    barrier = pltpu.get_barrier_semaphore()
    for device in neighbours:
        pl.semaphore_signal(barrier, inc=1, device_id=device, device_id_type=pl.DeviceIdType.MESH)
    pl.semaphore_wait(barrier, len(neighbours))


class Swap:
    def __init__(self, src, dst, send, recv, local, moves, partner):
        self.stays, self.moves = jnp.logical_not(moves), moves
        self.away = pltpu.make_async_remote_copy(
            src_ref=src, dst_ref=dst, send_sem=send, recv_sem=recv,
            device_id=partner, device_id_type=pl.DeviceIdType.MESH,
        )
        self.here = pltpu.make_async_copy(src, dst, local)

    def start(self):
        pl.when(self.moves)(lambda: self.away.start())
        pl.when(self.stays)(lambda: self.here.start())

    def wait(self):
        pl.when(self.moves)(lambda: self.away.wait())
        pl.when(self.stays)(lambda: self.here.wait())


def remote(src, dst, send, recv, device):
    copy = pltpu.make_async_remote_copy(
        src_ref=src, dst_ref=dst, send_sem=send, recv_sem=recv,
        device_id=device, device_id_type=pl.DeviceIdType.MESH,
    )
    copy.start()
    return copy


GATHER_UNITS = (
    (3, 0, 640, 0, 0), (3, 640, 512, 1, 0), (3, 1152, 384, 2, 0), (5, 0, 128, 2, 0), (6, 0, 128, 1, 0),
    (0, 0, 768, 0, 1), (0, 768, 768, 1, 1), (2, 2, 2, 2, 1),
    (0, 1536, 768, 0, 2), (0, 2304, 768, 1, 2),
    (1, 0, 2, 0, 3), (1, 2, 2, 1, 3), (4, 1280, 256, 2, 3),
    (4, 0, 640, 0, 4), (4, 640, 640, 1, 4),
    (2, 0, 1, 0, 5), (2, 1, 1, 1, 5),
)
SCATTER_UNITS = (
    (0, 0, 768, 0, 0), (0, 768, 768, 1, 0), (2, 2, 2, 2, 0),
    (0, 1536, 768, 0, 1), (0, 2304, 768, 1, 1), (3, 1280, 256, 2, 1),
    (1, 0, 2, 0, 2), (1, 2, 2, 1, 2), (4, 1280, 256, 2, 2),
    (3, 0, 640, 0, 3), (3, 640, 640, 1, 3), (5, 0, 128, 2, 3), (6, 0, 128, 2, 3),
    (4, 0, 640, 0, 4), (4, 640, 640, 1, 4), (7, 0, 128, 2, 4),
    (2, 0, 1, 0, 5), (2, 1, 1, 0, 5),
)


def piece_of(unit, slabs):
    span = pl.ds(unit[1], unit[2])
    return (span, slice(None), slice(None)) if slabs else (slice(None), span)


def ticks(units, stages, shrinking):
    steps = [max(2**t, 2 ** (stages - 2)) for t in range(stages)]
    if shrinking:
        steps = steps[::-1]
    spacing = 2**stages // 4
    due = []
    for i, unit in enumerate(units):
        if shrinking:
            due.append((spacing * (unit[4] - 1) - 1, i, -1))
        due += [(spacing * unit[4] + sum(steps[:t]), i, t) for t in range(stages + 1)]
    return [(i, t) for _, i, t in sorted(due)]


def gather_kernel(dp_count, units, rows_in, rows_out, own, full, sems):
    bits, core_dim, _, orders = cube(dp_count)
    dims = bits + 2
    stages = dims - 1
    coords, neighbour = place(bits)
    core = coords[core_dim]
    sibling = neighbour(core_dim)
    moves, partner = across(coords, bits)
    greet([neighbour(d) for d in range(dims)] + [partner])
    ici_send, ici_recv, core_send, core_recv, local, swap_send, swap_recv, swap_local = sems
    swaps = [
        Swap(src, dst, swap_send.at[i], swap_recv.at[i], swap_local.at[i], moves, partner)
        for i, (src, dst) in enumerate(zip(rows_in, rows_out))
    ]
    mine = region(dict(enumerate(coords)), dims)
    firsts, forwards, sends = [], [], []
    last = [None] * len(units)
    for u, unit in enumerate(units):
        array, tail = unit[0], piece_of(unit, len(own[unit[0]].shape) == 4)
        piece = own[array].at[(slice(None),) + tail]
        here = full[array].at[(slice(None),) + mine + tail]
        keep = pltpu.make_async_copy(piece, here, local.at[u])
        keep.start()
        firsts.append((keep, remote(piece, here, core_send.at[u, 0], core_recv.at[u, 0], sibling)))
    for number, (u, t) in enumerate(ticks(units, stages, False)):
        if number == 4:
            for swap in swaps:
                swap.start()
        unit = units[u]
        array, tail, order = unit[0], piece_of(unit, len(own[unit[0]].shape) == 4), orders[unit[3]]
        fixed = {e: coords[e] for e in order[t:]}
        if t == 0:
            firsts[u][0].wait()
            firsts[u][1].wait_recv()
        else:
            last[u].wait_recv()
            got = full[array].at[(core,) + region(fixed | {order[t - 1]: 1 - coords[order[t - 1]]}, dims) + tail]
        if t < stages:
            held = full[array].at[(core,) + region(fixed, dims) + tail]
            last[u] = remote(held, held, ici_send.at[u, t], ici_recv.at[u, t], neighbour(order[t]))
            sends.append(last[u])
        if t > 0:
            forwards.append(remote(got, got, core_send.at[u, t], core_recv.at[u, t], sibling))
    for swap in swaps:
        swap.wait()
    beside = remote(rows_out[0], rows_out[-1], swap_send.at[len(swaps)], swap_recv.at[len(swaps)], sibling)
    for keep, copy in firsts:
        copy.wait_send()
    for copy in forwards:
        copy.wait()
    for copy in sends:
        copy.wait_send()
    beside.wait()


def gather_weights(rows, own, dp_count, number):
    bits = cube(dp_count)[0]
    stages = bits + 1
    units = GATHER_UNITS
    arrays = len(own)
    count = len(units)

    def body(*refs):
        rows_in, refs = refs[: len(rows)], refs[len(rows) :]
        own_refs, refs = refs[:arrays], refs[arrays:]
        rows_out, refs = refs[: len(rows) + 1], refs[len(rows) + 1 :]
        gather_kernel(dp_count, units, rows_in, rows_out, own_refs, refs[:arrays], refs[arrays:])

    grid = (2,) * (bits + 2)
    anywhere = pl.BlockSpec(memory_space=pl.ANY)
    return pl.pallas_call(
        body,
        out_shape=[jax.ShapeDtypeStruct(x.shape, x.dtype) for x in (*rows, rows[0])]
        + [jax.ShapeDtypeStruct(x.shape[:1] + grid + x.shape[1:], x.dtype) for x in own],
        in_specs=[anywhere] * (len(rows) + arrays),
        out_specs=[anywhere] * (len(rows) + 1 + arrays),
        scratch_shapes=[pltpu.SemaphoreType.DMA((count, stages))] * 2
        + [pltpu.SemaphoreType.DMA((count, stages + 1))] * 2
        + [pltpu.SemaphoreType.DMA((count,))]
        + [pltpu.SemaphoreType.DMA((len(rows) + 1,))] * 3,
        compiler_params=pltpu.CompilerParams(collective_id=number, has_side_effects=True),
    )(*rows, *own)


def scatter_kernel(dp_count, units, ends_in, token_ref, grads, outs, held, first, arrived, final, work, sems):
    bits, core_dim, _, orders = cube(dp_count)
    dims = bits + 2
    stages = dims - 1
    coords, neighbour = place(bits)
    core = coords[core_dim]
    sibling = neighbour(core_dim)
    moves, partner = across(coords, bits)
    greet([neighbour(d) for d in range(dims)] + [partner])
    ici_send, ici_recv, core_send, core_recv, local, end_send, end_recv, end_local = sems
    x_ref, dn_ref, away_ref, dmid_ref, gain_ref, dng_ref = ends_in
    other_ref, grad_ref, sum_ref, flat_ref, tall_ref, slab_ref = work
    grads = list(grads) + [slab_ref]
    exchange = remote(away_ref, other_ref, end_send.at[0], end_recv.at[0], sibling)
    begin = pltpu.make_async_copy(dmid_ref, grad_ref, end_local.at[1])
    begin.start()
    swap = Swap(other_ref, token_ref, end_send.at[1], end_recv.at[1], end_local.at[0], moves, partner)

    def finish_rows():
        exchange.wait()
        begin.wait()
        sum_ref[...] = jnp.zeros(sum_ref.shape, F32)
        share = slab_ref.shape[-2]

        @pl.loop(0, x_ref.shape[0] // 128)
        def _(i):
            rows = pl.ds(pl.multiple_of(i * 128, 128), 128)
            d = dn_ref[rows, :].astype(F32) + other_ref[rows, :].astype(F32)
            dx, dg = norm_back(x_ref[rows, :].astype(F32), gain_ref[...], d)
            other_ref[rows, :] = (grad_ref[rows, :] + dx).astype(BF)
            sum_ref[0:1, :] += dg

        swap.start()
        flat_ref[...] = jnp.zeros(flat_ref.shape, F32)
        for layer, row in enumerate((sum_ref, dng_ref)):
            for c in range(tall_ref.shape[0] // LANES):
                cols = slice(c * LANES, (c + 1) * LANES)
                flat_ref[0:1, :] = row[0:1, cols]
                tall_ref[cols, :] = flat_ref[...].T
            for i in range(2**dims):
                at = tuple((i >> (dims - 1 - d)) % 2 for d in range(dims))
                slab_ref[(layer,) + at] = tall_ref[i * share : (i + 1) * share, :].astype(BF)

    everything = region({}, dims)

    def add(u, fixed, extra):
        free = [d for d in range(dims) if d not in fixed]

        @pl.loop(0, 2 ** len(free))
        def _(i):
            at = {d: (i // 2 ** (len(free) - 1 - j)) % 2 for j, d in enumerate(free)}
            index = tuple(at[d] if d in at else fixed[d] for d in range(dims))
            held[u][index] += extra[tuple(at[d] for d in free)]

    starts, sends = [None] * len(units), []
    last = [None] * len(units)
    for u, t in ticks(units, stages, True):
        if t < 0 and units[u][0] == len(grads) - 1:
            finish_rows()
        if t < 0:
            array, tail = units[u][0], piece_of(units[u], len(outs[units[u][0]].shape) == 4)
            load = pltpu.make_async_copy(grads[array].at[(core,) + everything + tail], held[u], local.at[u, 0])
            load.start()
            other = grads[array].at[(1 - core,) + everything + tail]
            starts[u] = (load, remote(other, first[u], core_send.at[u, 0], core_recv.at[u, 0], sibling))
            continue
        order = orders[units[u][3]][::-1]
        fixed = {d: coords[d] for d in order[:t]}
        if t == 0:
            starts[u][0].wait()
            starts[u][1].wait_recv()
            add(u, fixed, first[u])
        else:
            last[u].wait_recv()
            add(u, fixed, arrived[u][t - 1])
        if t < stages:
            away = held[u].at[region(fixed | {order[t]: 1 - coords[order[t]]}, dims)]
            last[u] = remote(away, arrived[u][t], ici_send.at[u, t], ici_recv.at[u, t], neighbour(order[t]))
            sends.append(last[u])
        else:
            away = held[u].at[region(fixed | {core_dim: 1 - core}, dims)]
            last[u] = remote(away, final[u], core_send.at[u, 1], core_recv.at[u, 1], sibling)
    ends = []
    mine = region(dict(enumerate(coords)), dims)
    for u, unit in enumerate(units):
        array, tail = unit[0], piece_of(unit, len(outs[unit[0]].shape) == 4)
        own = pltpu.make_async_copy(held[u].at[mine], outs[array].at[(core,) + tail], local.at[u, 1])
        own.start()
        last[u].wait_recv()
        other = pltpu.make_async_copy(final[u], outs[array].at[(1 - core,) + tail], local.at[u, 2])
        other.start()
        ends += [own, other]
    swap.wait()
    for copy in ends:
        copy.wait()
    for copy in sends + last + [s[1] for s in starts]:
        copy.wait_send()


def scatter_grads(ends, grads, units, dp_count, number):
    bits = cube(dp_count)[0]
    dims = bits + 2
    stages = dims - 1
    count = len(units)
    grid = (2,) * dims
    rows, features = ends[0].shape
    share = grads[0].shape[1 + dims]
    tails = [x.shape[1 + dims :] for x in grads] + [(share, LANES)]
    arrays = len(tails)
    slabs = []
    for array, _, size, _, _ in units:
        shape = tails[array]
        slabs.append((size,) + shape[1:] if len(shape) == 3 else shape[:-1] + (size,))
    work = [((rows, features), BF), ((rows, features), F32), ((8, features), F32), ((LANES, LANES), F32)]
    work += [((features, LANES), F32), ((2,) + grid + (share, LANES), BF)]

    def body(*refs):
        ends_in, refs = refs[: len(ends)], refs[len(ends) :]
        grads_in, refs = refs[: len(grads)], refs[len(grads) :]
        token, outs, refs = refs[0], refs[1 : 1 + arrays], refs[1 + arrays :]
        held, first, final = refs[:count], refs[count : 2 * count], refs[2 * count : 3 * count]
        refs = refs[3 * count :]
        arrived = [refs[u * stages : (u + 1) * stages] for u in range(count)]
        refs = refs[count * stages :]
        scatter_kernel(
            dp_count, units, ends_in, token, grads_in, outs, held, first, arrived, final,
            refs[: len(work)], refs[len(work) :],
        )

    anywhere, vmem = pl.BlockSpec(memory_space=pl.ANY), pl.BlockSpec(memory_space=pltpu.VMEM)
    return pl.pallas_call(
        body,
        out_shape=[jax.ShapeDtypeStruct((rows, features), BF)]
        + [jax.ShapeDtypeStruct((2,) + tail, BF) for tail in tails],
        in_specs=[vmem, vmem, anywhere, anywhere, vmem, vmem] + [anywhere] * len(grads),
        out_specs=[anywhere] * (1 + arrays),
        scratch_shapes=[pltpu.VMEM(grid + slab, BF) for slab in slabs] * 2
        + [pltpu.VMEM(slab, BF) for slab in slabs]
        + [pltpu.VMEM((2,) * (dims - 1 - t) + slab, BF) for slab in slabs for t in range(stages)]
        + [pltpu.VMEM(*x) for x in work]
        + [pltpu.SemaphoreType.DMA((count, stages))] * 2
        + [pltpu.SemaphoreType.DMA((count, 2))] * 2
        + [pltpu.SemaphoreType.DMA((count, 3))]
        + [pltpu.SemaphoreType.DMA((2,))] * 2
        + [pltpu.SemaphoreType.DMA((2,))],
        compiler_params=pltpu.CompilerParams(
            collective_id=number, has_side_effects=True, vmem_limit_bytes=VMEM_LIMIT
        ),
    )(*ends, *grads)


def norm_parts(x):
    center = x - jnp.mean(x, axis=-1, keepdims=True)
    r = lax.rsqrt(jnp.mean(center * center, axis=-1, keepdims=True) + EPS)
    return center * r, r


def norm_back(x, gain, d):
    xhat, r = norm_parts(x)
    h = d * gain
    dx = r * (h - jnp.mean(h, axis=-1, keepdims=True) - xhat * jnp.mean(h * xhat, axis=-1, keepdims=True))
    return dx, jnp.sum(d * xhat, axis=0, keepdims=True)


SLOPE = math.sqrt(2.0 / math.pi)
CUBE = 0.044715


def gelu_parts(x):
    square = x * x
    t = jnp.tanh(SLOPE * (x + CUBE * square * x))
    flat = 0.5 + 0.5 * t
    return x * flat, flat + 0.5 * x * (1.0 - t * t) * (SLOPE + 3.0 * SLOPE * CUBE * square)


def mlp_forward_kernel(
    gain, next_gain, x_ref, g0_ref, g1_ref, o0_ref, o1_ref, gains_ref, wg_ref, wu_ref, d0_ref, d1_ref,
    mid_ref, hm_ref, pre_ref, out_ref, next_ref,
):
    j = pl.program_id(0)

    @pl.when(j == 0)
    def _():
        width = g0_ref.shape[1]
        mid = x_ref[...]
        core = lax.axis_index("dp") % 2
        for ref, side in ((g0_ref, core), (g1_ref, 1 - core)):
            rows = pl.ds(pl.multiple_of(side * width, STRIP), width)
            mid += dot(ref[...], jnp.concatenate([o0_ref[rows, :], o1_ref[rows, :]], axis=1))
        mid_ref[...] = mid
        out_ref[...] = mid
        hm_ref[...] = (norm_parts(mid)[0] * gains_ref[gain : gain + 1, :]).astype(BF)

    hm = hm_ref[...]
    total = out_ref[...]
    for i in range(TILE // PART_F):
        part = slice(i * PART_F, (i + 1) * PART_F)
        gate = dot(hm, wg_ref[:, part])
        up = dot(hm, wu_ref[:, part])
        pre_ref[0, :, part] = gate.astype(BF)
        pre_ref[1, :, part] = up.astype(BF)
        hid = (gelu_parts(gate)[0] * up).astype(BF)
        total += dot(hid, jnp.concatenate([d0_ref[part, :], d1_ref[part, :]], axis=1))
    out_ref[...] = total

    @pl.when(j == pl.num_programs(0) - 1)
    def _():
        next_ref[...] = (norm_parts(out_ref[...])[0] * gains_ref[next_gain : next_gain + 1, :]).astype(BF)


def mlp_backward_kernel(
    gain, g_ref, hm_ref, mid_ref, gains_ref, pre_ref, wg_ref, wu_ref, d0_ref, d1_ref,
    dgu_ref, ddn_ref, dmid_ref, mlow_ref, dmg_ref,
    glow, hm_t, acc,
):
    j = pl.program_id(0)
    width = d0_ref.shape[1]

    @pl.when(j == 0)
    def _():
        glow[...] = g_ref[...].astype(BF)
        hm_t[...] = hm_ref[...].T
        acc[...] = jnp.zeros(acc.shape, F32)

    low, hm = glow[...], hm_t[...]
    total = acc[...]
    for i in range(TILE // PART_B):
        part = slice(i * PART_B, (i + 1) * PART_B)
        dh = dot(low, jnp.concatenate([d0_ref[part, :], d1_ref[part, :]], axis=1), ((1,), (1,)))
        value, slope = gelu_parts(pre_ref[0, :, part].astype(F32))
        up = pre_ref[1, :, part].astype(F32)
        hid = (value * up).astype(BF)
        d_gate = (dh * up * slope).astype(BF)
        d_up = (dh * value).astype(BF)
        d_down = dot(hid, low, ((0,), (0,))).astype(BF)
        ddn_ref[0, part, :] = d_down[:, :width]
        ddn_ref[1, part, :] = d_down[:, width:]
        for h, d in enumerate((d_gate, d_up)):
            grad = dot(hm, d).astype(BF)
            if len(dgu_ref.shape) == 3:
                dgu_ref[h, :, part] = grad
            else:
                dgu_ref[:, h * TILE + i * PART_B : h * TILE + (i + 1) * PART_B] = grad
        total += dot(d_gate, wg_ref[:, part], ((1,), (1,))) + dot(d_up, wu_ref[:, part], ((1,), (1,)))
    acc[...] = total

    @pl.when(j == pl.num_programs(0) - 1)
    def _():
        dx, dg = norm_back(mid_ref[...], gains_ref[gain : gain + 1, :], acc[...])
        dmid = g_ref[...] + dx
        dmid_ref[...] = dmid
        mlow_ref[...] = dmid.astype(BF)
        dmg_ref[...] = dg


TILE = 512
PART_F = 512
PART_B = 512


def whole(shape):
    return pl.BlockSpec(shape, lambda j: (0,) * len(shape))


def weight_specs(layout, hidden, features):
    steps = hidden // TILE
    gate_up = pl.BlockSpec((features, TILE), lambda j: (0, j))
    up = pl.BlockSpec((features, TILE), lambda j: (1, j) if layout == "halves" else (0, steps + j))
    down = [
        pl.BlockSpec((TILE, features // 2), lambda j: (j, 0)),
        pl.BlockSpec((TILE, features // 2), lambda j: (steps + j, 0)),
    ]
    return [gate_up, up] + down


def mlp_forward(x, g0, g1, weight, gains, gain, next_gain, weights):
    layout, gu, dn = weights
    rows, features = x.shape
    hidden = dn.shape[0] // 2
    square = whole((rows, features))
    narrow = [whole(a.shape) for a in (g0, g1)]
    narrow += [pl.BlockSpec((features, features // 2), lambda j, h=h: (h, 3)) for h in range(2)]
    shapes = [((rows, features), F32), ((rows, features), BF), ((2, rows, hidden), BF), ((rows, features), F32), ((rows, features), BF)]
    return pl.pallas_call(
        functools.partial(mlp_forward_kernel, gain, next_gain),
        grid=(hidden // TILE,),
        out_shape=[jax.ShapeDtypeStruct(*s) for s in shapes],
        in_specs=[square] + narrow + [whole(gains.shape)] + weight_specs(layout, hidden, features),
        out_specs=[square, square, pl.BlockSpec((2, rows, TILE), lambda j: (0, 0, j)), square, square],
        compiler_params=pltpu.CompilerParams(vmem_limit_bytes=VMEM_LIMIT),
    )(x, g0, g1, weight, weight, gains, gu, gu, dn, dn)


def mlp_backward(g, hm, mid, gains, gain, pre, weights, side_by_side):
    layout, gu, dn = weights
    rows, features = g.shape
    hidden = pre.shape[2]
    width = features // 2
    square, vector = whole((rows, features)), whole((1, features))
    both = (features, 2 * hidden) if side_by_side else (2, features, hidden)
    shapes = [(both, BF), ((2, hidden, width), BF), ((rows, features), F32), ((rows, features), BF), ((1, features), F32)]
    return pl.pallas_call(
        functools.partial(mlp_backward_kernel, gain),
        grid=(hidden // TILE,),
        out_shape=[jax.ShapeDtypeStruct(*s) for s in shapes],
        in_specs=[square] * 3
        + [whole(gains.shape), pl.BlockSpec((2, rows, TILE), lambda j: (0, 0, j))]
        + weight_specs(layout, hidden, features),
        out_specs=[
            pl.BlockSpec((features, 2 * TILE), lambda j: (0, j))
            if side_by_side
            else pl.BlockSpec((2, features, TILE), lambda j: (0, 0, j)),
            pl.BlockSpec((2, TILE, width), lambda j: (0, j, 0)),
            square, square, vector,
        ],
        scratch_shapes=[pltpu.VMEM((rows, features), BF), pltpu.VMEM((features, rows), BF), pltpu.VMEM((rows, features), F32)],
        compiler_params=pltpu.CompilerParams(vmem_limit_bytes=VMEM_LIMIT),
    )(g, hm, mid, gains, pre, gu, gu, dn, dn)


def shards(
    tokens, split_points, cotangent, norm_gain, in_weight, short_taps, cond_taps,
    out_weight, mlp_gain, gate_up, down_weight,
):
    rows, features = tokens.shape[1:]
    dp_count, seq_count = lax.axis_size("dp"), lax.axis_size("seq")
    devices = dp_count * seq_count
    length = rows * seq_count
    width = features // 2
    layers = in_weight.shape[0]
    share = norm_gain.shape[1]
    hidden = down_weight.shape[1] * devices
    core = lax.axis_index("dp") % 2
    seq = lax.axis_index("seq")

    swap = [(4 * k + a, 4 * k + 3 - a) for k in range(devices // 4) for a in (1, 2)]
    flip = [(i, i ^ 1) for i in range(dp_count)]

    def swap_rows(x):
        return jnp.where(core == seq, x, lax.ppermute(x, AXES, swap))

    def sibling(x):
        return lax.ppermute(x, "dp", flip)

    def beside(own, other, axis):
        return jnp.where(
            core == 0,
            jnp.concatenate([own, other], axis=axis),
            jnp.concatenate([other, own], axis=axis),
        )

    def half_of(x, which, axis):
        size = x.shape[axis] // 2
        return lax.dynamic_slice_in_dim(x, which * size, size, axis)

    table = transform_matrix(length)
    fwd = jnp.asarray(table, BF)
    inv = jnp.asarray(np.ascontiguousarray(table.T), BF)
    decay = jnp.asarray(decay_table(length, features))

    def halves(x):
        parts = x.shape[-1] // features
        x = x.reshape(x.shape[:-1] + (parts, 2, width))
        x = jnp.moveaxis(x, -2, 0)
        return x.reshape(x.shape[:-2] + (parts * width,))

    grid = (2,) * (cube(dp_count)[0] + 2)

    ch = jnp.concatenate([norm_gain[:, :, None], mlp_gain[:, :, None], cond_taps.transpose(0, 2, 1)], axis=2)
    ch = jnp.pad(ch, ((0, 0), (0, 0), (0, LANES - 7)))
    st = jnp.pad(short_taps.transpose(0, 2, 1), ((0, 0), (0, 0), (0, LANES - 5)))
    own = [gate_up[0].reshape(share, 2, hidden).transpose(1, 0, 2)]
    own += [halves(down_weight[layer]).reshape(2, hidden // features, share, width) for layer in range(layers)]
    for layer in range(layers):
        own.append(jnp.concatenate([halves(in_weight[layer]), halves(out_weight[layer])], axis=2))
    place_rows = [tokens[0], jnp.broadcast_to(split_points, (8, LANES))]
    x_low, split, x_far, *full = gather_weights(place_rows, own + [ch, st], dp_count, 0)
    downs = [x.reshape(2 * hidden, width) for x in full[1 : 1 + layers]]
    mixer_w = [x.reshape(2, features, 4 * width) for x in full[1 + layers : 1 + 2 * layers]]
    ch, st = full[-2].reshape(layers, features, LANES), full[-1].reshape(layers, 3 * features, LANES)
    late, _ = lax.optimization_barrier((gate_up[1:], full[0]))
    gate_ups = [("halves", full[0].reshape(2 * features, hidden))]
    gate_ups += [("plain", lax.all_gather(x, AXES, axis=0, tiled=True)) for x in late]
    gains = ch[:, :, :2].astype(F32).transpose(0, 2, 1).reshape(2 * layers, features)
    stream, far = x_low.astype(F32), x_far.astype(F32)
    normed, normed_far = [(norm_parts(x)[0] * gains[0]).astype(BF) for x in (stream, far)]
    kept = []
    for layer in range(layers):
        if layer > 0:
            normed_far = sibling(normed)
        gated, mine, away, branches, q, key, conv, fh, uh = mixer_forward(
            layer, split, normed, normed_far, ch, st, mixer_w[layer], decay, fwd, inv
        )
        if layer == layers - 1:
            arrived, _, _ = lax.optimization_barrier((cotangent, gate_ups[-1][1], mine))
            grad = swap_rows(arrived)[0].astype(F32)
        middle, normed_mlp, pre, out, normed_next = mlp_forward(
            stream, mine, sibling(away), mixer_w[layer].reshape(2 * features, -1), gains,
            2 * layer + 1, (2 * layer + 2) % (2 * layers), gate_ups[layer] + (downs[layer],),
        )
        kept.append((stream, normed, normed_far, gated, branches, q, key, conv, fh, uh, middle, normed_mlp, pre))
        stream, normed = out, normed_next
    activations = swap_rows(stream.astype(BF)[None])

    summed = []
    early = [None] * layers
    for layer in reversed(range(layers)):
        x, normed, normed_far, gated, branches, q, key, conv, fh, uh, middle, normed_mlp, pre = kept[layer]
        d_gu, d_down, d_middle, m_low, d_mg = mlp_backward(
            grad, normed_mlp, middle, gains, 2 * layer + 1, pre, gate_ups[layer] + (downs[layer],), layer > 0
        )
        rest, d_normed, d_away, d_ch, d_st = mixer_backward(
            layer, split, m_low, sibling(m_low), d_mg, ch, st, mixer_w[layer], normed, normed_far, gated, branches,
            decay, fwd, inv, q, key, conv, fh, uh,
        )
        if layer > 0:
            early[layer] = lax.psum_scatter(d_gu, AXES, scatter_dimension=0, tiled=True)
            d_part, d_ng = norm_back(x, gains[2 * layer], d_normed.astype(F32) + sibling(d_away).astype(F32))
            grad = d_middle + d_part
        summed.append((d_gu, d_down, rest, d_ch, d_st))
    d_gus, d_downs, rests, *smalls = zip(*summed[::-1])
    pieces = [d_gus[0].reshape((2,) + grid + (share, hidden))]
    pieces += [x.reshape((2,) + grid + (hidden // features, share, width)) for x in d_downs]
    pieces += [x.reshape((2,) + grid + (share, 4 * width)) for x in rests]
    pieces += [jnp.stack(x).reshape((2,) + grid + (-1, LANES)) for x in smalls]
    ends = [x_low, d_normed, d_away, d_middle, gains[:1], d_ng]
    fits = share % 8 == 0
    units = tuple(unit for unit in SCATTER_UNITS if fits or unit[0] != 2)
    token_grad, *outs = scatter_grads(ends, pieces, units, dp_count, 1)
    if not fits:
        outs[2] = lax.psum_scatter(d_downs[1], AXES, scatter_dimension=1, tiled=True)
    token_grad = token_grad[None].astype(F32)

    def joined(x):
        parts = x.shape[-1] // width
        x = jnp.moveaxis(x.reshape(x.shape[:-1] + (parts, width)), 0, -2)
        return x.reshape(x.shape[:-3] + (parts * features,))

    early[0] = outs[0].transpose(1, 0, 2)
    for layer in range(1, layers):
        early[layer] = early[layer].reshape(share, hidden // TILE, 2, TILE).transpose(0, 2, 1, 3)
    g_gu = jnp.stack([x.reshape(share, 2 * hidden) for x in early]).astype(F32)
    g_down = jnp.stack([joined(x.reshape(2, -1, width)) for x in outs[1 : 1 + layers]]).astype(F32)
    rest = outs[1 + layers : 1 + 2 * layers]
    g_in = jnp.stack([joined(x[:, :, : 3 * width]) for x in rest]).astype(F32)
    g_out = jnp.stack([joined(x[:, :, 3 * width :]) for x in rest]).astype(F32)
    s_ch, s_st, s_ng = [x.astype(F32) for x in outs[1 + 2 * layers :]]
    g_ng, g_mg, g_ct, g_st = s_ng[:, :, 0], s_ch[:, :, 1], s_ch[:, :, 2:7].transpose(0, 2, 1), s_st[:, :, :5].transpose(0, 2, 1)
    return (
        activations,
        token_grad,
        g_ng,
        g_in,
        g_st,
        g_ct,
        g_out,
        g_mg,
        g_gu,
        g_down,
    )


def solution(mesh):
    every = ("dp", "seq")
    rows, part = P("dp", "seq", None), P(None, every, None)
    vector, taps = P(None, every), P(None, None, every)
    return jax.shard_map(
        shards,
        mesh=mesh,
        in_specs=(rows, P("dp"), rows, vector, part, taps, taps, part, vector, part, part),
        out_specs=(rows, rows, vector, part, taps, taps, part, vector, part, part),
        check_vma=False,
    )
```
